256 devices in a mesh: space: 32 (over x, z_hi, core), batch: 8 (over z_lo, y).
Axes of the slice: x: 4, y: 4, z: 8 (z_hi: 4, z_lo: 2; z = z_hi * 2 + z_lo), core: 2. Of those that a mesh axis runs over, the one named last changes fastest.
Arguments:
- inputs: bfloat16 [8, 64, 64, 64, 128], P('batch', 'space'), may hold values from -6 to 6
- cotangent: bfloat16 [8, 64, 64, 64, 128], P('batch', 'space'), may hold values from -6 to 6
- dense_weights: bfloat16 [32, 16, 16, 64, 128], P('space', 'batch'), may hold values from -0.5 to 0.5
- owner_table: int32 [16], replicated, may hold values from 0 to 15, each once
- hot_mask: int32 [32, 16, 16], P('space'), may hold values 0 or 1
- skip_weight: bfloat16 [64, 64], replicated, may hold values from -0.75 to 0.75
- bias_vector: float32 [64], replicated, may hold values from -3 to 3
- input_factor: bfloat16 [64, 16], replicated, may hold values from -0.75 to 0.75
- output_factor: bfloat16 [64, 16], replicated, may hold values from -1.5 to 1.5
- first_factor: float32 [2, 32, 16], replicated, may hold values from -4 to 4
- second_factor: float32 [32, 16], replicated, may hold values from -5 to 5
- third_factor: float32 [16, 16], replicated, may hold values from -5 to 5
Outputs:
- output: bfloat16 [8, 64, 64, 64, 128], P('batch', 'space')
- input_grad: bfloat16 [8, 64, 64, 64, 128], P('batch', 'space')
- dense_grad: float32 [32, 16, 16, 64, 128], P('space', 'batch')
- input_factor_grad: float32 [64, 16], replicated
- output_factor_grad: float32 [64, 16], replicated
- first_factor_grad: float32 [2, 32, 16], replicated
- second_factor_grad: float32 [32, 16], replicated
- third_factor_grad: float32 [16, 16], replicated
- skip_grad: float32 [64, 64], replicated
- bias_grad: float32 [64], replicated
The draws below stay inside these ranges and needn't reach their ends.
Inputs may be any that keep to these rules, and one draw needn't show every extreme that they name: `owner_table`: each of 0 to 15 appears once.
All inputs are finite; a program needn't handle non-finite values. No bound on the sum of `hot_mask` on one device may be relied on, other than what follows from the above.
Results may differ from the reference program's by a relative error of at most 0.025.
Values may be sent and summed in bfloat16 or wider, within the bound.
A program may use at most 128 MiB of HBM per device.

```python
import math
import jax
import jax.numpy as jnp
from jax import lax

C = 64
N1 = 64
N2 = 64
N3 = 128
K1 = 32
K2 = 32
K3 = 16
L2 = 16
R = 16
SAMPLES = 8


def set_ends(values, rng, least, top_value):
    extent = values.shape
    spot = [jax.random.randint(jax.random.fold_in(rng, axis), (), 0, extent[axis]) for axis in range(len(extent))]
    values = values.at[tuple(spot)].set(least)
    longest = extent.index(max(extent))
    spot[longest] = (spot[longest] + 1) % extent[longest]
    return values.at[tuple(spot)].set(top_value)


def shard_levels(own_key, dims, split, low, largest):
    loudness = 1.0
    for dim, blocks in split:
        draws = jax.random.uniform(jax.random.fold_in(jax.random.fold_in(own_key, 6), dim), (blocks,), jnp.float32, low / len(split), largest / len(split))
        loudness = loudness * jnp.repeat(jnp.exp(draws), dims[dim] // blocks).reshape((-1,) + (1,) * (len(dims) - 1 - dim))
    return loudness


def centred(stream_key, extent, spread, reach, cuts=(), kind=jnp.bfloat16):
    entries = spread * jax.random.normal(stream_key, extent, jnp.float32)
    if cuts:
        entries = entries * shard_levels(stream_key, extent, cuts, -0.22, 0.18)
    return jnp.clip(entries, -reach, reach).astype(kind)


def setup_inputs(seed: int = 0) -> dict:
    key_of = jax.random.split(jax.random.key(seed), 13)
    return {
        "inputs": centred(key_of[0], (SAMPLES, N2, C, N1, N3), 1.0, 6.0, ((0, 8), (1, 32))),
        "cotangent": centred(key_of[1], (SAMPLES, N2, C, N1, N3), 1.0, 6.0, ((0, 8), (1, 32))),
        "dense_weights": centred(key_of[2], (K1, L2, K3, C, 2 * C), (2 * C) ** -0.5, 0.5, ((0, 32), (1, 8))),
        "owner_table": jax.random.permutation(key_of[3], L2).astype(jnp.int32),
        "hot_mask": set_ends((jax.random.randint(key_of[4], (K1, L2, K3), 0, 2) < 1).astype(jnp.int32), jax.random.fold_in(key_of[4], 1), 0, 1),
        "skip_weight": centred(key_of[5], (C, C), C ** -0.5, 0.75),
        "bias_vector": centred(key_of[6], (C,), 0.5, 3.0, (), jnp.float32),
        "input_factor": centred(key_of[7], (C, R), C ** -0.5, 0.75),
        "output_factor": centred(key_of[8], (C, R), R ** -0.5, 1.5),
        "first_factor": centred(key_of[9], (2, K1, R), 0.7, 4.0, (), jnp.float32),
        "second_factor": centred(key_of[10], (K2, R), 1.0, 5.0, (), jnp.float32),
        "third_factor": centred(key_of[11], (K3, R), 1.0, 5.0, (), jnp.float32),
    }


def product(pattern, left_op, right_op):
    return jnp.einsum(pattern, left_op.astype(jnp.float32), right_op.astype(jnp.float32), precision=lax.Precision.HIGHEST)

def retained(amount):
    position = jnp.arange(amount, dtype=jnp.int32)
    return jnp.where(position % 2 == 0, position // 2, -((position + 1) // 2))

def twiddles(frequency, length):
    phase_index = jnp.mod(frequency[:, None] * jnp.arange(length, dtype=jnp.int32)[None, :], length)
    radians = phase_index.astype(jnp.float32) * (2.0 * math.pi / length)
    return (jnp.cos(radians), jnp.sin(radians))

def rotation(frequency, length):
    cos_table, sin_table = twiddles(frequency, length)
    return jnp.stack([jnp.stack([cos_table, sin_table]), jnp.stack([-sin_table, cos_table])]).astype(jnp.bfloat16)

def transform_tables(length_one, length_two, length_three, amount_one, amount_two, amount_three):
    factor = float(length_one * length_two * length_three * amount_one * amount_two * amount_three) ** (-0.25)
    cos_table, sin_table = twiddles(retained(amount_one), length_one)
    table_one = jnp.stack([factor * cos_table, -factor * sin_table]).astype(jnp.bfloat16)
    table_two = rotation(retained(amount_two), length_two)
    table_three = rotation(jnp.arange(amount_three, dtype=jnp.int32), length_three)
    return (table_one, table_two, table_three)

def modes_of(values, tables):
    table_one, table_two, table_three = tables
    section_one = product('pjn,smcnq->pjsmcq', table_one, values).astype(jnp.bfloat16)
    section_two = product('opkq,pjsmcq->smjkoc', table_three, section_one).astype(jnp.bfloat16)
    return product('opkn,snjtpc->skjtoc', table_two, section_two).astype(jnp.bfloat16)

def cells_of(spectrum, tables):
    table_one, table_two, table_three = tables
    back_two = product('pokn,skjtpc->snjtoc', table_two, spectrum).astype(jnp.bfloat16)
    back_one = product('pokq,snjkpc->ojsncq', table_three, back_two).astype(jnp.bfloat16)
    return product('pjn,pjsmcq->smcnq', table_one, back_one)

def slot_matrix(owner_table, amount):
    return (owner_table[:, None] == jnp.arange(amount, dtype=jnp.int32)[None, :]).astype(jnp.bfloat16)

def split_weights(weights):
    weight_shape = weights.shape
    parted = weights.reshape(weight_shape[0], weight_shape[1], weight_shape[2], weight_shape[3], 2, weight_shape[3])
    return (parted[..., 0, :], parted[..., 1, :])

def dense_apply(slot_form, weights):
    weight_real, weight_imag = split_weights(weights)
    slot_real, slot_imag = (slot_form[..., 0, :], slot_form[..., 1, :])
    pattern = 'sljti,jltio->sljto'
    out_real = product(pattern, slot_real, weight_real) - product(pattern, slot_imag, weight_imag)
    out_imag = product(pattern, slot_real, weight_imag) + product(pattern, slot_imag, weight_real)
    return jnp.stack([out_real, out_imag], axis=4).astype(jnp.bfloat16)

def dense_back(slot_form, grad_slots, weights):
    weight_real, weight_imag = split_weights(weights)
    slot_real, slot_imag = (slot_form[..., 0, :], slot_form[..., 1, :])
    grad_real, grad_imag = (grad_slots[..., 0, :], grad_slots[..., 1, :])
    pattern = 'sljto,jltio->sljti'
    back_real = product(pattern, grad_real, weight_real) + product(pattern, grad_imag, weight_imag)
    back_imag = product(pattern, grad_imag, weight_real) - product(pattern, grad_real, weight_imag)
    back_values = jnp.stack([back_real, back_imag], axis=4).astype(jnp.bfloat16)
    weight_pattern = 'sljti,sljto->jltio'
    wgrad_real = product(weight_pattern, slot_real, grad_real) + product(weight_pattern, slot_imag, grad_imag)
    wgrad_imag = product(weight_pattern, slot_real, grad_imag) - product(weight_pattern, slot_imag, grad_real)
    return (back_values, jnp.concatenate([wgrad_real, wgrad_imag], axis=4))

def factor_apply(spectrum, input_factor, output_factor, phase_real, phase_imag):
    coefficient = product('skjtpc,cr->skjtpr', spectrum, input_factor)
    coefficient_real, coefficient_imag = (coefficient[..., 0, :], coefficient[..., 1, :])
    scaled_real = phase_real * coefficient_real - phase_imag * coefficient_imag
    scaled_imag = phase_real * coefficient_imag + phase_imag * coefficient_real
    scaled = jnp.stack([scaled_real, scaled_imag], axis=4).astype(jnp.bfloat16)
    return (product('skjtpr,or->skjtpo', scaled, output_factor), coefficient, scaled)

def factor_back(spectrum, coefficient, scaled, grad_cold, input_factor, output_factor, phase_real, phase_imag):
    back_factor = product('skjtpo,or->skjtpr', grad_cold, output_factor)
    output_grad = product('skjtpr,skjtpo->or', scaled, grad_cold)
    coefficient_real, coefficient_imag = (coefficient[..., 0, :], coefficient[..., 1, :])
    back_real, back_imag = (back_factor[..., 0, :], back_factor[..., 1, :])
    phase_grad_real = lax.optimization_barrier(jnp.sum(back_real * coefficient_real + back_imag * coefficient_imag, axis=0))
    phase_grad_imag = lax.optimization_barrier(jnp.sum(back_imag * coefficient_real - back_real * coefficient_imag, axis=0))
    coefficient_grad = jnp.stack([phase_real * back_real + phase_imag * back_imag, phase_real * back_imag - phase_imag * back_real], axis=4).astype(jnp.bfloat16)
    input_grad = product('skjtpc,skjtpr->cr', spectrum, coefficient_grad)
    spectrum_grad = product('skjtpr,cr->skjtpc', coefficient_grad, input_factor)
    return (spectrum_grad, input_grad, output_grad, phase_grad_real, phase_grad_imag)

def reference(inputs, cotangent, dense_weights, owner_table, hot_mask, skip_weight, bias_vector, input_factor, output_factor, first_factor, second_factor, third_factor):
    tables = transform_tables(N1, N2, N3, K1, K2, K3)

    def sample_modes(values):
        return modes_of(values[None], tables)[0]
    spectrum = lax.map(sample_modes, inputs)
    slot_onehot = slot_matrix(owner_table, L2)
    slot_form = product('lf,sfjtpc->sljtpc', slot_onehot, spectrum[:, :L2]).astype(jnp.bfloat16)
    dense_out = dense_apply(slot_form, dense_weights)
    hot_low = jnp.transpose(hot_mask, (1, 0, 2)).astype(jnp.float32)
    use_dense = jnp.concatenate([hot_low, jnp.zeros((K2 - L2, K1, K3), jnp.float32)], axis=0)
    dense_flag = use_dense[None, :, :, :, None, None]
    phase_base = second_factor[:, None, None, :] * third_factor[None, None, :, :]
    phase_real = first_factor[0][None, :, None, :] * phase_base
    phase_imag = first_factor[1][None, :, None, :] * phase_base
    factor_out, coefficient, scaled = factor_apply(spectrum, input_factor, output_factor, phase_real, phase_imag)
    dense_freq = product('lf,sljtpc->sfjtpc', slot_onehot, dense_out)
    dense_full = jnp.concatenate([dense_freq, jnp.zeros_like(factor_out[:, L2:])], axis=1)
    out_spec = jnp.where(dense_flag > 0, dense_full, factor_out).astype(jnp.bfloat16)

    def forward_sample(sample_args):
        values, cot_values, spec_values = sample_args
        spatial = cells_of(spec_values[None], tables)
        pre_act = spatial + product('smcnq,co->smonq', values[None], skip_weight) + bias_vector[None, None, :, None, None]
        activated, gelu_vjp = jax.vjp(jax.nn.gelu, pre_act)
        grad_pre, = gelu_vjp(cot_values[None].astype(jnp.float32))
        grad_pre = grad_pre.astype(jnp.bfloat16)
        grad_spec = modes_of(grad_pre, tables)
        skip_part = product('smcnq,smonq->co', values[None], grad_pre)
        bias_part = lax.optimization_barrier(jnp.sum(grad_pre.astype(jnp.float32), axis=(0, 1, 3, 4)))
        return (activated.astype(jnp.bfloat16)[0], grad_pre[0], grad_spec[0], skip_part, bias_part)
    output, grad_pre, grad_spec, skip_parts, bias_parts = lax.map(forward_sample, (inputs, cotangent, out_spec))
    masked = (grad_spec.astype(jnp.float32) * dense_flag).astype(jnp.bfloat16)
    grad_slots = product('lf,sfjtpc->sljtpc', slot_onehot, masked[:, :L2]).astype(jnp.bfloat16)
    grad_cold = (grad_spec.astype(jnp.float32) * (1.0 - dense_flag)).astype(jnp.bfloat16)
    back_slots, dense_grad = dense_back(slot_form, grad_slots, dense_weights)
    spectrum_grad, in_grad, out_grad, phase_grad_real, phase_grad_imag = factor_back(spectrum, coefficient, scaled, grad_cold, input_factor, output_factor, phase_real, phase_imag)
    back_freq = product('lf,sljtpc->sfjtpc', slot_onehot, back_slots)
    back_full = jnp.concatenate([back_freq, jnp.zeros_like(spectrum_grad[:, L2:])], axis=1)
    grad_spectrum = (spectrum_grad + back_full).astype(jnp.bfloat16)

    def backward_sample(sample_args):
        spec_values, pre_values = sample_args
        spatial = cells_of(spec_values[None], tables)
        return (spatial + product('smonq,co->smcnq', pre_values[None], skip_weight)).astype(jnp.bfloat16)[0]
    input_grad = lax.map(backward_sample, (grad_spectrum, grad_pre))
    grad_scale = float(SAMPLES * N1 * N2 * N3) ** (-0.5)
    first_grad = jnp.stack([lax.optimization_barrier(jnp.sum(phase_grad_real * phase_base, axis=(0, 2))), lax.optimization_barrier(jnp.sum(phase_grad_imag * phase_base, axis=(0, 2)))])
    mixed_phase = phase_grad_real * first_factor[0][None, :, None, :] + phase_grad_imag * first_factor[1][None, :, None, :]
    second_grad = lax.optimization_barrier(jnp.sum(mixed_phase * third_factor[None, None, :, :], axis=(1, 2)))
    third_grad = lax.optimization_barrier(jnp.sum(mixed_phase * second_factor[:, None, None, :], axis=(0, 1)))
    skip_grad = lax.optimization_barrier(jnp.sum(skip_parts, axis=0))
    bias_grad = lax.optimization_barrier(jnp.sum(bias_parts, axis=0))
    return (output, input_grad, dense_grad, in_grad * grad_scale, out_grad * grad_scale, first_grad * grad_scale, second_grad * grad_scale, third_grad * grad_scale, skip_grad * grad_scale, bias_grad * grad_scale)
```

```python
import math

import jax
import jax.numpy as jnp
import ml_dtypes
import numpy as np
from jax import lax
from jax.experimental import pallas as pl
from jax.experimental.pallas import tpu as pltpu
from jax.sharding import PartitionSpec as P

MESH = pl.DeviceIdType.MESH
F32 = jnp.float32
BF16 = jnp.bfloat16
HIGH = lax.Precision.HIGHEST

C = 64
N1 = 64
N2 = 64
N3 = 128
K1 = 32
K2 = 32
K3 = 16
L2 = 16
R = 16
SAMPLES = 8
NS = 32
NB = 8
ROWS = N2 // NS
CG = 8
CQ = 8
SLOTS = L2 // NB
GRAD_SCALE = float(SAMPLES * N1 * N2 * N3) ** (-0.5)


def rounded(values):
    return np.asarray(values, np.float32).astype(ml_dtypes.bfloat16)


def twiddles(frequency, length):
    index = np.mod(frequency[:, None] * np.arange(length)[None, :], length)
    radians = index.astype(np.float32) * np.float32(2.0 * math.pi / length)
    return np.cos(radians), np.sin(radians)


def retained(amount):
    position = np.arange(amount)
    return np.where(position % 2 == 0, position // 2, -((position + 1) // 2))


def build_tables():
    factor = float(N1 * N2 * N3 * K1 * K2 * K3) ** (-0.25)
    cos1, sin1 = twiddles(retained(K1), N1)
    t0 = np.float32(factor) * cos1
    t1 = np.float32(-factor) * sin1
    one = np.block([[t0, -t1], [t1, t0]])
    cos2, sin2 = twiddles(retained(K2), N2)
    two = np.zeros((2, K2, N2, 2), np.float32)
    two[0, :, :, 0] = cos2
    two[0, :, :, 1] = sin2
    two[1, :, :, 0] = -sin2
    two[1, :, :, 1] = cos2
    two = two.reshape(2 * K2, 2 * N2)
    cos3, sin3 = twiddles(np.arange(K3), N3)
    three = np.zeros((CQ, N3, 2, K3, CQ), np.float32)
    for q in range(CQ):
        three[q, :, 0, :, q] = cos3.T
        three[q, :, 1, :, q] = -sin3.T
    three = three.reshape(CQ * N3, 2 * K3 * CQ)
    eye = np.eye(R, dtype=np.float32)

    def tiled(signs):
        return np.concatenate([sign * eye for sign in signs] + [np.zeros((R, 64), np.float32)], axis=1)

    patterns = np.concatenate(
        [
            tiled((1, 0, 0, 1)),
            tiled((1, 0, 1, 0)),
            tiled((0, 1, -1, 0)),
            tiled((0, 1, 0, 1)),
            tiled((1, 0, 0, -1)),
            tiled((0, 1, 1, 0)),
        ],
        axis=1,
    )
    spread = np.stack([tiled((1, 1, 1, 1)), tiled((1, 1, 0, 0)), tiled((0, 0, 1, 1))])
    select = np.zeros((K3, K3, 128), np.float32)
    for k in range(K3):
        select[k, k] = 1.0
    return (
        rounded(three),
        rounded(three.T),
        rounded(one),
        rounded(one.T),
        rounded(two),
        rounded(two.T),
        rounded(patterns),
        spread.astype(np.float32),
        rounded(select.reshape(K3, K3 * 128)),
    )


def dot(a, b, precision=None):
    return jnp.dot(a, b, preferred_element_type=F32, precision=precision)


def dot_nt(a, b):
    return lax.dot_general(a, b, (((1,), (1,)), ((), ())), preferred_element_type=F32)


def dot_tn(a, b):
    return lax.dot_general(a, b, (((0,), (0,)), ((), ())), preferred_element_type=F32)


def lanes(shape):
    return lax.broadcasted_iota(jnp.int32, shape, len(shape) - 1)


def rows(shape):
    return lax.broadcasted_iota(jnp.int32, shape, 0)


def swap_groups(parts):
    parts = list(parts)
    group = lanes(parts[0].shape) // CQ
    for bit in (1, 2, 4, 8):
        low = (group & bit) == 0
        for a in range(16):
            if a & bit:
                continue
            first, second = parts[a], parts[a + bit]
            parts[a] = jnp.where(low, first, pltpu.roll(second, 8 * bit, 1))
            parts[a + bit] = jnp.where(low, pltpu.roll(first, 128 - 8 * bit, 1), second)
    return parts


def kernel(
    x_ref,
    hot_ref,
    skip_ref,
    fin_ref,
    fout_ref,
    first_ref,
    second_ref,
    third_ref,
    three_ref,
    three_t_ref,
    one_ref,
    one_t_ref,
    two_ref,
    two_t_ref,
    pat_ref,
    spread_ref,
    select_ref,
    owner_ref,
    bias_ref,
    cot_hbm,
    w_hbm,
    out_hbm,
    ig_hbm,
    dg_hbm,
    red_ref,
    cot_v,
    w_v,
    out_v,
    gp_v,
    ig_v,
    dg_v,
    skip_v,
    kron_v,
    left_v,
    zf,
    sbuf,
    rbuf,
    bsend,
    brecv,
    sm,
    s16,
    maskf,
    ph,
    coef_b,
    prod_v,
    fac_v,
    xs,
    bz,
    sgs,
    in_sem,
    out_sem,
    ssend,
    srecv,
    bssem,
    brsem,
):
    me_s = lax.axis_index("space")
    me_b = lax.axis_index("batch")
    cot_copy = pltpu.make_async_copy(cot_hbm, cot_v, in_sem.at[0])
    cot_copy.start()
    w_copy = pltpu.make_async_copy(w_hbm.at[0], w_v, in_sem.at[1])
    w_copy.start()

    barrier = pltpu.get_barrier_semaphore()

    @pl.loop(1, NS)
    def _(d):
        pl.semaphore_signal(
            barrier, inc=1, device_id={"space": lax.rem(me_s + d, NS)}, device_id_type=MESH
        )

    @pl.loop(1, NB)
    def _(d):
        pl.semaphore_signal(
            barrier, inc=1, device_id={"batch": lax.rem(me_b + d, NB)}, device_id_type=MESH
        )

    def space_start(phase):
        @pl.loop(1, NS)
        def _(d):
            peer = lax.rem(me_s + d, NS)
            pltpu.make_async_remote_copy(
                src_ref=sbuf.at[phase, peer],
                dst_ref=rbuf.at[phase, me_s],
                send_sem=ssend.at[phase],
                recv_sem=srecv.at[phase],
                device_id={"space": peer},
                device_id_type=MESH,
            ).start()

        rbuf[phase, me_s] = sbuf[phase, me_s]

    def space_wait(phase):
        block = rbuf.at[phase, pl.ds(0, NS - 1)]
        pltpu.make_async_copy(block, block, srecv.at[phase]).wait()

    def batch_start(phase):
        @pl.loop(1, NB)
        def _(d):
            peer = lax.rem(me_b + d, NB)
            pltpu.make_async_remote_copy(
                src_ref=bsend.at[phase, peer],
                dst_ref=brecv.at[phase, me_b],
                send_sem=bssem.at[phase],
                recv_sem=brsem.at[phase],
                device_id={"batch": peer},
                device_id_type=MESH,
            ).start()

        brecv[phase, me_b] = bsend[phase, me_b]

    def batch_wait(phase):
        block = brecv.at[phase, pl.ds(0, NB - 1)]
        pltpu.make_async_copy(block, block, brsem.at[phase]).wait()

    def forward_cells(src, phase):
        for n in range(ROWS):
            total = None
            for q in range(0, CQ, 2):
                pair = jnp.concatenate(
                    [src[n, :, q].reshape(CG * N1, N3), src[n, :, q + 1].reshape(CG * N1, N3)], axis=1
                )
                term = dot(pair, three_ref[q * N3 : (q + 2) * N3, :])
                total = term if total is None else total + term
            total = total.astype(BF16)
            right = jnp.concatenate(
                [
                    jnp.concatenate(
                        [total[g * N1 : (g + 1) * N1, :128], total[g * N1 : (g + 1) * N1, 128:]], axis=0
                    )
                    for g in range(CG)
                ],
                axis=1,
            )
            modes = dot(one_ref[...], right)
            for g in range(CG):
                for part in range(2):
                    zf[pl.ds(n * 16 + part * 8 + g, K1, stride=32), :] = modes[
                        part * K1 : (part + 1) * K1, g * 128 : (g + 1) * 128
                    ]
        sbuf[phase] = zf[...].astype(BF16).reshape(NS, 32, 128)

    def modes_in(phase, table):
        zf[...] = rbuf[phase].reshape(NS * 32, 128).astype(F32)
        cells = jnp.concatenate(
            [zf[pl.ds(g, 2 * N2, stride=8), :].astype(BF16) for g in range(CG)], axis=1
        )
        modes = dot(table, cells)
        parts = [
            modes[part * K2 : (part + 1) * K2, g * 128 : (g + 1) * 128]
            for part in range(2)
            for g in range(CG)
        ]
        return swap_groups(parts)

    def modes_out(by_frequency, table, phase):
        parts = swap_groups(by_frequency)
        spectrum = jnp.concatenate(
            [
                jnp.concatenate([parts[part * CG + g] for g in range(CG)], axis=1).astype(BF16)
                for part in range(2)
            ],
            axis=0,
        )
        cells = dot(table, spectrum)
        for g in range(CG):
            zf[pl.ds(g, 2 * N2, stride=8), :] = cells[:, g * 128 : (g + 1) * 128]
        sbuf[phase] = zf[...].astype(BF16).reshape(NS, 32, 128)

    def backward_rows(phase):
        zf[...] = rbuf[phase].reshape(NS * 32, 128).astype(F32)
        for n in range(ROWS):
            block = jnp.concatenate(
                [
                    jnp.concatenate(
                        [
                            zf[pl.ds(n * 16 + part * 8 + g, K1, stride=32), :].astype(BF16)
                            for part in range(2)
                        ],
                        axis=0,
                    )
                    for g in range(CG)
                ],
                axis=1,
            )
            field = dot(one_t_ref[...], block).astype(BF16)
            for g in range(CG):
                left_v[n, g * N1 : (g + 1) * N1, :128] = field[:N1, g * 128 : (g + 1) * 128]
                left_v[n, g * N1 : (g + 1) * N1, 128:] = field[N1:, g * 128 : (g + 1) * 128]

    def each_pair(body):
        @pl.loop(0, ROWS * CQ // 2)
        def _(step):
            n = step // (CQ // 2)
            pair = lax.rem(step, CQ // 2)
            column = pl.multiple_of(pair * 256, 256)
            field = dot(left_v[n], three_t_ref[:, pl.ds(column, 256)])
            for half in range(2):
                body(n, pair * 2 + half, field[:, half * 128 : (half + 1) * 128].reshape(CG, N1, N3))

    def mix_channels(src, with_bias):
        @pl.loop(0, N1 // 16)
        def _(step):
            cut = pl.ds(pl.multiple_of(step * 16, 16), 16)
            right = jnp.concatenate(
                [src[n, :, :, cut, :].reshape(C * 16, N3) for n in range(ROWS)], axis=1
            )
            mixed = dot(kron_v[...], right)
            for n in range(ROWS):
                value = mixed[:, n * N3 : (n + 1) * N3].reshape(C, 16, N3)
                if with_bias:
                    value = jnp.concatenate([value[c : c + 1] + bias_ref[c] for c in range(C)], axis=0)
                skip_v[n, :, :, cut, :] = value.reshape(CG, CQ, 16, N3)

    spread_rows = (rows((C * 16, C)) // 16 == lanes((C * 16, C))).astype(F32)
    spread_half = spread_rows.astype(BF16)

    def build_kron(base):
        expanded = dot(spread_half, base).astype(BF16)
        for block in range(4):
            cut = slice(block * 256, (block + 1) * 256)
            full = dot_nt(expanded[cut], spread_half)
            same = (rows((256, 1024)) & 15) == (lanes((256, 1024)) & 15)
            kron_v[cut, :] = jnp.where(same, full, 0.0).astype(BF16)

    forward_cells(x_ref, 0)
    pl.semaphore_wait(barrier, NS - 1 + NB - 1)
    space_start(0)

    side = (2 * K2, 2 * K2)

    def permutation(index, other):
        position = index & (K2 - 1)
        target = index
        for slot in range(L2):
            target = jnp.where(position == slot, index - position + owner_ref[slot], target)
        return (target == other).astype(F32)

    perm = permutation(rows(side), lanes(side))
    perm_t = permutation(lanes(side), rows(side))
    perm_half = perm.astype(BF16)
    two = dot(perm_half, two_ref[...]).astype(BF16)
    two_t = dot_nt(two_t_ref[...], perm_half).astype(BF16)
    second = dot(perm[:K2, :K2], second_ref[...], HIGH)
    second_l = dot(second, spread_ref[0], HIGH)
    third_l = dot(third_ref[...], spread_ref[0], HIGH)
    first_l = (
        dot(jnp.broadcast_to(first_ref[0, pl.ds(me_s, 1), :], (8, R)), spread_ref[1], HIGH)
        + dot(jnp.broadcast_to(first_ref[1, pl.ds(me_s, 1), :], (8, R)), spread_ref[2], HIGH)
    )[0:1]
    for k in range(K3):
        ph[k * K2 : (k + 1) * K2, :] = first_l * (second_l * third_l[k : k + 1])
    hot = dot(perm_half[:L2, :L2], hot_ref[0].astype(F32).astype(BF16)).astype(BF16)
    spread_hot = dot(hot, select_ref[...])
    for k in range(K3):
        maskf[k] = spread_hot[:, k * 128 : (k + 1) * 128]

    def expand(factor, top, bottom, width):
        pieces = [
            dot(factor, pat_ref[:, start * 128 : start * 128 + width]) for start in (top, bottom)
        ]
        return jnp.concatenate(pieces, axis=0).astype(BF16)

    fin_all = expand(fin_ref[...], 0, 2, 256)
    fin_b = fin_all[:, 128:]
    fout_b = expand(fout_ref[...], 1, 3, 128)
    fout_c = expand(fout_ref[...], 4, 5, 128)

    build_kron(skip_ref[...].astype(F32).T.astype(BF16))
    mix_channels(x_ref, True)

    space_wait(0)
    spectrum = modes_in(0, two)
    for k in range(K3):
        sm[k * K2 : (k + 1) * K2, :] = spectrum[k]

    def slots_out(phase):
        for owner in range(NB):
            for slot in range(SLOTS):
                bsend[phase, owner, slot * K3 : (slot + 1) * K3, :] = sm[
                    pl.ds(owner * SLOTS + slot, K3, stride=K2), :
                ].astype(BF16)

    def slots_in(phase):
        bz[...] = brecv[phase].reshape(NB * 32, 128).astype(F32)
        for slot in range(L2):
            sm[pl.ds(slot, K3, stride=K2), :] = bz[slot * K3 : (slot + 1) * K3, :]

    slots_out(0)
    batch_start(0)
    s16[...] = sm[...].astype(BF16)
    coef = dot(s16[...], fin_all)
    coef_b[...] = coef[:, 128:]
    prod_v[...] = (coef[:, :128] * ph[...]).astype(BF16)
    fac_v[...] = dot_nt(prod_v[...], fout_b)
    w_copy.wait()
    batch_wait(0)
    xs[...] = brecv[0].reshape(NB * 32, 128).astype(F32)
    sign = jnp.where(lanes((8, 128)) < 64, -1.0, 1.0)
    for index in range(SLOTS * K3):
        slot, k = divmod(index, K3)
        value = xs[pl.ds(index, NB, stride=32), :]
        left = jnp.concatenate([value, pltpu.roll(value, 64, 1)], axis=0)[:, :C].astype(BF16)
        both = dot(left, w_v[slot, k])
        bz[pl.ds(index, NB, stride=32), :] = both[:8] + sign * pltpu.roll(both[8:], 64, 1)
    bsend[1] = bz[...].astype(BF16).reshape(NB, 32, 128)
    batch_start(1)
    batch_wait(1)
    slots_in(1)
    out_spec = []
    for k in range(K3):
        low = jnp.where(
            maskf[k] > 0.0, sm[k * K2 : k * K2 + L2, :], fac_v[k * K2 : k * K2 + L2, :]
        )
        out_spec.append(jnp.concatenate([low, fac_v[k * K2 + L2 : (k + 1) * K2, :]], axis=0))
    modes_out(out_spec, two_t, 1)
    space_start(1)
    cot_copy.wait()
    space_wait(1)
    backward_rows(1)

    def activate(n, q, field):
        v = field + skip_v[n, :, q]
        square = v * v
        k0 = math.sqrt(2.0 / math.pi)
        gate = 0.5 * jnp.tanh(v * (k0 + (k0 * 0.044715) * square)) + 0.5
        active = v * gate
        out_v[n, :, q] = active.astype(BF16)
        slope = gate + active * (1.0 - gate) * (2.0 * k0 + (6.0 * k0 * 0.044715) * square)
        gp_v[n, :, q] = (cot_v[n, :, q].astype(F32) * slope).astype(BF16)

    each_pair(activate)
    out_copy = pltpu.make_async_copy(out_v, out_hbm, out_sem.at[0])
    out_copy.start()

    forward_cells(gp_v, 2)
    space_start(2)

    build_kron(skip_ref[...])
    mix_channels(gp_v, False)
    same = ((rows((16, 256)) & 15) == (lanes((16, 256)) & 15)).astype(F32)
    ones = jnp.ones((16, ROWS * 4 * N3), BF16)

    def cut_channels(src, start):
        return jnp.concatenate(
            [
                src[n, pl.ds(start * 2, 2), :, b * 16 : (b + 1) * 16, :].reshape(256, N3)
                for n in range(ROWS)
                for b in range(N1 // 16)
            ],
            axis=1,
        )

    for column in range(4):
        grads = cut_channels(gp_v, column)
        here = slice(column * 256, (column + 1) * 256)
        sgs[C : C + 16, here] = dot_nt(ones, grads)

        @pl.loop(0, 4)
        def _(block):
            full = dot_nt(cut_channels(x_ref, block), grads).reshape(16, 16, 256)
            sgs[pl.ds(pl.multiple_of(block * 16, 16), 16), here] = jnp.sum(full * same[None], axis=1)

    skip_grad = dot(sgs[...], spread_rows, HIGH)

    space_wait(2)
    grad_spec = modes_in(2, two)
    cold = []
    for k in range(K3):
        low = grad_spec[k][:L2]
        sm[k * K2 : k * K2 + L2, :] = low * maskf[k]
        cold.append(
            jnp.concatenate([low * (1.0 - maskf[k]), grad_spec[k][L2:]], axis=0).astype(BF16)
        )
    slots_out(2)
    batch_start(2)
    cold = jnp.concatenate(cold, axis=0)
    back = dot(cold, fout_c)
    prod_back = (back * ph[...]).astype(BF16)
    fac_v[...] = dot_nt(prod_back, fin_b)
    in_full = dot_tn(s16[...], prod_back)
    out_full = dot_tn(cold, prod_v[...])
    back = back * coef_b[...]
    first_sum = jnp.zeros((K2, 128), F32)
    second_sum = jnp.zeros((K2, 128), F32)
    third_rows = []
    for k in range(K3):
        term = back[k * K2 : (k + 1) * K2]
        by_third = term * third_l[k : k + 1]
        first_sum = first_sum + by_third * second_l
        second_sum = second_sum + by_third * first_l
        third_rows.append(jnp.sum(term * first_l * second_l, axis=0, keepdims=True))
    first_row = jnp.sum(first_sum, axis=0, keepdims=True)
    third_sum = jnp.concatenate(third_rows, axis=0)

    batch_wait(2)
    bz[...] = brecv[2].reshape(NB * 32, 128).astype(F32)
    for index in range(SLOTS * K3):
        slot, k = divmod(index, K3)
        value = xs[pl.ds(index, NB, stride=32), :]
        grad = bz[pl.ds(index, NB, stride=32), :]
        left = jnp.concatenate([value, pltpu.roll(value, 64, 1)], axis=0).astype(BF16)
        grads = jnp.concatenate([grad, -sign * pltpu.roll(grad, 64, 1)], axis=0).astype(BF16)
        weights = w_v[slot, k]
        both = dot_nt(grads, jnp.concatenate([weights, weights], axis=0))
        bz[pl.ds(index, NB, stride=32), :] = jnp.where(sign < 0.0, both[:8], both[8:])
        dg_v[slot, k] = dot_tn(left, grads)[:C]
    bsend[3] = bz[...].astype(BF16).reshape(NB, 32, 128)
    batch_start(3)
    dg_copy = pltpu.make_async_copy(dg_v, dg_hbm.at[0], out_sem.at[1])
    dg_copy.start()
    batch_wait(3)
    slots_in(3)
    grad_spectrum = []
    for k in range(K3):
        low = fac_v[k * K2 : k * K2 + L2, :] + sm[k * K2 : k * K2 + L2, :]
        grad_spectrum.append(
            jnp.concatenate([low, fac_v[k * K2 + L2 : (k + 1) * K2, :]], axis=0)
        )
    modes_out(grad_spectrum, two_t, 3)
    space_start(3)

    def left_by(value, amount):
        return pltpu.roll(value, 128 - amount, 1)

    def folded(full):
        pairs = full + left_by(full, 32)
        return pairs[:C] + left_by(pairs[C:], 16)

    shape = (C, 128)
    lane, row = lanes(shape), rows(shape)

    def below(value):
        return jnp.concatenate([value, jnp.zeros((C - value.shape[0], 128), F32)], axis=0)

    def fold_all(value):
        pairs = value + left_by(value, 16)
        return pairs + left_by(pairs, 32)

    second_part = dot(perm_t[:K2, :K2], fold_all(second_sum), HIGH)
    third_part = fold_all(third_sum)
    first_part = first_row + left_by(first_row, 16)
    middle = jnp.concatenate([second_part, third_part, jnp.zeros((16, 128), F32)], axis=0)
    zero64 = jnp.zeros((C, 64), F32)
    wide = jnp.concatenate([skip_grad[:C], zero64], axis=1)
    bias_row = jnp.concatenate([skip_grad[C : C + 1], zero64[:1]], axis=1)
    packed = jnp.where(lane < 64, wide, 0.0)
    packed = jnp.where((lane >= 64) & (lane < 80), pltpu.roll(folded(in_full), 64, 1), packed)
    packed = jnp.where((lane >= 80) & (lane < 96), pltpu.roll(folded(out_full), 80, 1), packed)
    inside = (lane >= 96) & (lane < 112)
    packed = jnp.where(inside, pltpu.roll(middle, 96, 1), packed)
    for piece in range(4):
        moved = pltpu.roll(bias_row, 96 - 16 * piece, 1)
        packed = jnp.where(inside & (row == 48 + piece), moved, packed)
    last = lane >= 112
    packed = jnp.where(last & (row == me_s), pltpu.roll(first_part, 112, 1), packed)
    packed = jnp.where(last & (row == me_s + 32), pltpu.roll(first_part, 80, 1), packed)
    red_ref[...] = packed * GRAD_SCALE

    space_wait(3)
    backward_rows(3)

    def finish(n, q, field):
        ig_v[n, :, q] = (field + skip_v[n, :, q]).astype(BF16)

    each_pair(finish)
    ig_copy = pltpu.make_async_copy(ig_v, ig_hbm, out_sem.at[2])
    ig_copy.start()
    for phase in range(4):
        block = sbuf.at[phase, pl.ds(0, NS - 1)]
        pltpu.make_async_copy(block, block, ssend.at[phase]).wait()
        block = bsend.at[phase, pl.ds(0, NB - 1)]
        pltpu.make_async_copy(block, block, bssem.at[phase]).wait()
    out_copy.wait()
    dg_copy.wait()
    ig_copy.wait()


def local(
    inputs,
    cotangent,
    dense_weights,
    owner_table,
    hot_mask,
    skip_weight,
    bias_vector,
    input_factor,
    output_factor,
    first_factor,
    second_factor,
    third_factor,
):
    field = (ROWS, CG, CQ, N1, N3)
    tables = [jnp.asarray(table) for table in build_tables()]
    vmem = pl.BlockSpec(memory_space=pltpu.VMEM)
    smem = pl.BlockSpec(memory_space=pltpu.SMEM)
    hbm = pl.BlockSpec(memory_space=pl.ANY)
    dense = (SLOTS, K3, C, 2 * C)
    output, input_grad, dense_grad, packed = pl.pallas_call(
        kernel,
        out_shape=(
            jax.ShapeDtypeStruct(field, BF16),
            jax.ShapeDtypeStruct(field, BF16),
            jax.ShapeDtypeStruct((1,) + dense, F32),
            jax.ShapeDtypeStruct((C, 128), F32),
        ),
        in_specs=[vmem] * 17 + [smem, smem, hbm, hbm],
        out_specs=(hbm, hbm, hbm, vmem),
        scratch_shapes=[
            pltpu.VMEM(field, BF16),
            pltpu.VMEM(dense, BF16),
            pltpu.VMEM(field, BF16),
            pltpu.VMEM(field, BF16),
            pltpu.VMEM(field, BF16),
            pltpu.VMEM(dense, F32),
            pltpu.VMEM(field, F32),
            pltpu.VMEM((C * 16, C * 16), BF16),
            pltpu.VMEM((ROWS, CG * N1, 256), BF16),
            pltpu.VMEM((NS * 32, 128), F32),
            pltpu.VMEM((4, NS, 32, 128), BF16),
            pltpu.VMEM((4, NS, 32, 128), BF16),
            pltpu.VMEM((4, NB, 32, 128), BF16),
            pltpu.VMEM((4, NB, 32, 128), BF16),
            pltpu.VMEM((K3 * K2, 128), F32),
            pltpu.VMEM((K3 * K2, 128), BF16),
            pltpu.VMEM((K3, L2, 128), F32),
            pltpu.VMEM((K3 * K2, 128), F32),
            pltpu.VMEM((K3 * K2, 128), F32),
            pltpu.VMEM((K3 * K2, 128), BF16),
            pltpu.VMEM((K3 * K2, 128), F32),
            pltpu.VMEM((NB * 32, 128), F32),
            pltpu.VMEM((NB * 32, 128), F32),
            pltpu.VMEM((C + 16, C * 16), F32),
            pltpu.SemaphoreType.DMA((2,)),
            pltpu.SemaphoreType.DMA((3,)),
            pltpu.SemaphoreType.DMA((4,)),
            pltpu.SemaphoreType.DMA((4,)),
            pltpu.SemaphoreType.DMA((4,)),
            pltpu.SemaphoreType.DMA((4,)),
        ],
        compiler_params=pltpu.CompilerParams(
            collective_id=0, has_side_effects=True, vmem_limit_bytes=50 * 2**20
        ),
    )(
        inputs.reshape(field),
        hot_mask,
        skip_weight,
        input_factor,
        output_factor,
        first_factor,
        second_factor,
        third_factor,
        *tables,
        owner_table,
        bias_vector,
        cotangent.reshape(field),
        dense_weights,
    )
    packed = lax.psum(packed, ("space", "batch"))
    return (
        output.reshape(inputs.shape),
        input_grad.reshape(inputs.shape),
        dense_grad,
        packed[:, 64:80],
        packed[:, 80:96],
        packed[:, 112:].reshape(2, K1, R),
        packed[:K2, 96:112],
        packed[K2 : K2 + K3, 96:112],
        packed[:, :64],
        packed[48:52, 96:112].reshape(C),
    )


def solution(mesh):
    field = P("batch", "space", None, None, None)
    dense = P("space", "batch", None, None, None)
    whole = P()
    return jax.shard_map(
        local,
        mesh=mesh,
        in_specs=(field, field, dense, whole, P("space", None, None)) + (whole,) * 7,
        out_specs=(field, field, dense) + (whole,) * 7,
        check_vma=False,
    )
```

```python
import math

import jax
import jax.numpy as jnp
import ml_dtypes
import numpy as np
from jax import lax
from jax.experimental import pallas as pl
from jax.experimental.pallas import tpu as pltpu
from jax.sharding import PartitionSpec as P

MESH = pl.DeviceIdType.MESH
F32 = jnp.float32
BF16 = jnp.bfloat16
HIGH = lax.Precision.HIGHEST

C = 64
N1 = 64
N2 = 64
N3 = 128
K1 = 32
K2 = 32
K3 = 16
L2 = 16
R = 16
SAMPLES = 8
NS = 32
NB = 8
ROWS = N2 // NS
CG = 8
CQ = 8
SLOTS = L2 // NB
GRAD_SCALE = float(SAMPLES * N1 * N2 * N3) ** (-0.5)


def rounded(values):
    return np.asarray(values, np.float32).astype(ml_dtypes.bfloat16)


def twiddles(frequency, length):
    index = np.mod(frequency[:, None] * np.arange(length)[None, :], length)
    radians = index.astype(np.float32) * np.float32(2.0 * math.pi / length)
    return np.cos(radians), np.sin(radians)


def retained(amount):
    position = np.arange(amount)
    return np.where(position % 2 == 0, position // 2, -((position + 1) // 2))


def build_tables():
    factor = float(N1 * N2 * N3 * K1 * K2 * K3) ** (-0.25)
    cos1, sin1 = twiddles(retained(K1), N1)
    t0 = np.float32(factor) * cos1
    t1 = np.float32(-factor) * sin1
    one = np.block([[t0, -t1], [t1, t0]])
    cos2, sin2 = twiddles(retained(K2), N2)
    two = np.zeros((2, K2, N2, 2), np.float32)
    two[0, :, :, 0] = cos2
    two[0, :, :, 1] = sin2
    two[1, :, :, 0] = -sin2
    two[1, :, :, 1] = cos2
    two = two.reshape(2 * K2, 2 * N2)
    cos3, sin3 = twiddles(np.arange(K3), N3)
    three = np.zeros((CQ, N3, 2, K3, CQ), np.float32)
    for q in range(CQ):
        three[q, :, 0, :, q] = cos3.T
        three[q, :, 1, :, q] = -sin3.T
    three = three.reshape(CQ * N3, 2 * K3 * CQ)
    eye = np.eye(R, dtype=np.float32)

    def tiled(signs):
        return np.concatenate([sign * eye for sign in signs] + [np.zeros((R, 64), np.float32)], axis=1)

    patterns = np.concatenate(
        [
            tiled((1, 0, 0, 1)),
            tiled((1, 0, 1, 0)),
            tiled((0, 1, -1, 0)),
            tiled((0, 1, 0, 1)),
            tiled((1, 0, 0, -1)),
            tiled((0, 1, 1, 0)),
        ],
        axis=1,
    )
    spread = np.stack([tiled((1, 1, 1, 1)), tiled((1, 1, 0, 0)), tiled((0, 0, 1, 1))])
    select = np.zeros((K3, K3, 128), np.float32)
    for k in range(K3):
        select[k, k] = 1.0
    return (
        rounded(three),
        rounded(three.T),
        rounded(one),
        rounded(one.T),
        rounded(two),
        rounded(two.T),
        rounded(patterns),
        spread.astype(np.float32),
        rounded(select.reshape(K3, K3 * 128)),
    )


def dot(a, b, precision=None):
    return jnp.dot(a, b, preferred_element_type=F32, precision=precision)


def dot_nt(a, b, precision=None):
    return lax.dot_general(
        a, b, (((1,), (1,)), ((), ())), preferred_element_type=F32, precision=precision
    )


def dot_tn(a, b):
    return lax.dot_general(a, b, (((0,), (0,)), ((), ())), preferred_element_type=F32)


def lanes(shape):
    return lax.broadcasted_iota(jnp.int32, shape, len(shape) - 1)


def rows(shape):
    return lax.broadcasted_iota(jnp.int32, shape, 0)


def swap_groups(parts):
    parts = list(parts)
    group = lanes(parts[0].shape) // CQ
    for bit in (1, 2, 4, 8):
        low = (group & bit) == 0
        for a in range(16):
            if a & bit:
                continue
            first, second = parts[a], parts[a + bit]
            parts[a] = jnp.where(low, first, pltpu.roll(second, 8 * bit, 1))
            parts[a + bit] = jnp.where(low, pltpu.roll(first, 128 - 8 * bit, 1), second)
    return parts


def left_by(value, amount):
    return pltpu.roll(value, 128 - amount, 1)


def drain(block, sem):
    pltpu.make_async_copy(block, block, sem).wait()


def backward_rows(blocks, zf, left_v, one_t):
    zf[...] = blocks.reshape(NS * 32, 128).astype(F32)
    for n in range(ROWS):
        block = jnp.concatenate(
            [
                jnp.concatenate(
                    [
                        zf[pl.ds(n * 16 + part * 8 + g, K1, stride=32), :].astype(BF16)
                        for part in range(2)
                    ],
                    axis=0,
                )
                for g in range(CG)
            ],
            axis=1,
        )
        field = dot(one_t, block).astype(BF16)
        for g in range(CG):
            left_v[n, g * N1 : (g + 1) * N1, :128] = field[:N1, g * 128 : (g + 1) * 128]
            left_v[n, g * N1 : (g + 1) * N1, 128:] = field[N1:, g * 128 : (g + 1) * 128]


def each_pair(n, left_v, three_t, body):
    @pl.loop(0, CQ // 2)
    def _(pair):
        column = pl.multiple_of(pair * 256, 256)
        field = dot(left_v[n], three_t[:, pl.ds(column, 256)])
        for half in range(2):
            body(pair * 2 + half, field[:, half * 128 : (half + 1) * 128].reshape(CG, N1, N3))


def kernel(
    owner_ref,
    bias_ref,
    x_hbm,
    three_hbm,
    one_hbm,
    hot_hbm,
    skip_hbm,
    fin_hbm,
    fout_hbm,
    first_hbm,
    second_hbm,
    third_hbm,
    two_hbm,
    two_t_hbm,
    pat_hbm,
    spread_hbm,
    select_hbm,
    one_t_hbm,
    three_t_hbm,
    cot_hbm,
    w_hbm,
    out_hbm,
    skip_out_hbm,
    dg_hbm,
    blocks_ref,
    red_ref,
    x_ref,
    three_ref,
    one_ref,
    hot_ref,
    skip_ref,
    fin_ref,
    fout_ref,
    first_ref,
    second_ref,
    third_ref,
    two_ref,
    two_t_ref,
    pat_ref,
    spread_ref,
    select_ref,
    one_t_ref,
    three_t_ref,
    cot_v,
    w_v,
    out_v,
    gp_v,
    dg_v,
    skip_v,
    kron_v,
    left_v,
    zf,
    sbuf,
    rbuf,
    bsend,
    brecv,
    sm,
    s16,
    maskf,
    ph,
    coef_b,
    prod_v,
    fac_v,
    xs,
    bz,
    sgs,
    pk,
    r_batch,
    r_near,
    r_far,
    r_all,
    part_near,
    part_far,
    part_all,
    in_sem,
    out_sem,
    ssend,
    srecv,
    bssem,
    brsem,
    rsend,
    rrecv,
):
    me_s = lax.axis_index("space")
    me_b = lax.axis_index("batch")
    def fetch(src, dst, index):
        copy = pltpu.make_async_copy(src, dst, in_sem.at[index])
        copy.start()
        return copy

    x_copies = [fetch(x_hbm.at[n], x_ref.at[n], n) for n in range(ROWS)]
    three_copy = fetch(three_hbm, three_ref, 2)
    one_copy = fetch(one_hbm, one_ref, 3)
    small_copies = [
        fetch(src, dst, 4 + index)
        for index, (src, dst) in enumerate(
            (
                (hot_hbm, hot_ref),
                (skip_hbm, skip_ref),
                (fin_hbm, fin_ref),
                (fout_hbm, fout_ref),
                (first_hbm, first_ref),
                (second_hbm, second_ref),
                (third_hbm, third_ref),
                (two_hbm, two_ref),
                (two_t_hbm, two_t_ref),
                (pat_hbm, pat_ref),
                (spread_hbm, spread_ref),
                (select_hbm, select_ref),
                (one_t_hbm, one_t_ref),
                (three_t_hbm, three_t_ref),
            )
        )
    ]
    cot_copy = fetch(cot_hbm, cot_v, 18)
    w_copy = fetch(w_hbm.at[0], w_v, 19)

    barrier = pltpu.get_barrier_semaphore()

    @pl.loop(1, NS)
    def _(d):
        pl.semaphore_signal(
            barrier, inc=1, device_id={"space": lax.rem(me_s + d, NS)}, device_id_type=MESH
        )

    @pl.loop(1, NB)
    def _(d):
        pl.semaphore_signal(
            barrier, inc=1, device_id={"batch": lax.rem(me_b + d, NB)}, device_id_type=MESH
        )

    def space_start(phase):
        @pl.loop(1, NS)
        def _(d):
            peer = lax.rem(me_s + d, NS)
            pltpu.make_async_remote_copy(
                src_ref=sbuf.at[phase, peer],
                dst_ref=rbuf.at[phase, me_s],
                send_sem=ssend.at[phase],
                recv_sem=srecv.at[phase],
                device_id={"space": peer},
                device_id_type=MESH,
            ).start()

        rbuf[phase, me_s] = sbuf[phase, me_s]

    def space_wait(phase):
        drain(rbuf.at[phase, pl.ds(0, NS - 1)], srecv.at[phase])

    def batch_start(phase):
        @pl.loop(1, NB)
        def _(d):
            peer = lax.rem(me_b + d, NB)
            pltpu.make_async_remote_copy(
                src_ref=bsend.at[phase, peer],
                dst_ref=brecv.at[phase, me_b],
                send_sem=bssem.at[phase],
                recv_sem=brsem.at[phase],
                device_id={"batch": peer},
                device_id_type=MESH,
            ).start()

        brecv[phase, me_b] = bsend[phase, me_b]

    def batch_wait(phase):
        drain(brecv.at[phase, pl.ds(0, NB - 1)], brsem.at[phase])

    def forward_cells(src, phase, copies):
        for n in range(ROWS):
            if copies is not None:
                copies[n].wait()
            total = None
            for q in range(0, CQ, 2):
                pair = jnp.concatenate(
                    [src[n, :, q].reshape(CG * N1, N3), src[n, :, q + 1].reshape(CG * N1, N3)], axis=1
                )
                term = dot(pair, three_ref[q * N3 : (q + 2) * N3, :])
                total = term if total is None else total + term
            total = total.astype(BF16)
            right = jnp.concatenate(
                [
                    jnp.concatenate(
                        [total[g * N1 : (g + 1) * N1, :128], total[g * N1 : (g + 1) * N1, 128:]], axis=0
                    )
                    for g in range(CG)
                ],
                axis=1,
            )
            modes = dot(one_ref[...], right)
            for g in range(CG):
                for part in range(2):
                    zf[pl.ds(n * 16 + part * 8 + g, K1, stride=32), :] = modes[
                        part * K1 : (part + 1) * K1, g * 128 : (g + 1) * 128
                    ]
        sbuf[phase] = zf[...].astype(BF16).reshape(NS, 32, 128)

    def modes_in(phase, table):
        zf[...] = rbuf[phase].reshape(NS * 32, 128).astype(F32)
        cells = jnp.concatenate(
            [zf[pl.ds(g, 2 * N2, stride=8), :].astype(BF16) for g in range(CG)], axis=1
        )
        modes = dot(table, cells)
        parts = [
            modes[part * K2 : (part + 1) * K2, g * 128 : (g + 1) * 128]
            for part in range(2)
            for g in range(CG)
        ]
        return swap_groups(parts)

    def modes_out(by_frequency, table, phase):
        parts = swap_groups(by_frequency)
        spectrum = jnp.concatenate(
            [
                jnp.concatenate([parts[part * CG + g] for g in range(CG)], axis=1).astype(BF16)
                for part in range(2)
            ],
            axis=0,
        )
        cells = dot(table, spectrum)
        for g in range(CG):
            zf[pl.ds(g, 2 * N2, stride=8), :] = cells[:, g * 128 : (g + 1) * 128]
        sbuf[phase] = zf[...].astype(BF16).reshape(NS, 32, 128)

    def mix_channels(src, with_bias):
        @pl.loop(0, N1 // 16)
        def _(step):
            cut = pl.ds(pl.multiple_of(step * 16, 16), 16)
            right = jnp.concatenate(
                [src[n, :, :, cut, :].reshape(C * 16, N3) for n in range(ROWS)], axis=1
            )
            mixed = dot(kron_v[...], right)
            for n in range(ROWS):
                value = mixed[:, n * N3 : (n + 1) * N3].reshape(C, 16, N3)
                if with_bias:
                    value = jnp.concatenate([value[c : c + 1] + bias_ref[c] for c in range(C)], axis=0)
                skip_v[n, :, :, cut, :] = value.astype(BF16).reshape(CG, CQ, 16, N3)

    spread_rows = (rows((C * 16, C)) // 16 == lanes((C * 16, C))).astype(F32)
    spread_half = spread_rows.astype(BF16)

    def build_kron(base):
        expanded = dot(spread_half, base).astype(BF16)
        for block in range(4):
            cut = slice(block * 256, (block + 1) * 256)
            full = dot_nt(expanded[cut], spread_half)
            same = (rows((256, 1024)) & 15) == (lanes((256, 1024)) & 15)
            kron_v[cut, :] = jnp.where(same, full, 0.0).astype(BF16)

    three_copy.wait()
    one_copy.wait()
    forward_cells(x_ref, 0, x_copies)
    pl.semaphore_wait(barrier, NS - 1 + NB - 1)
    space_start(0)

    for copy in small_copies:
        copy.wait()
    side = (2 * K2, 2 * K2)

    def permutation(index, other):
        position = index & (K2 - 1)
        target = index
        for slot in range(L2):
            target = jnp.where(position == slot, index - position + owner_ref[slot], target)
        return (target == other).astype(F32)

    perm = permutation(rows(side), lanes(side))
    perm_t = permutation(lanes(side), rows(side))
    perm_half = perm.astype(BF16)
    two = dot(perm_half, two_ref[...]).astype(BF16)
    two_t = dot_nt(two_t_ref[...], perm_half).astype(BF16)
    second = dot_nt(perm[:K2, :K2], second_ref[...], HIGH)
    second_l = dot(second, spread_ref[0], HIGH)
    third_l = dot(third_ref[...], spread_ref[0], HIGH)
    own = (lanes((8, K1)) == me_s).astype(F32)
    first_l = (
        dot(dot_nt(own, first_ref[0], HIGH), spread_ref[1], HIGH)
        + dot(dot_nt(own, first_ref[1], HIGH), spread_ref[2], HIGH)
    )[0:1]
    for k in range(K3):
        ph[k * K2 : (k + 1) * K2, :] = first_l * (second_l * third_l[k : k + 1])
    hot = dot(perm_half[:L2, :L2], hot_ref[0].astype(F32).astype(BF16)).astype(BF16)
    spread_hot = dot(hot, select_ref[...])
    for k in range(K3):
        maskf[k] = spread_hot[:, k * 128 : (k + 1) * 128]

    def expand(factor, top, bottom, width):
        pieces = [
            dot_tn(factor, pat_ref[:, start * 128 : start * 128 + width]) for start in (top, bottom)
        ]
        return jnp.concatenate(pieces, axis=0).astype(BF16)

    fin_all = expand(fin_ref[...], 0, 2, 256)
    fin_b = fin_all[:, 128:]
    fout_b = expand(fout_ref[...], 1, 3, 128)
    fout_c = expand(fout_ref[...], 4, 5, 128)

    build_kron(skip_ref[...].astype(F32).T.astype(BF16))
    mix_channels(x_ref, True)

    space_wait(0)
    spectrum = modes_in(0, two)
    for k in range(K3):
        sm[k * K2 : (k + 1) * K2, :] = spectrum[k]

    def slots_out(phase):
        for owner in range(NB):
            for slot in range(SLOTS):
                bsend[phase, owner, slot * K3 : (slot + 1) * K3, :] = sm[
                    pl.ds(owner * SLOTS + slot, K3, stride=K2), :
                ].astype(BF16)

    def slots_in(phase):
        bz[...] = brecv[phase].reshape(NB * 32, 128).astype(F32)
        for slot in range(L2):
            sm[pl.ds(slot, K3, stride=K2), :] = bz[slot * K3 : (slot + 1) * K3, :]

    slots_out(0)
    batch_start(0)
    s16[...] = sm[...].astype(BF16)
    coef = dot(s16[...], fin_all)
    coef_b[...] = coef[:, 128:]
    prod_v[...] = (coef[:, :128] * ph[...]).astype(BF16)
    fac_v[...] = dot_nt(prod_v[...], fout_b)
    w_copy.wait()
    batch_wait(0)
    xs[...] = brecv[0].reshape(NB * 32, 128).astype(F32)
    sign = jnp.where(lanes((8, 128)) < 64, -1.0, 1.0)
    for index in range(SLOTS * K3):
        slot, k = divmod(index, K3)
        value = xs[pl.ds(index, NB, stride=32), :]
        left = jnp.concatenate([value, pltpu.roll(value, 64, 1)], axis=0)[:, :C].astype(BF16)
        both = dot(left, w_v[slot, k])
        bz[pl.ds(index, NB, stride=32), :] = both[:8] + sign * pltpu.roll(both[8:], 64, 1)
    bsend[1] = bz[...].astype(BF16).reshape(NB, 32, 128)
    batch_start(1)
    batch_wait(1)
    slots_in(1)
    out_spec = []
    for k in range(K3):
        low = jnp.where(
            maskf[k] > 0.0, sm[k * K2 : k * K2 + L2, :], fac_v[k * K2 : k * K2 + L2, :]
        )
        out_spec.append(jnp.concatenate([low, fac_v[k * K2 + L2 : (k + 1) * K2, :]], axis=0))
    modes_out(out_spec, two_t, 1)
    space_start(1)
    cot_copy.wait()
    space_wait(1)
    backward_rows(rbuf[1], zf, left_v, one_t_ref[...])

    for n in range(ROWS):

        def activate(q, field):
            v = field + skip_v[n, :, q].astype(F32)
            square = v * v
            k0 = math.sqrt(2.0 / math.pi)
            gate = 0.5 * jnp.tanh(v * (k0 + (k0 * 0.044715) * square)) + 0.5
            active = v * gate
            out_v[n, :, q] = active.astype(BF16)
            slope = gate + active * (1.0 - gate) * (2.0 * k0 + (6.0 * k0 * 0.044715) * square)
            gp_v[n, :, q] = (cot_v[n, :, q].astype(F32) * slope).astype(BF16)

        each_pair(n, left_v, three_t_ref, activate)
    out_copy = pltpu.make_async_copy(out_v, out_hbm, out_sem.at[0])
    out_copy.start()

    forward_cells(gp_v, 2, None)
    space_start(2)

    build_kron(skip_ref[...])
    mix_channels(gp_v, False)
    skip_copy = pltpu.make_async_copy(skip_v, skip_out_hbm, out_sem.at[2])
    skip_copy.start()
    same = ((rows((16, 256)) & 15) == (lanes((16, 256)) & 15)).astype(F32)
    ones = jnp.ones((16, ROWS * 4 * N3), BF16)

    def cut_channels(src, start):
        return jnp.concatenate(
            [
                src[n, pl.ds(start * 2, 2), :, b * 16 : (b + 1) * 16, :].reshape(256, N3)
                for n in range(ROWS)
                for b in range(N1 // 16)
            ],
            axis=1,
        )

    for column in range(4):
        grads = cut_channels(gp_v, column)
        here = slice(column * 256, (column + 1) * 256)
        sgs[C : C + 16, here] = dot_nt(ones, grads)

        @pl.loop(0, 4)
        def _(block):
            full = dot_nt(cut_channels(x_ref, block), grads).reshape(16, 16, 256)
            sgs[pl.ds(pl.multiple_of(block * 16, 16), 16), here] = jnp.sum(full * same[None], axis=1)

    skip_grad = dot(sgs[...], spread_rows, HIGH)

    space_wait(2)
    grad_spec = modes_in(2, two)
    cold = []
    for k in range(K3):
        low = grad_spec[k][:L2]
        sm[k * K2 : k * K2 + L2, :] = low * maskf[k]
        cold.append(
            jnp.concatenate([low * (1.0 - maskf[k]), grad_spec[k][L2:]], axis=0).astype(BF16)
        )
    slots_out(2)
    batch_start(2)
    cold = jnp.concatenate(cold, axis=0)
    back = dot(cold, fout_c)
    prod_back = (back * ph[...]).astype(BF16)
    fac_v[...] = dot_nt(prod_back, fin_b)
    in_full = dot_tn(s16[...], prod_back)
    out_full = dot_tn(cold, prod_v[...])
    back = back * coef_b[...]
    first_sum = jnp.zeros((K2, 128), F32)
    second_sum = jnp.zeros((K2, 128), F32)
    third_rows = []
    for k in range(K3):
        term = back[k * K2 : (k + 1) * K2]
        by_third = term * third_l[k : k + 1]
        first_sum = first_sum + by_third * second_l
        second_sum = second_sum + by_third * first_l
        third_rows.append(jnp.sum(term * first_l * second_l, axis=0, keepdims=True))
    first_row = jnp.sum(first_sum, axis=0, keepdims=True)
    third_sum = jnp.concatenate(third_rows, axis=0)

    def folded(full):
        pairs = full + left_by(full, 32)
        return pairs[:C] + left_by(pairs[C:], 16)

    shape = (C, 128)
    lane, row = lanes(shape), rows(shape)

    def below(value):
        return jnp.concatenate([value, jnp.zeros((C - value.shape[0], 128), F32)], axis=0)

    def fold_all(value):
        pairs = value + left_by(value, 16)
        return pairs + left_by(pairs, 32)

    second_part = dot(perm_t[:K2, :K2], fold_all(second_sum), HIGH)
    third_part = fold_all(third_sum)
    first_part = first_row + left_by(first_row, 16)
    middle = jnp.concatenate([second_part, third_part, jnp.zeros((16, 128), F32)], axis=0)
    zero64 = jnp.zeros((C, 64), F32)
    wide = jnp.concatenate([skip_grad[:C], zero64], axis=1)
    bias_row = jnp.concatenate([skip_grad[C : C + 1], zero64[:1]], axis=1)
    packed = jnp.where(lane < 64, wide, 0.0)
    packed = jnp.where((lane >= 64) & (lane < 80), pltpu.roll(folded(in_full), 64, 1), packed)
    packed = jnp.where((lane >= 80) & (lane < 96), pltpu.roll(folded(out_full), 80, 1), packed)
    inside = (lane >= 96) & (lane < 112)
    packed = jnp.where(inside, pltpu.roll(middle, 96, 1), packed)
    for piece in range(4):
        moved = pltpu.roll(bias_row, 96 - 16 * piece, 1)
        packed = jnp.where(inside & (row == 48 + piece), moved, packed)
    last = lane >= 112
    packed = jnp.where(last & (row == me_s), pltpu.roll(first_part, 112, 1), packed)
    packed = jnp.where(last & (row == me_s + 32), pltpu.roll(first_part, 80, 1), packed)
    pk[...] = (packed * GRAD_SCALE).reshape(NB, 8, 128)

    def send(src, dst, step, to):
        pltpu.make_async_remote_copy(
            src_ref=src,
            dst_ref=dst,
            send_sem=rsend.at[step],
            recv_sem=rrecv.at[step],
            device_id=to,
            device_id_type=MESH,
        ).start()

    near = (me_s // 8) * 2 + lax.rem(me_s, 2)
    far = lax.rem(me_s // 2, 4)

    @pl.loop(1, NB)
    def _(d):
        peer = lax.rem(me_b + d, NB)
        send(pk.at[peer], r_batch.at[me_b], 0, {"batch": peer})

    r_batch[me_b] = pk[me_b]

    batch_wait(2)
    bz[...] = brecv[2].reshape(NB * 32, 128).astype(F32)
    for index in range(SLOTS * K3):
        slot, k = divmod(index, K3)
        value = xs[pl.ds(index, NB, stride=32), :]
        grad = bz[pl.ds(index, NB, stride=32), :]
        left = jnp.concatenate([value, pltpu.roll(value, 64, 1)], axis=0).astype(BF16)
        grads = jnp.concatenate([grad, -sign * pltpu.roll(grad, 64, 1)], axis=0).astype(BF16)
        weights = w_v[slot, k]
        both = dot_nt(grads, jnp.concatenate([weights, weights], axis=0))
        bz[pl.ds(index, NB, stride=32), :] = jnp.where(sign < 0.0, both[:8], both[8:])
        dg_v[slot, k] = dot_tn(left, grads)[:C]
    bsend[3] = bz[...].astype(BF16).reshape(NB, 32, 128)
    batch_start(3)
    dg_copy = pltpu.make_async_copy(dg_v, dg_hbm.at[0], out_sem.at[1])
    dg_copy.start()

    drain(r_batch.at[pl.ds(0, NB - 1)], rrecv.at[0])
    part_near[...] = jnp.sum(r_batch[...], axis=0)

    @pl.loop(1, 8)
    def _(d):
        slot = lax.rem(near + d, 8)
        peer = (slot // 2) * 8 + far * 2 + lax.rem(slot, 2)
        send(part_near, r_near.at[near], 1, {"space": peer})

    r_near[near] = part_near[...]

    batch_wait(3)
    slots_in(3)
    grad_spectrum = []
    for k in range(K3):
        low = fac_v[k * K2 : k * K2 + L2, :] + sm[k * K2 : k * K2 + L2, :]
        grad_spectrum.append(
            jnp.concatenate([low, fac_v[k * K2 + L2 : (k + 1) * K2, :]], axis=0)
        )
    modes_out(grad_spectrum, two_t, 3)
    space_start(3)


    drain(r_near.at[pl.ds(0, 7)], rrecv.at[1])
    part_far[...] = jnp.sum(r_near[...], axis=0)

    @pl.loop(1, 4)
    def _(d):
        slot = lax.rem(far + d, 4)
        peer = (near // 2) * 8 + slot * 2 + lax.rem(near, 2)
        send(part_far, r_far.at[far], 2, {"space": peer})

    r_far[far] = part_far[...]
    drain(r_far.at[pl.ds(0, 3)], rrecv.at[2])
    part_all[...] = jnp.sum(r_far[...], axis=0)

    @pl.loop(1, NB)
    def _(d):
        send(part_all, r_all.at[me_b], 3, {"batch": lax.rem(me_b + d, NB)})

    r_all[me_b] = part_all[...]
    drain(r_all.at[pl.ds(0, NB - 1)], rrecv.at[3])
    red_ref[...] = r_all[...].reshape(C, 128)

    space_wait(3)
    blocks_ref[...] = rbuf[3]
    for phase in range(4):
        drain(sbuf.at[phase, pl.ds(0, NS - 1)], ssend.at[phase])
        drain(bsend.at[phase, pl.ds(0, NB - 1)], bssem.at[phase])
    drain(pk.at[pl.ds(0, NB - 1)], rsend.at[0])
    drain(r_near.at[pl.ds(0, 7)], rsend.at[1])
    drain(r_far.at[pl.ds(0, 3)], rsend.at[2])
    drain(r_all.at[pl.ds(0, NB - 1)], rsend.at[3])
    out_copy.wait()
    dg_copy.wait()
    skip_copy.wait()


def finish_kernel(
    blocks_ref,
    packed_ref,
    one_t_ref,
    three_t_hbm,
    skip_hbm,
    out_in,
    dg_in,
    out_hbm,
    ig_hbm,
    dg_hbm,
    fin_hbm,
    fout_hbm,
    first_hbm,
    second_hbm,
    third_hbm,
    mix_hbm,
    bias_hbm,
    three_t_v,
    out_v,
    dg_v,
    skip_v,
    ig_v,
    left_v,
    zf,
    fin_v,
    fout_v,
    first_v,
    second_v,
    third_v,
    mix_v,
    bias_v,
    sem,
):
    def copy(src, dst, index):
        started = pltpu.make_async_copy(src, dst, sem.at[index])
        started.start()
        return started

    three_copy = copy(three_t_hbm, three_t_v, 2)
    skip_copies = [copy(skip_hbm.at[n], skip_v.at[n], n) for n in range(ROWS)]
    moved_in = [copy(out_in, out_v, 3), copy(dg_in, dg_v, 4)]
    backward_rows(blocks_ref[...], zf, left_v, one_t_ref[...])
    packed = packed_ref[...]
    turned = packed.T
    fin_v[...] = turned[64:80]
    fout_v[...] = turned[80:96]
    second_v[...] = turned[96:112, :K2]
    first_v[0] = turned[112:, :K1]
    first_v[1] = turned[112:, K1:]
    third_v[...] = left_by(packed, 96)[K2 : K2 + K3, :R]
    mix_v[...] = packed[:, :C]
    bias = jnp.zeros((1, 128), F32)
    lane = lanes((1, 128))
    for piece in range(4):
        moved = pltpu.roll(packed[48 + piece : 49 + piece], (32 + 16 * piece) % 128, 1)
        bias = jnp.where((lane >= 16 * piece) & (lane < 16 * (piece + 1)), moved, bias)
    bias_v[...] = bias[:, :C]
    small = (
        (fin_v, fin_hbm),
        (fout_v, fout_hbm),
        (first_v, first_hbm),
        (second_v, second_hbm),
        (third_v, third_hbm),
        (mix_v, mix_hbm),
        (bias_v, bias_hbm),
    )
    waits = [copy(src, dst, 5 + index) for index, (src, dst) in enumerate(small)]
    for arrived in moved_in:
        arrived.wait()
    waits += [copy(out_v, out_hbm, 14), copy(dg_v, dg_hbm, 15)]
    three_copy.wait()
    for n in range(ROWS):
        skip_copies[n].wait()

        def finish(q, field):
            ig_v[n, :, q] = (field + skip_v[n, :, q].astype(F32)).astype(BF16)

        each_pair(n, left_v, three_t_v, finish)
        waits.append(copy(ig_v.at[n], ig_hbm.at[n], 12 + n))
    for started in waits:
        started.wait()


def local(
    inputs,
    cotangent,
    dense_weights,
    owner_table,
    hot_mask,
    skip_weight,
    bias_vector,
    input_factor,
    output_factor,
    first_factor,
    second_factor,
    third_factor,
):
    field = (ROWS, CG, CQ, N1, N3)
    three, three_t, one, one_t, two, two_t, patterns, spread, select = [
        jnp.asarray(table) for table in build_tables()
    ]
    vmem = pl.BlockSpec(memory_space=pltpu.VMEM)
    smem = pl.BlockSpec(memory_space=pltpu.SMEM)
    hbm = pl.BlockSpec(memory_space=pltpu.HBM)
    dense = (SLOTS, K3, C, 2 * C)
    operands = (
        inputs.reshape(field),
        three,
        one,
        hot_mask,
        skip_weight,
        input_factor.T,
        output_factor.T,
        jnp.swapaxes(first_factor, 1, 2),
        second_factor.T,
        third_factor,
        two,
        two_t,
        patterns,
        spread,
        select,
        one_t,
        three_t,
        cotangent.reshape(field),
    )
    blocks = (NS, 32, 128)
    output, skip_part, dense_grad, received, packed = pl.pallas_call(
        kernel,
        out_shape=(
            jax.ShapeDtypeStruct(field, BF16),
            jax.ShapeDtypeStruct(field, BF16),
            jax.ShapeDtypeStruct((1,) + dense, F32),
            jax.ShapeDtypeStruct(blocks, BF16),
            jax.ShapeDtypeStruct((C, 128), F32),
        ),
        in_specs=[smem, smem] + [hbm] * 19,
        out_specs=(hbm, hbm, hbm, vmem, vmem),
        scratch_shapes=[pltpu.VMEM(value.shape, value.dtype) for value in operands]
        + [
            pltpu.VMEM(dense, BF16),
            pltpu.VMEM(field, BF16),
            pltpu.VMEM(field, BF16),
            pltpu.VMEM(dense, F32),
            pltpu.VMEM(field, BF16),
            pltpu.VMEM((C * 16, C * 16), BF16),
            pltpu.VMEM((ROWS, CG * N1, 256), BF16),
            pltpu.VMEM((NS * 32, 128), F32),
            pltpu.VMEM((4,) + blocks, BF16),
            pltpu.VMEM((4,) + blocks, BF16),
            pltpu.VMEM((4, NB, 32, 128), BF16),
            pltpu.VMEM((4, NB, 32, 128), BF16),
            pltpu.VMEM((K3 * K2, 128), F32),
            pltpu.VMEM((K3 * K2, 128), BF16),
            pltpu.VMEM((K3, L2, 128), F32),
            pltpu.VMEM((K3 * K2, 128), F32),
            pltpu.VMEM((K3 * K2, 128), F32),
            pltpu.VMEM((K3 * K2, 128), BF16),
            pltpu.VMEM((K3 * K2, 128), F32),
            pltpu.VMEM((NB * 32, 128), F32),
            pltpu.VMEM((NB * 32, 128), F32),
            pltpu.VMEM((C + 16, C * 16), F32),
            pltpu.VMEM((NB, 8, 128), F32),
            pltpu.VMEM((NB, 8, 128), F32),
            pltpu.VMEM((8, 8, 128), F32),
            pltpu.VMEM((4, 8, 128), F32),
            pltpu.VMEM((NB, 8, 128), F32),
            pltpu.VMEM((8, 128), F32),
            pltpu.VMEM((8, 128), F32),
            pltpu.VMEM((8, 128), F32),
            pltpu.SemaphoreType.DMA((20,)),
            pltpu.SemaphoreType.DMA((3,)),
            pltpu.SemaphoreType.DMA((4,)),
            pltpu.SemaphoreType.DMA((4,)),
            pltpu.SemaphoreType.DMA((4,)),
            pltpu.SemaphoreType.DMA((4,)),
            pltpu.SemaphoreType.DMA((4,)),
            pltpu.SemaphoreType.DMA((4,)),
        ],
        compiler_params=pltpu.CompilerParams(
            collective_id=0, has_side_effects=True, vmem_limit_bytes=64 * 2**20
        ),
    )(owner_table, bias_vector, *operands, dense_weights)
    results = (
        (field, BF16),
        (field, BF16),
        ((1,) + dense, F32),
        ((R, C), F32),
        ((R, C), F32),
        ((2, R, K1), F32),
        ((R, K2), F32),
        ((K3, R), F32),
        ((C, C), F32),
        ((1, C), F32),
    )
    output, input_grad, dense_grad, in_t, out_t, first_t, second_t, third, skip, bias = pl.pallas_call(
        finish_kernel,
        out_shape=tuple(jax.ShapeDtypeStruct(*result) for result in results),
        in_specs=[vmem, vmem, vmem] + [hbm] * 4,
        out_specs=(hbm,) * len(results),
        scratch_shapes=[
            pltpu.VMEM(three_t.shape, BF16),
            pltpu.VMEM(field, BF16),
            pltpu.VMEM((1,) + dense, F32),
            pltpu.VMEM(field, BF16),
            pltpu.VMEM(field, BF16),
            pltpu.VMEM((ROWS, CG * N1, 256), BF16),
            pltpu.VMEM((NS * 32, 128), F32),
        ]
        + [pltpu.VMEM(*result) for result in results[3:]]
        + [pltpu.SemaphoreType.DMA((16,))],
        compiler_params=pltpu.CompilerParams(vmem_limit_bytes=64 * 2**20),
    )(received, packed, one_t, three_t, skip_part, output, dense_grad)
    return (
        output.reshape(inputs.shape),
        input_grad.reshape(inputs.shape),
        dense_grad,
        in_t.T,
        out_t.T,
        jnp.swapaxes(first_t, 1, 2),
        second_t.T,
        third,
        skip,
        bias.reshape(C),
    )


def solution(mesh):
    field = P("batch", "space", None, None, None)
    dense = P("space", "batch", None, None, None)
    whole = P()
    return jax.shard_map(
        local,
        mesh=mesh,
        in_specs=(field, field, dense, whole, P("space", None, None)) + (whole,) * 7,
        out_specs=(field, field, dense) + (whole,) * 7,
        check_vma=False,
    )
```

```python
import math

import jax
import jax.numpy as jnp
import ml_dtypes
import numpy as np
from jax import lax
from jax.experimental import pallas as pl
from jax.experimental.pallas import tpu as pltpu
from jax.sharding import PartitionSpec as P

MESH = pl.DeviceIdType.MESH
F32 = jnp.float32
BF16 = jnp.bfloat16
HIGH = lax.Precision.HIGHEST

C = 64
N1 = 64
N2 = 64
N3 = 128
K1 = 32
K2 = 32
K3 = 16
L2 = 16
R = 16
SAMPLES = 8
NS = 32
NB = 8
ROWS = N2 // NS
CG = 8
CQ = 8
SLOTS = L2 // NB
HALF = NS * 16
GRAD_SCALE = float(SAMPLES * N1 * N2 * N3) ** (-0.5)


def rounded(values):
    return np.asarray(values, np.float32).astype(ml_dtypes.bfloat16)


def twiddles(frequency, length):
    index = np.mod(frequency[:, None] * np.arange(length)[None, :], length)
    radians = index.astype(np.float32) * np.float32(2.0 * math.pi / length)
    return np.cos(radians), np.sin(radians)


def retained(amount):
    position = np.arange(amount)
    return np.where(position % 2 == 0, position // 2, -((position + 1) // 2))


def build_tables():
    factor = float(N1 * N2 * N3 * K1 * K2 * K3) ** (-0.25)
    cos1, sin1 = twiddles(retained(K1), N1)
    t0 = np.float32(factor) * cos1
    t1 = np.float32(-factor) * sin1
    one = np.block([[t0, -t1], [t1, t0]])
    cos2, sin2 = twiddles(retained(K2), N2)
    two = np.zeros((2, K2, N2, 2), np.float32)
    two[0, :, :, 0] = cos2
    two[0, :, :, 1] = sin2
    two[1, :, :, 0] = -sin2
    two[1, :, :, 1] = cos2
    two = two.reshape(2, K2, NS, ROWS, 2).transpose(0, 1, 3, 2, 4).reshape(2 * K2, 2 * N2)
    cos3, sin3 = twiddles(np.arange(K3), N3)
    three = np.zeros((CQ, N3, 2, K3, CQ), np.float32)
    for q in range(CQ):
        three[q, :, 0, :, q] = cos3.T
        three[q, :, 1, :, q] = -sin3.T
    three = three.reshape(CQ * N3, 2 * K3 * CQ)
    eye = np.eye(R, dtype=np.float32)

    def tiled(signs):
        return np.concatenate([sign * eye for sign in signs] + [np.zeros((R, 64), np.float32)], axis=1)

    patterns = np.concatenate(
        [
            tiled((1, 0, 0, 1)),
            tiled((1, 0, 1, 0)),
            tiled((0, 1, -1, 0)),
            tiled((0, 1, 0, 1)),
            tiled((1, 0, 0, -1)),
            tiled((0, 1, 1, 0)),
        ],
        axis=1,
    )
    spread = np.stack([tiled((1, 1, 1, 1)), tiled((1, 1, 0, 0)), tiled((0, 0, 1, 1))])
    select = np.zeros((K3, K3, 128), np.float32)
    for k in range(K3):
        select[k, k] = 1.0
    return (
        rounded(three),
        rounded(three.T),
        rounded(one),
        rounded(one.T),
        rounded(two),
        rounded(two.T),
        rounded(patterns),
        spread.astype(np.float32),
        rounded(select.reshape(K3, K3 * 128)),
    )


def dot(a, b, precision=None):
    return jnp.dot(a, b, preferred_element_type=F32, precision=precision)


def dot_nt(a, b, precision=None):
    return lax.dot_general(
        a, b, (((1,), (1,)), ((), ())), preferred_element_type=F32, precision=precision
    )


def dot_tn(a, b):
    return lax.dot_general(a, b, (((0,), (0,)), ((), ())), preferred_element_type=F32)


def lanes(shape):
    return lax.broadcasted_iota(jnp.int32, shape, len(shape) - 1)


def rows(shape):
    return lax.broadcasted_iota(jnp.int32, shape, 0)


def swap_groups(parts):
    parts = list(parts)
    group = lanes(parts[0].shape) // CQ
    for bit in (1, 2, 4, 8):
        low = (group & bit) == 0
        for a in range(16):
            if a & bit:
                continue
            first, second = parts[a], parts[a + bit]
            parts[a] = jnp.where(low, first, pltpu.roll(second, 8 * bit, 1))
            parts[a + bit] = jnp.where(low, pltpu.roll(first, 128 - 8 * bit, 1), second)
    return parts


def left_by(value, amount):
    return pltpu.roll(value, 128 - amount, 1)


def drain(block, sem):
    pltpu.make_async_copy(block, block, sem).wait()


def backward_row(blocks, zf, left_v, one_t):
    zf[...] = blocks.reshape(HALF, 128).astype(F32)
    block = jnp.concatenate(
        [
            jnp.concatenate(
                [zf[pl.ds(part * 8 + g, K1, stride=16), :].astype(BF16) for part in range(2)],
                axis=0,
            )
            for g in range(CG)
        ],
        axis=1,
    )
    field = dot(one_t, block).astype(BF16)
    for g in range(CG):
        left_v[g * N1 : (g + 1) * N1, :128] = field[:N1, g * 128 : (g + 1) * 128]
        left_v[g * N1 : (g + 1) * N1, 128:] = field[N1:, g * 128 : (g + 1) * 128]


def each_pair(left_v, three_t, body, after=None):
    @pl.loop(0, CQ // 2, unroll=4)
    def _(pair):
        column = pl.multiple_of(pair * 256, 256)
        field = dot(left_v[...], three_t[:, pl.ds(column, 256)])
        made = [
            body(pair * 2 + half, field[:, half * 128 : (half + 1) * 128].reshape(CG, N1, N3))
            for half in range(2)
        ]
        if after is not None:
            after(column, jnp.concatenate([v.reshape(CG * N1, N3) for v in made], axis=1))


def kernel(
    owner_ref,
    bias_ref,
    x_hbm,
    three_hbm,
    one_hbm,
    hot_hbm,
    skip_hbm,
    fin_hbm,
    fout_hbm,
    first_hbm,
    second_hbm,
    third_hbm,
    two_hbm,
    two_t_hbm,
    pat_hbm,
    spread_hbm,
    select_hbm,
    one_t_hbm,
    three_t_hbm,
    cot_hbm,
    w_hbm,
    out_hbm,
    skip_out_hbm,
    ig_hbm,
    dg_hbm,
    blocks_hbm,
    red_hbm,
    x_ref,
    three_ref,
    one_ref,
    hot_ref,
    skip_ref,
    fin_ref,
    fout_ref,
    first_ref,
    second_ref,
    third_ref,
    two_ref,
    two_t_ref,
    pat_ref,
    spread_ref,
    select_ref,
    one_t_ref,
    three_t_ref,
    cot_v,
    w_v,
    out_v,
    gp_v,
    dg_v,
    skip_v,
    ig_v,
    kron_v,
    kron_back_v,
    left_v,
    total_v,
    zf,
    sbuf,
    rbuf,
    bsend,
    brecv,
    sm,
    s16,
    maskf,
    ph,
    coef_b,
    prod_v,
    fac_v,
    xs,
    bz,
    lefts_v,
    grads_v,
    sgs,
    pk,
    r_batch,
    r_near,
    r_far,
    r_all,
    part_near,
    part_far,
    part_all,
    in_sem,
    out_sem,
    ssend,
    srecv,
    bssem,
    brsem,
    rsend,
    rrecv,
):
    me_s = lax.axis_index("space")
    me_b = lax.axis_index("batch")
    def fetch(src, dst, index):
        copy = pltpu.make_async_copy(src, dst, in_sem.at[index])
        copy.start()
        return copy

    x_copies = [fetch(x_hbm.at[0], x_ref.at[0], 0)]
    three_copy = fetch(three_hbm, three_ref, 2)
    one_copy = fetch(one_hbm, one_ref, 3)
    x_copies.append(fetch(x_hbm.at[1], x_ref.at[1], 1))
    barrier = pltpu.get_barrier_semaphore()

    def each_space_peer(body):
        for step in (2, 1, 3, 0):

            @pl.loop(0 if step else 1, 8)
            def _(d):
                body(
                    lax.rem(me_s // 8 + d // 2, 4) * 8
                    + lax.rem(me_s // 2 + step, 4) * 2
                    + lax.rem(me_s + d, 2)
                )

    def greet(peer):
        pl.semaphore_signal(barrier, inc=1, device_id={"space": peer}, device_id_type=MESH)

    each_space_peer(greet)

    @pl.loop(1, NB)
    def _(d):
        pl.semaphore_signal(
            barrier, inc=1, device_id={"batch": lax.rem(me_b + d, NB)}, device_id_type=MESH
        )

    small_copies = [
        fetch(src, dst, 4 + index)
        for index, (src, dst) in enumerate(
            (
                (hot_hbm, hot_ref),
                (skip_hbm, skip_ref),
                (fin_hbm, fin_ref),
                (fout_hbm, fout_ref),
                (first_hbm, first_ref),
                (second_hbm, second_ref),
                (third_hbm, third_ref),
                (two_hbm, two_ref),
                (two_t_hbm, two_t_ref),
                (pat_hbm, pat_ref),
                (spread_hbm, spread_ref),
                (select_hbm, select_ref),
                (one_t_hbm, one_t_ref),
                (three_t_hbm, three_t_ref),
            )
        )
    ]
    cot_copy = fetch(cot_hbm, cot_v, 18)
    w_copy = fetch(w_hbm.at[0], w_v, 19)

    def space_start(index):
        def send_block(peer):
            pltpu.make_async_remote_copy(
                src_ref=sbuf.at[index, peer],
                dst_ref=rbuf.at[index, me_s],
                send_sem=ssend.at[index],
                recv_sem=srecv.at[index],
                device_id={"space": peer},
                device_id_type=MESH,
            ).start()

        each_space_peer(send_block)
        rbuf[index, me_s] = sbuf[index, me_s]

    def space_wait(index):
        drain(rbuf.at[index, pl.ds(0, NS - 1)], srecv.at[index])

    def batch_start(phase):
        @pl.loop(1, NB)
        def _(d):
            peer = lax.rem(me_b + d, NB)
            pltpu.make_async_remote_copy(
                src_ref=bsend.at[phase, peer],
                dst_ref=brecv.at[phase, me_b],
                send_sem=bssem.at[phase],
                recv_sem=brsem.at[phase],
                device_id={"batch": peer},
                device_id_type=MESH,
            ).start()

        brecv[phase, me_b] = bsend[phase, me_b]

    def batch_wait(phase):
        drain(brecv.at[phase, pl.ds(0, NB - 1)], brsem.at[phase])

    def forward_row(src, n, index):
        total = None
        for q in range(0, CQ, 2):
            pair = jnp.concatenate(
                [src[n, :, q].reshape(CG * N1, N3), src[n, :, q + 1].reshape(CG * N1, N3)], axis=1
            )
            term = dot(pair, three_ref[q * N3 : (q + 2) * N3, :])
            total = term if total is None else total + term
        send_row(total, n, index)

    def send_row(total, n, index):
        total = total.astype(BF16)
        right = jnp.concatenate(
            [
                jnp.concatenate(
                    [total[g * N1 : (g + 1) * N1, :128], total[g * N1 : (g + 1) * N1, 128:]], axis=0
                )
                for g in range(CG)
            ],
            axis=1,
        )
        modes = dot(one_ref[...], right)
        for g in range(CG):
            for part in range(2):
                zf[pl.ds(n * HALF + part * 8 + g, K1, stride=16), :] = modes[
                    part * K1 : (part + 1) * K1, g * 128 : (g + 1) * 128
                ]
        sbuf[index] = zf[n * HALF : (n + 1) * HALF, :].astype(BF16).reshape(NS, 16, 128)
        space_start(index)

    def modes_in(phase, table):
        for n in range(ROWS):
            space_wait(2 * phase + n)
            zf[n * HALF : (n + 1) * HALF, :] = rbuf[2 * phase + n].reshape(HALF, 128).astype(F32)
        cells = jnp.concatenate(
            [zf[pl.ds(g, 2 * N2, stride=8), :].astype(BF16) for g in range(CG)], axis=1
        )
        modes = dot(table, cells)
        parts = [
            modes[part * K2 : (part + 1) * K2, g * 128 : (g + 1) * 128]
            for part in range(2)
            for g in range(CG)
        ]
        return swap_groups(parts)

    def modes_out(by_frequency, table, phase):
        parts = swap_groups(by_frequency)
        spectrum = jnp.concatenate(
            [
                jnp.concatenate([parts[part * CG + g] for g in range(CG)], axis=1).astype(BF16)
                for part in range(2)
            ],
            axis=0,
        )
        for n in range(ROWS):
            cells = dot(table[n * N2 : (n + 1) * N2], spectrum)
            for g in range(CG):
                zf[pl.ds(n * HALF + g, N2, stride=8), :] = cells[:, g * 128 : (g + 1) * 128]
            sbuf[2 * phase + n] = (
                zf[n * HALF : (n + 1) * HALF, :].astype(BF16).reshape(NS, 16, 128)
            )
            space_start(2 * phase + n)

    def mix_channels(src, kron, with_bias):
        @pl.loop(0, N1 // 16)
        def _(step):
            cut = pl.ds(pl.multiple_of(step * 16, 16), 16)
            right = jnp.concatenate(
                [src[n, :, :, cut, :].reshape(C * 16, N3) for n in range(ROWS)], axis=1
            )
            mixed = dot(kron[...], right)
            for n in range(ROWS):
                value = mixed[:, n * N3 : (n + 1) * N3].reshape(C, 16, N3)
                if with_bias:
                    value = jnp.concatenate([value[c : c + 1] + bias_ref[c] for c in range(C)], axis=0)
                skip_v[n, :, :, cut, :] = value.astype(BF16).reshape(CG, CQ, 16, N3)

    spread_rows = (rows((C * 16, C)) // 16 == lanes((C * 16, C))).astype(F32)
    spread_half = spread_rows.astype(BF16)

    def build_kron(base, kron):
        expanded = dot(spread_half, base).astype(BF16)
        for block in range(4):
            cut = slice(block * 256, (block + 1) * 256)
            full = dot_nt(expanded[cut], spread_half)
            same = (rows((256, 1024)) & 15) == (lanes((256, 1024)) & 15)
            kron[cut, :] = jnp.where(same, full, 0.0).astype(BF16)

    three_copy.wait()
    one_copy.wait()
    for n in range(ROWS):
        x_copies[n].wait()
        if n == 0:
            pl.semaphore_wait(barrier, NS - 1 + NB - 1)
        forward_row(x_ref, n, n)

    for copy in small_copies:
        copy.wait()
    side = (2 * K2, 2 * K2)

    def permutation(index, other):
        position = index & (K2 - 1)
        target = index
        for slot in range(L2):
            target = jnp.where(position == slot, index - position + owner_ref[slot], target)
        return (target == other).astype(F32)

    perm = permutation(rows(side), lanes(side))
    perm_t = permutation(lanes(side), rows(side))
    perm_half = perm.astype(BF16)
    two = dot(perm_half, two_ref[...]).astype(BF16)
    two_t = dot_nt(two_t_ref[...], perm_half).astype(BF16)
    second = dot_nt(perm[:K2, :K2], second_ref[...], HIGH)
    second_l = dot(second, spread_ref[0], HIGH)
    third_l = dot(third_ref[...], spread_ref[0], HIGH)
    own = (lanes((8, K1)) == me_s).astype(F32)
    first_l = (
        dot(dot_nt(own, first_ref[0], HIGH), spread_ref[1], HIGH)
        + dot(dot_nt(own, first_ref[1], HIGH), spread_ref[2], HIGH)
    )[0:1]
    for k in range(K3):
        ph[k * K2 : (k + 1) * K2, :] = first_l * (second_l * third_l[k : k + 1])
    hot = dot(perm_half[:L2, :L2], hot_ref[0].astype(F32).astype(BF16)).astype(BF16)
    spread_hot = dot(hot, select_ref[...])
    for k in range(K3):
        maskf[k] = spread_hot[:, k * 128 : (k + 1) * 128]

    def expand(factor, top, bottom, width):
        pieces = [
            dot_tn(factor, pat_ref[:, start * 128 : start * 128 + width]) for start in (top, bottom)
        ]
        return jnp.concatenate(pieces, axis=0).astype(BF16)

    fin_all = expand(fin_ref[...], 0, 2, 256)
    fin_b = fin_all[:, 128:]
    fout_b = expand(fout_ref[...], 1, 3, 128)
    fout_c = expand(fout_ref[...], 4, 5, 128)

    build_kron(skip_ref[...].astype(F32).T.astype(BF16), kron_v)
    mix_channels(x_ref, kron_v, True)
    build_kron(skip_ref[...], kron_back_v)

    spectrum = modes_in(0, two)
    for k in range(K3):
        sm[k * K2 : (k + 1) * K2, :] = spectrum[k]

    def slots_out(phase):
        for owner in range(NB):
            for slot in range(SLOTS):
                bsend[phase, owner, slot * K3 : (slot + 1) * K3, :] = sm[
                    pl.ds(owner * SLOTS + slot, K3, stride=K2), :
                ].astype(BF16)

    def slots_in(phase):
        bz[...] = brecv[phase].reshape(NB * 32, 128).astype(F32)
        for slot in range(L2):
            sm[pl.ds(slot, K3, stride=K2), :] = bz[slot * K3 : (slot + 1) * K3, :]

    slots_out(0)
    batch_start(0)
    s16[...] = sm[...].astype(BF16)
    coef = dot(s16[...], fin_all)
    coef_b[...] = coef[:, 128:]
    prod_v[...] = (coef[:, :128] * ph[...]).astype(BF16)
    fac_v[...] = dot_nt(prod_v[...], fout_b)
    w_copy.wait()
    batch_wait(0)
    xs[...] = brecv[0].reshape(NB * 32, 128).astype(F32)
    sign = jnp.where(lanes((8, 128)) < 64, -1.0, 1.0)
    for index in range(SLOTS * K3):
        slot, k = divmod(index, K3)
        value = xs[pl.ds(index, NB, stride=32), :]
        left = jnp.concatenate([value, pltpu.roll(value, 64, 1)], axis=0).astype(BF16)
        lefts_v[index] = left
        both = dot(left[:, :C], w_v[slot, k])
        bz[pl.ds(index, NB, stride=32), :] = both[:8] + sign * pltpu.roll(both[8:], 64, 1)
    bsend[1] = bz[...].astype(BF16).reshape(NB, 32, 128)
    batch_start(1)
    batch_wait(1)
    slots_in(1)
    out_spec = []
    for k in range(K3):
        low = jnp.where(
            maskf[k] > 0.0, sm[k * K2 : k * K2 + L2, :], fac_v[k * K2 : k * K2 + L2, :]
        )
        out_spec.append(jnp.concatenate([low, fac_v[k * K2 + L2 : (k + 1) * K2, :]], axis=0))
    modes_out(out_spec, two_t, 1)
    cot_copy.wait()

    for n in range(ROWS):
        space_wait(2 + n)
        backward_row(rbuf[2 + n], zf.at[pl.ds(n * HALF, HALF)], left_v, one_t_ref[...])

        def activate(q, field):
            v = field + skip_v[n, :, q].astype(F32)
            square = v * v
            k0 = math.sqrt(2.0 / math.pi)
            gate = 0.5 * jnp.tanh(v * (k0 + (k0 * 0.044715) * square)) + 0.5
            active = v * gate
            out_v[n, :, q] = active.astype(BF16)
            slope = gate + active * (1.0 - gate) * (2.0 * k0 + (6.0 * k0 * 0.044715) * square)
            made = (cot_v[n, :, q].astype(F32) * slope).astype(BF16)
            gp_v[n, :, q] = made
            return made

        def gather(column, pair):
            total_v[...] += dot(pair, three_ref[pl.ds(column, 256), :])

        total_v[...] = jnp.zeros_like(total_v)
        each_pair(left_v, three_t_ref, activate, gather)
        send_row(total_v[...], n, 4 + n)
    out_copy = pltpu.make_async_copy(out_v, out_hbm, out_sem.at[0])
    out_copy.start()

    same = ((rows((16, 256)) & 15) == (lanes((16, 256)) & 15)).astype(F32)
    ones = jnp.ones((16, ROWS * 4 * N3), BF16)

    def cut_channels(src, start):
        return jnp.concatenate(
            [
                src[n, pl.ds(start * 2, 2), :, b * 16 : (b + 1) * 16, :].reshape(256, N3)
                for n in range(ROWS)
                for b in range(N1 // 16)
            ],
            axis=1,
        )

    for column in range(4):
        grads = cut_channels(gp_v, column)
        here = slice(column * 256, (column + 1) * 256)
        sgs[C : C + 16, here] = dot_nt(ones, grads)

        @pl.loop(0, 4)
        def _(block):
            full = dot_nt(cut_channels(x_ref, block), grads).reshape(16, 16, 256)
            sgs[pl.ds(pl.multiple_of(block * 16, 16), 16), here] = jnp.sum(full * same[None], axis=1)

    skip_grad = dot(sgs[...], spread_rows, HIGH)

    grad_spec = modes_in(2, two)
    cold = []
    for k in range(K3):
        low = grad_spec[k][:L2]
        sm[k * K2 : k * K2 + L2, :] = low * maskf[k]
        cold.append(
            jnp.concatenate([low * (1.0 - maskf[k]), grad_spec[k][L2:]], axis=0).astype(BF16)
        )
    slots_out(2)
    batch_start(2)
    cold = jnp.concatenate(cold, axis=0)
    back = dot(cold, fout_c)
    prod_back = (back * ph[...]).astype(BF16)
    fac_v[...] = dot_nt(prod_back, fin_b)
    in_full = dot_tn(s16[...], prod_back)
    out_full = dot_tn(cold, prod_v[...])
    back = back * coef_b[...]
    first_sum = jnp.zeros((K2, 128), F32)
    second_sum = jnp.zeros((K2, 128), F32)
    third_rows = []
    for k in range(K3):
        term = back[k * K2 : (k + 1) * K2]
        by_third = term * third_l[k : k + 1]
        first_sum = first_sum + by_third * second_l
        second_sum = second_sum + by_third * first_l
        third_rows.append(jnp.sum(term * first_l * second_l, axis=0, keepdims=True))
    first_row = jnp.sum(first_sum, axis=0, keepdims=True)
    third_sum = jnp.concatenate(third_rows, axis=0)

    def folded(full):
        pairs = full + left_by(full, 32)
        return pairs[:C] + left_by(pairs[C:], 16)

    shape = (C, 128)
    lane, row = lanes(shape), rows(shape)

    def below(value):
        return jnp.concatenate([value, jnp.zeros((C - value.shape[0], 128), F32)], axis=0)

    def fold_all(value):
        pairs = value + left_by(value, 16)
        return pairs + left_by(pairs, 32)

    second_part = dot(perm_t[:K2, :K2], fold_all(second_sum), HIGH)
    third_part = fold_all(third_sum)
    first_part = first_row + left_by(first_row, 16)
    middle = jnp.concatenate([second_part, third_part, jnp.zeros((16, 128), F32)], axis=0)
    zero64 = jnp.zeros((C, 64), F32)
    wide = jnp.concatenate([skip_grad[:C], zero64], axis=1)
    bias_row = jnp.concatenate([skip_grad[C : C + 1], zero64[:1]], axis=1)
    packed = jnp.where(lane < 64, wide, 0.0)
    packed = jnp.where((lane >= 64) & (lane < 80), pltpu.roll(folded(in_full), 64, 1), packed)
    packed = jnp.where((lane >= 80) & (lane < 96), pltpu.roll(folded(out_full), 80, 1), packed)
    inside = (lane >= 96) & (lane < 112)
    packed = jnp.where(inside, pltpu.roll(middle, 96, 1), packed)
    for piece in range(4):
        moved = pltpu.roll(bias_row, 96 - 16 * piece, 1)
        packed = jnp.where(inside & (row == 48 + piece), moved, packed)
    last = lane >= 112
    packed = jnp.where(last & (row == me_s), pltpu.roll(first_part, 112, 1), packed)
    packed = jnp.where(last & (row == me_s + 32), pltpu.roll(first_part, 80, 1), packed)
    pk[...] = (packed * GRAD_SCALE).reshape(NB, 8, 128)

    def send(src, dst, step, to):
        pltpu.make_async_remote_copy(
            src_ref=src,
            dst_ref=dst,
            send_sem=rsend.at[step],
            recv_sem=rrecv.at[step],
            device_id=to,
            device_id_type=MESH,
        ).start()

    near = (me_s // 8) * 2 + lax.rem(me_s, 2)
    far = lax.rem(me_s // 2, 4)

    @pl.loop(1, NB)
    def _(d):
        peer = lax.rem(me_b + d, NB)
        send(pk.at[peer], r_batch.at[me_b], 0, {"batch": peer})

    r_batch[me_b] = pk[me_b]

    batch_wait(2)
    bz[...] = brecv[2].reshape(NB * 32, 128).astype(F32)
    for index in range(SLOTS * K3):
        slot, k = divmod(index, K3)
        grad = bz[pl.ds(index, NB, stride=32), :]
        grads = jnp.concatenate([grad, -sign * pltpu.roll(grad, 64, 1)], axis=0).astype(BF16)
        grads_v[index] = grads
        weights = w_v[slot, k]
        both = dot_nt(grads, jnp.concatenate([weights, weights], axis=0))
        bz[pl.ds(index, NB, stride=32), :] = jnp.where(sign < 0.0, both[:8], both[8:])
    bsend[3] = bz[...].astype(BF16).reshape(NB, 32, 128)
    batch_start(3)
    for index in range(SLOTS * K3):
        slot, k = divmod(index, K3)
        dg_v[slot, k] = dot_tn(lefts_v[index], grads_v[index])[:C]
    dg_copy = pltpu.make_async_copy(dg_v, dg_hbm.at[0], out_sem.at[1])
    dg_copy.start()

    drain(r_batch.at[pl.ds(0, NB - 1)], rrecv.at[0])
    part_near[...] = jnp.sum(r_batch[...], axis=0)

    @pl.loop(1, 8)
    def _(d):
        slot = lax.rem(near + d, 8)
        peer = (slot // 2) * 8 + far * 2 + lax.rem(slot, 2)
        send(part_near, r_near.at[near], 1, {"space": peer})

    r_near[near] = part_near[...]

    mix_channels(gp_v, kron_back_v, False)
    skip_copy = pltpu.make_async_copy(skip_v, skip_out_hbm, out_sem.at[2])
    skip_copy.start()

    batch_wait(3)
    slots_in(3)
    grad_spectrum = []
    for k in range(K3):
        low = fac_v[k * K2 : k * K2 + L2, :] + sm[k * K2 : k * K2 + L2, :]
        grad_spectrum.append(
            jnp.concatenate([low, fac_v[k * K2 + L2 : (k + 1) * K2, :]], axis=0)
        )
    modes_out(grad_spectrum, two_t, 3)


    drain(r_near.at[pl.ds(0, 7)], rrecv.at[1])
    part_far[...] = jnp.sum(r_near[...], axis=0)

    @pl.loop(1, 4)
    def _(d):
        slot = lax.rem(far + d, 4)
        peer = (near // 2) * 8 + slot * 2 + lax.rem(near, 2)
        send(part_far, r_far.at[far], 2, {"space": peer})

    r_far[far] = part_far[...]

    space_wait(6)
    backward_row(rbuf[6], zf.at[pl.ds(0, HALF)], left_v, one_t_ref[...])

    def finish(q, field):
        ig_v[:, q] = (field + skip_v[0, :, q].astype(F32)).astype(BF16)

    each_pair(left_v, three_t_ref, finish)
    ig_copy = pltpu.make_async_copy(ig_v, ig_hbm, out_sem.at[3])
    ig_copy.start()

    drain(r_far.at[pl.ds(0, 3)], rrecv.at[2])
    part_all[...] = jnp.sum(r_far[...], axis=0)

    @pl.loop(1, NB)
    def _(d):
        send(part_all, r_all.at[me_b], 3, {"batch": lax.rem(me_b + d, NB)})

    r_all[me_b] = part_all[...]
    space_wait(7)
    blocks_copy = pltpu.make_async_copy(rbuf.at[7], blocks_hbm, out_sem.at[4])
    blocks_copy.start()
    drain(r_all.at[pl.ds(0, NB - 1)], rrecv.at[3])
    red_copy = pltpu.make_async_copy(r_all, red_hbm, out_sem.at[5])
    red_copy.start()
    for index in range(8):
        drain(sbuf.at[index, pl.ds(0, NS - 1)], ssend.at[index])
    for phase in range(4):
        drain(bsend.at[phase, pl.ds(0, NB - 1)], bssem.at[phase])
    drain(pk.at[pl.ds(0, NB - 1)], rsend.at[0])
    drain(r_near.at[pl.ds(0, 7)], rsend.at[1])
    drain(r_far.at[pl.ds(0, 3)], rsend.at[2])
    drain(r_all.at[pl.ds(0, NB - 1)], rsend.at[3])
    for started in (out_copy, dg_copy, skip_copy, ig_copy, blocks_copy, red_copy):
        started.wait()


def finish_kernel(
    blocks_hbm,
    packed_hbm,
    one_t_hbm,
    three_t_hbm,
    skip_hbm,
    out_in,
    dg_in,
    ig_in,
    out_hbm,
    ig_hbm,
    dg_hbm,
    fin_hbm,
    fout_hbm,
    first_hbm,
    second_hbm,
    third_hbm,
    mix_hbm,
    bias_hbm,
    blocks_v,
    packed_v,
    one_t_v,
    three_t_v,
    skip_v,
    out_v,
    dg_v,
    ig_v,
    left_v,
    zf,
    fin_v,
    fout_v,
    first_v,
    second_v,
    third_v,
    mix_v,
    bias_v,
    sem,
):
    def copy(src, dst, index):
        started = pltpu.make_async_copy(src, dst, sem.at[index])
        started.start()
        return started

    arriving = [
        copy(src, dst, index)
        for index, (src, dst) in enumerate(
            (
                (blocks_hbm, blocks_v),
                (one_t_hbm, one_t_v),
                (three_t_hbm, three_t_v),
                (skip_hbm.at[1], skip_v),
                (packed_hbm, packed_v),
                (out_in, out_v),
                (ig_in, ig_v.at[0]),
                (dg_in, dg_v),
            )
        )
    ]
    waits = []

    def pass_on(index, src, dst):
        arriving[index].wait()
        waits.append(copy(src, dst, 8 + index))

    for index in range(4):
        arriving[index].wait()
    backward_row(blocks_v[...], zf, left_v, one_t_v[...])
    arriving[4].wait()
    packed = packed_v[...].reshape(C, 128)
    turned = packed.T
    fin_v[...] = turned[64:80]
    fout_v[...] = turned[80:96]
    second_v[...] = turned[96:112, :K2]
    first_v[0] = turned[112:, :K1]
    first_v[1] = turned[112:, K1:]
    third_v[...] = left_by(packed, 96)[K2 : K2 + K3, :R]
    mix_v[...] = packed[:, :C]
    bias = jnp.zeros((1, 128), F32)
    lane = lanes((1, 128))
    for piece in range(4):
        moved = pltpu.roll(packed[48 + piece : 49 + piece], (32 + 16 * piece) % 128, 1)
        bias = jnp.where((lane >= 16 * piece) & (lane < 16 * (piece + 1)), moved, bias)
    bias_v[...] = bias[:, :C]
    small = (
        (fin_v, fin_hbm),
        (fout_v, fout_hbm),
        (first_v, first_hbm),
        (second_v, second_hbm),
        (third_v, third_hbm),
        (mix_v, mix_hbm),
        (bias_v, bias_hbm),
    )
    waits += [copy(src, dst, 17 + index) for index, (src, dst) in enumerate(small)]
    for pair in range(CQ // 2):
        field = dot(left_v[...], three_t_v[:, pair * 256 : (pair + 1) * 256])
        for half in range(2):
            q = pair * 2 + half
            value = field[:, half * 128 : (half + 1) * 128].reshape(CG, N1, N3)
            ig_v[1, :, q] = (value + skip_v[:, q].astype(F32)).astype(BF16)
        cut = (1, slice(None), pl.ds(pair * 2, 2))
        waits.append(copy(ig_v.at[cut], ig_hbm.at[cut], 24 + pair))
        if pair == 0:
            pass_on(5, out_v, out_hbm)
        if pair == 1:
            pass_on(6, ig_v.at[0], ig_hbm.at[0])
        if pair == 2:
            pass_on(7, dg_v, dg_hbm)
    for started in waits:
        started.wait()


def local(
    inputs,
    cotangent,
    dense_weights,
    owner_table,
    hot_mask,
    skip_weight,
    bias_vector,
    input_factor,
    output_factor,
    first_factor,
    second_factor,
    third_factor,
):
    field = (ROWS, CG, CQ, N1, N3)
    three, three_t, one, one_t, two, two_t, patterns, spread, select = [
        jnp.asarray(table) for table in build_tables()
    ]
    smem = pl.BlockSpec(memory_space=pltpu.SMEM)
    hbm = pl.BlockSpec(memory_space=pltpu.HBM)
    dense = (SLOTS, K3, C, 2 * C)
    operands = (
        inputs.reshape(field),
        three,
        one,
        hot_mask,
        skip_weight,
        input_factor.T,
        output_factor.T,
        jnp.swapaxes(first_factor, 1, 2),
        second_factor.T,
        third_factor,
        two,
        two_t,
        patterns,
        spread,
        select,
        one_t,
        three_t,
        cotangent.reshape(field),
    )
    blocks = (NS, 16, 128)
    row = field[1:]
    output, skip_part, grad_row, dense_grad, received, packed = pl.pallas_call(
        kernel,
        out_shape=(
            jax.ShapeDtypeStruct(field, BF16),
            jax.ShapeDtypeStruct(field, BF16),
            jax.ShapeDtypeStruct(row, BF16),
            jax.ShapeDtypeStruct((1,) + dense, F32),
            jax.ShapeDtypeStruct(blocks, BF16),
            jax.ShapeDtypeStruct((NB, 8, 128), F32),
        ),
        in_specs=[smem, smem] + [hbm] * 19,
        out_specs=(hbm,) * 6,
        scratch_shapes=[pltpu.VMEM(value.shape, value.dtype) for value in operands]
        + [
            pltpu.VMEM(dense, BF16),
            pltpu.VMEM(field, BF16),
            pltpu.VMEM(field, BF16),
            pltpu.VMEM(dense, F32),
            pltpu.VMEM(field, BF16),
            pltpu.VMEM(row, BF16),
            pltpu.VMEM((C * 16, C * 16), BF16),
            pltpu.VMEM((C * 16, C * 16), BF16),
            pltpu.VMEM((CG * N1, 256), BF16),
            pltpu.VMEM((CG * N1, 256), F32),
            pltpu.VMEM((ROWS * HALF, 128), F32),
            pltpu.VMEM((8,) + blocks, BF16),
            pltpu.VMEM((8,) + blocks, BF16),
            pltpu.VMEM((4, NB, 32, 128), BF16),
            pltpu.VMEM((4, NB, 32, 128), BF16),
            pltpu.VMEM((K3 * K2, 128), F32),
            pltpu.VMEM((K3 * K2, 128), BF16),
            pltpu.VMEM((K3, L2, 128), F32),
            pltpu.VMEM((K3 * K2, 128), F32),
            pltpu.VMEM((K3 * K2, 128), F32),
            pltpu.VMEM((K3 * K2, 128), BF16),
            pltpu.VMEM((K3 * K2, 128), F32),
            pltpu.VMEM((NB * 32, 128), F32),
            pltpu.VMEM((NB * 32, 128), F32),
            pltpu.VMEM((SLOTS * K3, 16, 128), BF16),
            pltpu.VMEM((SLOTS * K3, 16, 128), BF16),
            pltpu.VMEM((C + 16, C * 16), F32),
            pltpu.VMEM((NB, 8, 128), F32),
            pltpu.VMEM((NB, 8, 128), F32),
            pltpu.VMEM((8, 8, 128), F32),
            pltpu.VMEM((4, 8, 128), F32),
            pltpu.VMEM((NB, 8, 128), F32),
            pltpu.VMEM((8, 128), F32),
            pltpu.VMEM((8, 128), F32),
            pltpu.VMEM((8, 128), F32),
            pltpu.SemaphoreType.DMA((20,)),
            pltpu.SemaphoreType.DMA((6,)),
            pltpu.SemaphoreType.DMA((8,)),
            pltpu.SemaphoreType.DMA((8,)),
            pltpu.SemaphoreType.DMA((4,)),
            pltpu.SemaphoreType.DMA((4,)),
            pltpu.SemaphoreType.DMA((4,)),
            pltpu.SemaphoreType.DMA((4,)),
        ],
        compiler_params=pltpu.CompilerParams(
            collective_id=0, has_side_effects=True, vmem_limit_bytes=64 * 2**20
        ),
    )(owner_table, bias_vector, *operands, dense_weights)
    results = (
        (field, BF16),
        (field, BF16),
        ((1,) + dense, F32),
        ((R, C), F32),
        ((R, C), F32),
        ((2, R, K1), F32),
        ((R, K2), F32),
        ((K3, R), F32),
        ((C, C), F32),
        ((1, C), F32),
    )
    output, input_grad, dense_grad, in_t, out_t, first_t, second_t, third, skip, bias = pl.pallas_call(
        finish_kernel,
        out_shape=tuple(jax.ShapeDtypeStruct(*result) for result in results),
        in_specs=[hbm] * 8,
        out_specs=(hbm,) * len(results),
        scratch_shapes=[
            pltpu.VMEM(blocks, BF16),
            pltpu.VMEM((NB, 8, 128), F32),
            pltpu.VMEM(one_t.shape, BF16),
            pltpu.VMEM(three_t.shape, BF16),
            pltpu.VMEM(row, BF16),
            pltpu.VMEM(field, BF16),
            pltpu.VMEM((1,) + dense, F32),
            pltpu.VMEM(field, BF16),
            pltpu.VMEM((CG * N1, 256), BF16),
            pltpu.VMEM((HALF, 128), F32),
        ]
        + [pltpu.VMEM(*result) for result in results[3:]]
        + [pltpu.SemaphoreType.DMA((28,))],
        compiler_params=pltpu.CompilerParams(vmem_limit_bytes=64 * 2**20),
    )(received, packed, one_t, three_t, skip_part, output, dense_grad, grad_row)
    return (
        output.reshape(inputs.shape),
        input_grad.reshape(inputs.shape),
        dense_grad,
        in_t.T,
        out_t.T,
        jnp.swapaxes(first_t, 1, 2),
        second_t.T,
        third,
        skip,
        bias.reshape(C),
    )


def solution(mesh):
    field = P("batch", "space", None, None, None)
    dense = P("space", "batch", None, None, None)
    whole = P()
    return jax.shard_map(
        local,
        mesh=mesh,
        in_specs=(field, field, dense, whole, P("space", None, None)) + (whole,) * 7,
        out_specs=(field, field, dense) + (whole,) * 7,
        check_vma=False,
    )
```

```python
import math

import jax
import jax.numpy as jnp
import ml_dtypes
import numpy as np
from jax import lax
from jax.experimental import pallas as pl
from jax.experimental.pallas import tpu as pltpu
from jax.sharding import PartitionSpec as P

MESH = pl.DeviceIdType.MESH
F32 = jnp.float32
BF16 = jnp.bfloat16
HIGH = lax.Precision.HIGHEST

C = 64
N1 = 64
N2 = 64
N3 = 128
K1 = 32
K2 = 32
K3 = 16
L2 = 16
R = 16
SAMPLES = 8
NS = 32
NB = 8
ROWS = N2 // NS
CG = 8
CQ = 8
SLOTS = L2 // NB
HALF = NS * 16
GRAD_SCALE = float(SAMPLES * N1 * N2 * N3) ** (-0.5)


def rounded(values):
    return np.asarray(values, np.float32).astype(ml_dtypes.bfloat16)


def twiddles(frequency, length):
    index = np.mod(frequency[:, None] * np.arange(length)[None, :], length)
    radians = index.astype(np.float32) * np.float32(2.0 * math.pi / length)
    return np.cos(radians), np.sin(radians)


def retained(amount):
    position = np.arange(amount)
    return np.where(position % 2 == 0, position // 2, -((position + 1) // 2))


def build_tables():
    factor = float(N1 * N2 * N3 * K1 * K2 * K3) ** (-0.25)
    cos1, sin1 = twiddles(retained(K1), N1)
    t0 = np.float32(factor) * cos1
    t1 = np.float32(-factor) * sin1
    one = np.block([[t0, -t1], [t1, t0]])
    cos2, sin2 = twiddles(retained(K2), N2)
    two = np.zeros((2, K2, N2, 2), np.float32)
    two[0, :, :, 0] = cos2
    two[0, :, :, 1] = sin2
    two[1, :, :, 0] = -sin2
    two[1, :, :, 1] = cos2
    two = two.reshape(2, K2, NS, ROWS, 2).transpose(0, 1, 3, 2, 4).reshape(2 * K2, 2 * N2)
    cos3, sin3 = twiddles(np.arange(K3), N3)
    three = np.zeros((CQ, N3, 2, K3, CQ), np.float32)
    for q in range(CQ):
        three[q, :, 0, :, q] = cos3.T
        three[q, :, 1, :, q] = -sin3.T
    three = three.reshape(CQ * N3, 2 * K3 * CQ)
    eye = np.eye(R, dtype=np.float32)

    def tiled(signs):
        return np.concatenate([sign * eye for sign in signs] + [np.zeros((R, 64), np.float32)], axis=1)

    patterns = np.concatenate(
        [
            tiled((1, 0, 0, 1)),
            tiled((1, 0, 1, 0)),
            tiled((0, 1, -1, 0)),
            tiled((0, 1, 0, 1)),
            tiled((1, 0, 0, -1)),
            tiled((0, 1, 1, 0)),
        ],
        axis=1,
    )
    spread = np.stack([tiled((1, 1, 1, 1)), tiled((1, 1, 0, 0)), tiled((0, 0, 1, 1))])
    select = np.zeros((K3, K3, 128), np.float32)
    for k in range(K3):
        select[k, k] = 1.0
    return (
        rounded(three),
        rounded(three.T),
        rounded(one),
        rounded(one.T),
        rounded(two),
        rounded(two.T),
        rounded(patterns),
        spread.astype(np.float32),
        rounded(select.reshape(K3, K3 * 128)),
    )


def dot(a, b, precision=None):
    return jnp.dot(a, b, preferred_element_type=F32, precision=precision)


def dot_nt(a, b, precision=None):
    return lax.dot_general(
        a, b, (((1,), (1,)), ((), ())), preferred_element_type=F32, precision=precision
    )


def dot_tn(a, b):
    return lax.dot_general(a, b, (((0,), (0,)), ((), ())), preferred_element_type=F32)


def lanes(shape):
    return lax.broadcasted_iota(jnp.int32, shape, len(shape) - 1)


def rows(shape):
    return lax.broadcasted_iota(jnp.int32, shape, 0)


def swap_groups(parts):
    parts = list(parts)
    group = lanes(parts[0].shape) // CQ
    for bit in (1, 2, 4, 8):
        low = (group & bit) == 0
        for a in range(16):
            if a & bit:
                continue
            first, second = parts[a], parts[a + bit]
            parts[a] = jnp.where(low, first, pltpu.roll(second, 8 * bit, 1))
            parts[a + bit] = jnp.where(low, pltpu.roll(first, 128 - 8 * bit, 1), second)
    return parts


def left_by(value, amount):
    return pltpu.roll(value, 128 - amount, 1)


def drain(block, sem):
    pltpu.make_async_copy(block, block, sem).wait()


def backward_row(blocks, zf, left_v, one_t):
    zf[...] = blocks.reshape(HALF, 128).astype(F32)
    block = jnp.concatenate(
        [
            jnp.concatenate(
                [zf[pl.ds(part * 8 + g, K1, stride=16), :].astype(BF16) for part in range(2)],
                axis=0,
            )
            for g in range(CG)
        ],
        axis=1,
    )
    field = dot(one_t, block).astype(BF16)
    for g in range(CG):
        left_v[g * N1 : (g + 1) * N1, :128] = field[:N1, g * 128 : (g + 1) * 128]
        left_v[g * N1 : (g + 1) * N1, 128:] = field[N1:, g * 128 : (g + 1) * 128]


def each_pair(left_v, three_t, body, after=None):
    @pl.loop(0, CQ // 2, unroll=4)
    def _(pair):
        column = pl.multiple_of(pair * 256, 256)
        field = dot(left_v[...], three_t[:, pl.ds(column, 256)])
        made = [
            body(pair * 2 + half, field[:, half * 128 : (half + 1) * 128].reshape(CG, N1, N3))
            for half in range(2)
        ]
        if after is not None:
            after(column, jnp.concatenate([v.reshape(CG * N1, N3) for v in made], axis=1))


def kernel(
    owner_ref,
    bias_ref,
    x_hbm,
    three_hbm,
    one_hbm,
    hot_hbm,
    skip_hbm,
    fin_hbm,
    fout_hbm,
    first_hbm,
    second_hbm,
    third_hbm,
    two_hbm,
    two_t_hbm,
    pat_hbm,
    spread_hbm,
    select_hbm,
    one_t_hbm,
    three_t_hbm,
    cot_hbm,
    w_hbm,
    out_hbm,
    skip_out_hbm,
    ig_hbm,
    dg_hbm,
    blocks_hbm,
    red_hbm,
    x_ref,
    three_ref,
    one_ref,
    hot_ref,
    skip_ref,
    fin_ref,
    fout_ref,
    first_ref,
    second_ref,
    third_ref,
    two_ref,
    two_t_ref,
    pat_ref,
    spread_ref,
    select_ref,
    one_t_ref,
    three_t_ref,
    cot_v,
    w_v,
    out_v,
    gp_v,
    dg_v,
    skip_v,
    ig_v,
    kron_v,
    kron_back_v,
    left_v,
    total_v,
    zf,
    sbuf,
    rbuf,
    bsend,
    brecv,
    sm,
    s16,
    maskf,
    ph,
    coef_b,
    prod_v,
    fac_v,
    xs,
    bz,
    lefts_v,
    grads_v,
    sgs,
    pk,
    r_batch,
    r_near,
    r_far,
    r_all,
    part_near,
    part_far,
    part_all,
    in_sem,
    out_sem,
    ssend,
    srecv,
    bssem,
    brsem,
    rsend,
    rrecv,
):
    me_s = lax.axis_index("space")
    me_b = lax.axis_index("batch")
    def fetch(src, dst, index):
        copy = pltpu.make_async_copy(src, dst, in_sem.at[index])
        copy.start()
        return copy

    x_copies = [fetch(x_hbm.at[0], x_ref.at[0], 0)]
    three_copy = fetch(three_hbm, three_ref, 2)
    one_copy = fetch(one_hbm, one_ref, 3)
    x_copies.append(fetch(x_hbm.at[1], x_ref.at[1], 1))
    barrier = pltpu.get_barrier_semaphore()

    def each_space_peer(body):
        for step in (2, 1, 3, 0):

            @pl.loop(0 if step else 1, 8)
            def _(d):
                body(
                    lax.rem(me_s // 8 + d // 2, 4) * 8
                    + lax.rem(me_s // 2 + step, 4) * 2
                    + lax.rem(me_s + d, 2)
                )

    def greet(peer):
        pl.semaphore_signal(barrier, inc=1, device_id={"space": peer}, device_id_type=MESH)

    each_space_peer(greet)

    def each_batch_peer(body):
        for z_step, y_step in ((1, 2), (1, 1), (1, 3), (0, 2), (1, 0), (0, 1), (0, 3)):
            body(lax.rem(me_b // 4 + z_step, 2) * 4 + lax.rem(me_b + y_step, 4))

    def greet_batch(peer):
        pl.semaphore_signal(barrier, inc=1, device_id={"batch": peer}, device_id_type=MESH)

    each_batch_peer(greet_batch)

    small_copies = [
        fetch(src, dst, 4 + index)
        for index, (src, dst) in enumerate(
            (
                (hot_hbm, hot_ref),
                (skip_hbm, skip_ref),
                (fin_hbm, fin_ref),
                (fout_hbm, fout_ref),
                (first_hbm, first_ref),
                (second_hbm, second_ref),
                (third_hbm, third_ref),
                (two_hbm, two_ref),
                (two_t_hbm, two_t_ref),
                (pat_hbm, pat_ref),
                (spread_hbm, spread_ref),
                (select_hbm, select_ref),
                (one_t_hbm, one_t_ref),
                (three_t_hbm, three_t_ref),
            )
        )
    ]
    cot_copy = fetch(cot_hbm, cot_v, 18)
    w_copy = fetch(w_hbm.at[0], w_v, 19)

    def space_start(index):
        def send_block(peer):
            pltpu.make_async_remote_copy(
                src_ref=sbuf.at[index, peer],
                dst_ref=rbuf.at[index, me_s],
                send_sem=ssend.at[index],
                recv_sem=srecv.at[index],
                device_id={"space": peer},
                device_id_type=MESH,
            ).start()

        each_space_peer(send_block)
        rbuf[index, me_s] = sbuf[index, me_s]

    def space_wait(index):
        drain(rbuf.at[index, pl.ds(0, NS - 1)], srecv.at[index])

    def batch_start(phase):
        def send_block(peer):
            pltpu.make_async_remote_copy(
                src_ref=bsend.at[phase, peer],
                dst_ref=brecv.at[phase, me_b],
                send_sem=bssem.at[phase],
                recv_sem=brsem.at[phase],
                device_id={"batch": peer},
                device_id_type=MESH,
            ).start()

        each_batch_peer(send_block)
        brecv[phase, me_b] = bsend[phase, me_b]

    def batch_wait(phase):
        drain(brecv.at[phase, pl.ds(0, NB - 1)], brsem.at[phase])

    def forward_row(src, n, index):
        total = None
        for q in range(0, CQ, 2):
            pair = jnp.concatenate(
                [src[n, :, q].reshape(CG * N1, N3), src[n, :, q + 1].reshape(CG * N1, N3)], axis=1
            )
            term = dot(pair, three_ref[q * N3 : (q + 2) * N3, :])
            total = term if total is None else total + term
        fill_row(total, n, index)

    def fill_row(total, n, index):
        total = total.astype(BF16)
        right = jnp.concatenate(
            [
                jnp.concatenate(
                    [total[g * N1 : (g + 1) * N1, :128], total[g * N1 : (g + 1) * N1, 128:]], axis=0
                )
                for g in range(CG)
            ],
            axis=1,
        )
        modes = dot(one_ref[...], right)
        for g in range(CG):
            for part in range(2):
                zf[pl.ds(n * HALF + part * 8 + g, K1, stride=16), :] = modes[
                    part * K1 : (part + 1) * K1, g * 128 : (g + 1) * 128
                ]
        sbuf[index] = zf[n * HALF : (n + 1) * HALF, :].astype(BF16).reshape(NS, 16, 128)

    def modes_in(phase, table):
        for n in range(ROWS):
            space_wait(2 * phase + n)
            zf[n * HALF : (n + 1) * HALF, :] = rbuf[2 * phase + n].reshape(HALF, 128).astype(F32)
        cells = jnp.concatenate(
            [zf[pl.ds(g, 2 * N2, stride=8), :].astype(BF16) for g in range(CG)], axis=1
        )
        modes = dot(table, cells)
        parts = [
            modes[part * K2 : (part + 1) * K2, g * 128 : (g + 1) * 128]
            for part in range(2)
            for g in range(CG)
        ]
        return swap_groups(parts)

    def modes_out(by_frequency, table, phase):
        parts = swap_groups(by_frequency)
        spectrum = jnp.concatenate(
            [
                jnp.concatenate([parts[part * CG + g] for g in range(CG)], axis=1).astype(BF16)
                for part in range(2)
            ],
            axis=0,
        )
        for n in range(ROWS):
            cells = dot(table[n * N2 : (n + 1) * N2], spectrum)
            for g in range(CG):
                zf[pl.ds(n * HALF + g, N2, stride=8), :] = cells[:, g * 128 : (g + 1) * 128]
            sbuf[2 * phase + n] = (
                zf[n * HALF : (n + 1) * HALF, :].astype(BF16).reshape(NS, 16, 128)
            )
            space_start(2 * phase + n)

    def mix_channels(src, kron, with_bias):
        @pl.loop(0, N1 // 16)
        def _(step):
            cut = pl.ds(pl.multiple_of(step * 16, 16), 16)
            right = jnp.concatenate(
                [src[n, :, :, cut, :].reshape(C * 16, N3) for n in range(ROWS)], axis=1
            )
            mixed = dot(kron[...], right)
            for n in range(ROWS):
                value = mixed[:, n * N3 : (n + 1) * N3].reshape(C, 16, N3)
                if with_bias:
                    value = jnp.concatenate([value[c : c + 1] + bias_ref[c] for c in range(C)], axis=0)
                skip_v[n, :, :, cut, :] = value.astype(BF16).reshape(CG, CQ, 16, N3)

    spread_rows = (rows((C * 16, C)) // 16 == lanes((C * 16, C))).astype(F32)
    spread_half = spread_rows.astype(BF16)

    def build_kron(base, kron):
        expanded = dot(spread_half, base).astype(BF16)
        for block in range(4):
            cut = slice(block * 256, (block + 1) * 256)
            full = dot_nt(expanded[cut], spread_half)
            same = (rows((256, 1024)) & 15) == (lanes((256, 1024)) & 15)
            kron[cut, :] = jnp.where(same, full, 0.0).astype(BF16)

    three_copy.wait()
    one_copy.wait()
    for n in range(ROWS):
        x_copies[n].wait()
        forward_row(x_ref, n, n)
    pl.semaphore_wait(barrier, NS - 1 + NB - 1)
    for n in range(ROWS):
        space_start(n)

    for copy in small_copies:
        copy.wait()
    side = (2 * K2, 2 * K2)

    def permutation(index, other):
        position = index & (K2 - 1)
        target = index
        for slot in range(L2):
            target = jnp.where(position == slot, index - position + owner_ref[slot], target)
        return (target == other).astype(F32)

    perm = permutation(rows(side), lanes(side))
    perm_t = permutation(lanes(side), rows(side))
    perm_half = perm.astype(BF16)
    two = dot(perm_half, two_ref[...]).astype(BF16)
    two_t = dot_nt(two_t_ref[...], perm_half).astype(BF16)
    second = dot_nt(perm[:K2, :K2], second_ref[...], HIGH)
    second_l = dot(second, spread_ref[0], HIGH)
    third_l = dot(third_ref[...], spread_ref[0], HIGH)
    own = (lanes((8, K1)) == me_s).astype(F32)
    first_l = (
        dot(dot_nt(own, first_ref[0], HIGH), spread_ref[1], HIGH)
        + dot(dot_nt(own, first_ref[1], HIGH), spread_ref[2], HIGH)
    )[0:1]
    for k in range(K3):
        ph[k * K2 : (k + 1) * K2, :] = first_l * (second_l * third_l[k : k + 1])
    hot = dot(perm_half[:L2, :L2], hot_ref[0].astype(F32).astype(BF16)).astype(BF16)
    spread_hot = dot(hot, select_ref[...])
    for k in range(K3):
        maskf[k] = spread_hot[:, k * 128 : (k + 1) * 128]

    def expand(factor, top, bottom, width):
        pieces = [
            dot_tn(factor, pat_ref[:, start * 128 : start * 128 + width]) for start in (top, bottom)
        ]
        return jnp.concatenate(pieces, axis=0).astype(BF16)

    fin_all = expand(fin_ref[...], 0, 2, 256)
    fin_b = fin_all[:, 128:]
    fout_b = expand(fout_ref[...], 1, 3, 128)
    fout_c = expand(fout_ref[...], 4, 5, 128)

    build_kron(skip_ref[...].astype(F32).T.astype(BF16), kron_v)
    mix_channels(x_ref, kron_v, True)
    build_kron(skip_ref[...], kron_back_v)

    spectrum = modes_in(0, two)
    for k in range(K3):
        sm[k * K2 : (k + 1) * K2, :] = spectrum[k]

    def slots_out(phase):
        for owner in range(NB):
            for slot in range(SLOTS):
                bsend[phase, owner, slot * K3 : (slot + 1) * K3, :] = sm[
                    pl.ds(owner * SLOTS + slot, K3, stride=K2), :
                ].astype(BF16)

    def slots_in(phase):
        bz[...] = brecv[phase].reshape(NB * 32, 128).astype(F32)
        for slot in range(L2):
            sm[pl.ds(slot, K3, stride=K2), :] = bz[slot * K3 : (slot + 1) * K3, :]

    slots_out(0)
    batch_start(0)
    s16[...] = sm[...].astype(BF16)
    coef = dot(s16[...], fin_all)
    coef_b[...] = coef[:, 128:]
    prod_v[...] = (coef[:, :128] * ph[...]).astype(BF16)
    fac_v[...] = dot_nt(prod_v[...], fout_b)
    w_copy.wait()
    batch_wait(0)
    xs[...] = brecv[0].reshape(NB * 32, 128).astype(F32)
    sign = jnp.where(lanes((8, 128)) < 64, -1.0, 1.0)
    for index in range(SLOTS * K3):
        slot, k = divmod(index, K3)
        value = xs[pl.ds(index, NB, stride=32), :]
        left = jnp.concatenate([value, pltpu.roll(value, 64, 1)], axis=0).astype(BF16)
        lefts_v[index] = left
        both = dot(left[:, :C], w_v[slot, k])
        bz[pl.ds(index, NB, stride=32), :] = both[:8] + sign * pltpu.roll(both[8:], 64, 1)
    bsend[1] = bz[...].astype(BF16).reshape(NB, 32, 128)
    batch_start(1)
    batch_wait(1)
    slots_in(1)
    out_spec = []
    for k in range(K3):
        low = jnp.where(
            maskf[k] > 0.0, sm[k * K2 : k * K2 + L2, :], fac_v[k * K2 : k * K2 + L2, :]
        )
        out_spec.append(jnp.concatenate([low, fac_v[k * K2 + L2 : (k + 1) * K2, :]], axis=0))
    modes_out(out_spec, two_t, 1)
    cot_copy.wait()

    for n in range(ROWS):
        space_wait(2 + n)
        backward_row(rbuf[2 + n], zf.at[pl.ds(n * HALF, HALF)], left_v, one_t_ref[...])

        def activate(q, field):
            v = field + skip_v[n, :, q].astype(F32)
            square = v * v
            k0 = math.sqrt(2.0 / math.pi)
            gate = 0.5 * jnp.tanh(v * (k0 + (k0 * 0.044715) * square)) + 0.5
            active = v * gate
            out_v[n, :, q] = active.astype(BF16)
            slope = gate + active * (1.0 - gate) * (2.0 * k0 + (6.0 * k0 * 0.044715) * square)
            made = (cot_v[n, :, q].astype(F32) * slope).astype(BF16)
            gp_v[n, :, q] = made
            return made

        def gather(column, pair):
            total_v[...] += dot(pair, three_ref[pl.ds(column, 256), :])

        total_v[...] = jnp.zeros_like(total_v)
        each_pair(left_v, three_t_ref, activate, gather)
        fill_row(total_v[...], n, 4 + n)
        space_start(4 + n)
    out_copy = pltpu.make_async_copy(out_v, out_hbm, out_sem.at[0])
    out_copy.start()

    same = ((rows((16, 256)) & 15) == (lanes((16, 256)) & 15)).astype(F32)
    ones = jnp.ones((16, ROWS * 4 * N3), BF16)

    def cut_channels(src, start):
        return jnp.concatenate(
            [
                src[n, pl.ds(start * 2, 2), :, b * 16 : (b + 1) * 16, :].reshape(256, N3)
                for n in range(ROWS)
                for b in range(N1 // 16)
            ],
            axis=1,
        )

    for column in range(4):
        grads = cut_channels(gp_v, column)
        here = slice(column * 256, (column + 1) * 256)
        sgs[C : C + 16, here] = dot_nt(ones, grads)

        @pl.loop(0, 4)
        def _(block):
            full = dot_nt(cut_channels(x_ref, block), grads).reshape(16, 16, 256)
            sgs[pl.ds(pl.multiple_of(block * 16, 16), 16), here] = jnp.sum(full * same[None], axis=1)

    skip_grad = dot(sgs[...], spread_rows, HIGH)

    grad_spec = modes_in(2, two)
    cold = []
    for k in range(K3):
        low = grad_spec[k][:L2]
        sm[k * K2 : k * K2 + L2, :] = low * maskf[k]
        cold.append(
            jnp.concatenate([low * (1.0 - maskf[k]), grad_spec[k][L2:]], axis=0).astype(BF16)
        )
    slots_out(2)
    batch_start(2)
    cold = jnp.concatenate(cold, axis=0)
    back = dot(cold, fout_c)
    prod_back = (back * ph[...]).astype(BF16)
    fac_v[...] = dot_nt(prod_back, fin_b)
    in_full = dot_tn(s16[...], prod_back)
    out_full = dot_tn(cold, prod_v[...])
    back = back * coef_b[...]
    first_sum = jnp.zeros((K2, 128), F32)
    second_sum = jnp.zeros((K2, 128), F32)
    third_rows = []
    for k in range(K3):
        term = back[k * K2 : (k + 1) * K2]
        by_third = term * third_l[k : k + 1]
        first_sum = first_sum + by_third * second_l
        second_sum = second_sum + by_third * first_l
        third_rows.append(jnp.sum(term * first_l * second_l, axis=0, keepdims=True))
    first_row = jnp.sum(first_sum, axis=0, keepdims=True)
    third_sum = jnp.concatenate(third_rows, axis=0)

    def folded(full):
        pairs = full + left_by(full, 32)
        return pairs[:C] + left_by(pairs[C:], 16)

    shape = (C, 128)
    lane, row = lanes(shape), rows(shape)

    def below(value):
        return jnp.concatenate([value, jnp.zeros((C - value.shape[0], 128), F32)], axis=0)

    def fold_all(value):
        pairs = value + left_by(value, 16)
        return pairs + left_by(pairs, 32)

    second_part = dot(perm_t[:K2, :K2], fold_all(second_sum), HIGH)
    third_part = fold_all(third_sum)
    first_part = first_row + left_by(first_row, 16)
    middle = jnp.concatenate([second_part, third_part, jnp.zeros((16, 128), F32)], axis=0)
    zero64 = jnp.zeros((C, 64), F32)
    wide = jnp.concatenate([skip_grad[:C], zero64], axis=1)
    bias_row = jnp.concatenate([skip_grad[C : C + 1], zero64[:1]], axis=1)
    packed = jnp.where(lane < 64, wide, 0.0)
    packed = jnp.where((lane >= 64) & (lane < 80), pltpu.roll(folded(in_full), 64, 1), packed)
    packed = jnp.where((lane >= 80) & (lane < 96), pltpu.roll(folded(out_full), 80, 1), packed)
    inside = (lane >= 96) & (lane < 112)
    packed = jnp.where(inside, pltpu.roll(middle, 96, 1), packed)
    for piece in range(4):
        moved = pltpu.roll(bias_row, 96 - 16 * piece, 1)
        packed = jnp.where(inside & (row == 48 + piece), moved, packed)
    last = lane >= 112
    packed = jnp.where(last & (row == me_s), pltpu.roll(first_part, 112, 1), packed)
    packed = jnp.where(last & (row == me_s + 32), pltpu.roll(first_part, 80, 1), packed)
    pk[...] = (packed * GRAD_SCALE).reshape(NB, 8, 128)

    def send(src, dst, step, to):
        pltpu.make_async_remote_copy(
            src_ref=src,
            dst_ref=dst,
            send_sem=rsend.at[step],
            recv_sem=rrecv.at[step],
            device_id=to,
            device_id_type=MESH,
        ).start()

    near = (me_s // 8) * 2 + lax.rem(me_s, 2)
    far = lax.rem(me_s // 2, 4)

    @pl.loop(1, NB)
    def _(d):
        peer = lax.rem(me_b + d, NB)
        send(pk.at[peer], r_batch.at[me_b], 0, {"batch": peer})

    r_batch[me_b] = pk[me_b]

    batch_wait(2)
    bz[...] = brecv[2].reshape(NB * 32, 128).astype(F32)
    for index in range(SLOTS * K3):
        slot, k = divmod(index, K3)
        grad = bz[pl.ds(index, NB, stride=32), :]
        grads = jnp.concatenate([grad, -sign * pltpu.roll(grad, 64, 1)], axis=0).astype(BF16)
        grads_v[index] = grads
        weights = w_v[slot, k]
        both = dot_nt(grads, jnp.concatenate([weights, weights], axis=0))
        bz[pl.ds(index, NB, stride=32), :] = jnp.where(sign < 0.0, both[:8], both[8:])
    bsend[3] = bz[...].astype(BF16).reshape(NB, 32, 128)
    batch_start(3)

    drain(r_batch.at[pl.ds(0, NB - 1)], rrecv.at[0])
    part_near[...] = jnp.sum(r_batch[...], axis=0)

    @pl.loop(1, 8)
    def _(d):
        slot = lax.rem(near + d, 8)
        peer = (slot // 2) * 8 + far * 2 + lax.rem(slot, 2)
        send(part_near, r_near.at[near], 1, {"space": peer})

    r_near[near] = part_near[...]

    mix_channels(gp_v, kron_back_v, False)
    skip_copy = pltpu.make_async_copy(skip_v, skip_out_hbm, out_sem.at[2])
    skip_copy.start()

    batch_wait(3)
    slots_in(3)
    grad_spectrum = []
    for k in range(K3):
        low = fac_v[k * K2 : k * K2 + L2, :] + sm[k * K2 : k * K2 + L2, :]
        grad_spectrum.append(
            jnp.concatenate([low, fac_v[k * K2 + L2 : (k + 1) * K2, :]], axis=0)
        )
    modes_out(grad_spectrum, two_t, 3)


    drain(r_near.at[pl.ds(0, 7)], rrecv.at[1])
    part_far[...] = jnp.sum(r_near[...], axis=0)

    @pl.loop(1, 4)
    def _(d):
        slot = lax.rem(far + d, 4)
        peer = (near // 2) * 8 + slot * 2 + lax.rem(near, 2)
        send(part_far, r_far.at[far], 2, {"space": peer})

    r_far[far] = part_far[...]

    for index in range(SLOTS * K3):
        slot, k = divmod(index, K3)
        dg_v[slot, k] = dot_tn(lefts_v[index], grads_v[index])[:C]
    dg_copy = pltpu.make_async_copy(dg_v, dg_hbm.at[0], out_sem.at[1])
    dg_copy.start()

    drain(r_far.at[pl.ds(0, 3)], rrecv.at[2])
    part_all[...] = jnp.sum(r_far[...], axis=0)

    @pl.loop(1, NB)
    def _(d):
        send(part_all, r_all.at[me_b], 3, {"batch": lax.rem(me_b + d, NB)})

    r_all[me_b] = part_all[...]
    space_wait(6)
    backward_row(rbuf[6], zf.at[pl.ds(0, HALF)], left_v, one_t_ref[...])

    def finish(q, field):
        ig_v[:, q] = (field + skip_v[0, :, q].astype(F32)).astype(BF16)

    each_pair(left_v, three_t_ref, finish)
    ig_copy = pltpu.make_async_copy(ig_v, ig_hbm, out_sem.at[3])
    ig_copy.start()

    space_wait(7)
    blocks_copy = pltpu.make_async_copy(rbuf.at[7], blocks_hbm, out_sem.at[4])
    blocks_copy.start()
    drain(r_all.at[pl.ds(0, NB - 1)], rrecv.at[3])
    red_copy = pltpu.make_async_copy(r_all, red_hbm, out_sem.at[5])
    red_copy.start()
    for index in range(8):
        drain(sbuf.at[index, pl.ds(0, NS - 1)], ssend.at[index])
    for phase in range(4):
        drain(bsend.at[phase, pl.ds(0, NB - 1)], bssem.at[phase])
    drain(pk.at[pl.ds(0, NB - 1)], rsend.at[0])
    drain(r_near.at[pl.ds(0, 7)], rsend.at[1])
    drain(r_far.at[pl.ds(0, 3)], rsend.at[2])
    drain(r_all.at[pl.ds(0, NB - 1)], rsend.at[3])
    for started in (out_copy, dg_copy, skip_copy, ig_copy, blocks_copy, red_copy):
        started.wait()


def finish_kernel(
    blocks_hbm,
    packed_hbm,
    one_t_hbm,
    three_t_hbm,
    skip_hbm,
    out_in,
    dg_in,
    ig_in,
    out_hbm,
    ig_hbm,
    dg_hbm,
    fin_hbm,
    fout_hbm,
    first_hbm,
    second_hbm,
    third_hbm,
    mix_hbm,
    bias_hbm,
    blocks_v,
    packed_v,
    one_t_v,
    three_t_v,
    skip_v,
    out_v,
    dg_v,
    ig_v,
    left_v,
    zf,
    fin_v,
    fout_v,
    first_v,
    second_v,
    third_v,
    mix_v,
    bias_v,
    sem,
):
    def copy(src, dst, index):
        started = pltpu.make_async_copy(src, dst, sem.at[index])
        started.start()
        return started

    arriving = [
        copy(src, dst, index)
        for index, (src, dst) in enumerate(
            (
                (blocks_hbm, blocks_v),
                (one_t_hbm, one_t_v),
                (three_t_hbm, three_t_v),
                (skip_hbm.at[1], skip_v),
                (packed_hbm, packed_v),
                (out_in, out_v),
                (ig_in, ig_v.at[0]),
                (dg_in, dg_v),
            )
        )
    ]
    waits = []

    def pass_on(index, src, dst):
        arriving[index].wait()
        waits.append(copy(src, dst, 8 + index))

    for index in range(4):
        arriving[index].wait()
    backward_row(blocks_v[...], zf, left_v, one_t_v[...])
    arriving[4].wait()
    packed = packed_v[...].reshape(C, 128)
    turned = packed.T
    fin_v[...] = turned[64:80]
    fout_v[...] = turned[80:96]
    second_v[...] = turned[96:112, :K2]
    first_v[0] = turned[112:, :K1]
    first_v[1] = turned[112:, K1:]
    third_v[...] = left_by(packed, 96)[K2 : K2 + K3, :R]
    mix_v[...] = packed[:, :C]
    bias = jnp.zeros((1, 128), F32)
    lane = lanes((1, 128))
    for piece in range(4):
        moved = pltpu.roll(packed[48 + piece : 49 + piece], (32 + 16 * piece) % 128, 1)
        bias = jnp.where((lane >= 16 * piece) & (lane < 16 * (piece + 1)), moved, bias)
    bias_v[...] = bias[:, :C]
    small = (
        (fin_v, fin_hbm),
        (fout_v, fout_hbm),
        (first_v, first_hbm),
        (second_v, second_hbm),
        (third_v, third_hbm),
        (mix_v, mix_hbm),
        (bias_v, bias_hbm),
    )
    waits += [copy(src, dst, 17 + index) for index, (src, dst) in enumerate(small)]
    for pair in range(CQ // 2):
        field = dot(left_v[...], three_t_v[:, pair * 256 : (pair + 1) * 256])
        for half in range(2):
            q = pair * 2 + half
            value = field[:, half * 128 : (half + 1) * 128].reshape(CG, N1, N3)
            ig_v[1, :, q] = (value + skip_v[:, q].astype(F32)).astype(BF16)
        cut = (1, slice(None), pl.ds(pair * 2, 2))
        waits.append(copy(ig_v.at[cut], ig_hbm.at[cut], 24 + pair))
        if pair == 0:
            pass_on(5, out_v, out_hbm)
        if pair == 1:
            pass_on(6, ig_v.at[0], ig_hbm.at[0])
        if pair == 2:
            pass_on(7, dg_v, dg_hbm)
    for started in waits:
        started.wait()


def local(
    inputs,
    cotangent,
    dense_weights,
    owner_table,
    hot_mask,
    skip_weight,
    bias_vector,
    input_factor,
    output_factor,
    first_factor,
    second_factor,
    third_factor,
):
    field = (ROWS, CG, CQ, N1, N3)
    three, three_t, one, one_t, two, two_t, patterns, spread, select = [
        jnp.asarray(table) for table in build_tables()
    ]
    smem = pl.BlockSpec(memory_space=pltpu.SMEM)
    hbm = pl.BlockSpec(memory_space=pltpu.HBM)
    dense = (SLOTS, K3, C, 2 * C)
    operands = (
        inputs.reshape(field),
        three,
        one,
        hot_mask,
        skip_weight,
        input_factor.T,
        output_factor.T,
        jnp.swapaxes(first_factor, 1, 2),
        second_factor.T,
        third_factor,
        two,
        two_t,
        patterns,
        spread,
        select,
        one_t,
        three_t,
        cotangent.reshape(field),
    )
    blocks = (NS, 16, 128)
    row = field[1:]
    output, skip_part, grad_row, dense_grad, received, packed = pl.pallas_call(
        kernel,
        out_shape=(
            jax.ShapeDtypeStruct(field, BF16),
            jax.ShapeDtypeStruct(field, BF16),
            jax.ShapeDtypeStruct(row, BF16),
            jax.ShapeDtypeStruct((1,) + dense, F32),
            jax.ShapeDtypeStruct(blocks, BF16),
            jax.ShapeDtypeStruct((NB, 8, 128), F32),
        ),
        in_specs=[smem, smem] + [hbm] * 19,
        out_specs=(hbm,) * 6,
        scratch_shapes=[pltpu.VMEM(value.shape, value.dtype) for value in operands]
        + [
            pltpu.VMEM(dense, BF16),
            pltpu.VMEM(field, BF16),
            pltpu.VMEM(field, BF16),
            pltpu.VMEM(dense, F32),
            pltpu.VMEM(field, BF16),
            pltpu.VMEM(row, BF16),
            pltpu.VMEM((C * 16, C * 16), BF16),
            pltpu.VMEM((C * 16, C * 16), BF16),
            pltpu.VMEM((CG * N1, 256), BF16),
            pltpu.VMEM((CG * N1, 256), F32),
            pltpu.VMEM((ROWS * HALF, 128), F32),
            pltpu.VMEM((8,) + blocks, BF16),
            pltpu.VMEM((8,) + blocks, BF16),
            pltpu.VMEM((4, NB, 32, 128), BF16),
            pltpu.VMEM((4, NB, 32, 128), BF16),
            pltpu.VMEM((K3 * K2, 128), F32),
            pltpu.VMEM((K3 * K2, 128), BF16),
            pltpu.VMEM((K3, L2, 128), F32),
            pltpu.VMEM((K3 * K2, 128), F32),
            pltpu.VMEM((K3 * K2, 128), F32),
            pltpu.VMEM((K3 * K2, 128), BF16),
            pltpu.VMEM((K3 * K2, 128), F32),
            pltpu.VMEM((NB * 32, 128), F32),
            pltpu.VMEM((NB * 32, 128), F32),
            pltpu.VMEM((SLOTS * K3, 16, 128), BF16),
            pltpu.VMEM((SLOTS * K3, 16, 128), BF16),
            pltpu.VMEM((C + 16, C * 16), F32),
            pltpu.VMEM((NB, 8, 128), F32),
            pltpu.VMEM((NB, 8, 128), F32),
            pltpu.VMEM((8, 8, 128), F32),
            pltpu.VMEM((4, 8, 128), F32),
            pltpu.VMEM((NB, 8, 128), F32),
            pltpu.VMEM((8, 128), F32),
            pltpu.VMEM((8, 128), F32),
            pltpu.VMEM((8, 128), F32),
            pltpu.SemaphoreType.DMA((20,)),
            pltpu.SemaphoreType.DMA((6,)),
            pltpu.SemaphoreType.DMA((8,)),
            pltpu.SemaphoreType.DMA((8,)),
            pltpu.SemaphoreType.DMA((4,)),
            pltpu.SemaphoreType.DMA((4,)),
            pltpu.SemaphoreType.DMA((4,)),
            pltpu.SemaphoreType.DMA((4,)),
        ],
        compiler_params=pltpu.CompilerParams(
            collective_id=0, has_side_effects=True, vmem_limit_bytes=64 * 2**20
        ),
    )(owner_table, bias_vector, *operands, dense_weights)
    results = (
        (field, BF16),
        (field, BF16),
        ((1,) + dense, F32),
        ((R, C), F32),
        ((R, C), F32),
        ((2, R, K1), F32),
        ((R, K2), F32),
        ((K3, R), F32),
        ((C, C), F32),
        ((1, C), F32),
    )
    output, input_grad, dense_grad, in_t, out_t, first_t, second_t, third, skip, bias = pl.pallas_call(
        finish_kernel,
        out_shape=tuple(jax.ShapeDtypeStruct(*result) for result in results),
        in_specs=[hbm] * 8,
        out_specs=(hbm,) * len(results),
        scratch_shapes=[
            pltpu.VMEM(blocks, BF16),
            pltpu.VMEM((NB, 8, 128), F32),
            pltpu.VMEM(one_t.shape, BF16),
            pltpu.VMEM(three_t.shape, BF16),
            pltpu.VMEM(row, BF16),
            pltpu.VMEM(field, BF16),
            pltpu.VMEM((1,) + dense, F32),
            pltpu.VMEM(field, BF16),
            pltpu.VMEM((CG * N1, 256), BF16),
            pltpu.VMEM((HALF, 128), F32),
        ]
        + [pltpu.VMEM(*result) for result in results[3:]]
        + [pltpu.SemaphoreType.DMA((28,))],
        compiler_params=pltpu.CompilerParams(vmem_limit_bytes=64 * 2**20),
    )(received, packed, one_t, three_t, skip_part, output, dense_grad, grad_row)
    return (
        output.reshape(inputs.shape),
        input_grad.reshape(inputs.shape),
        dense_grad,
        in_t.T,
        out_t.T,
        jnp.swapaxes(first_t, 1, 2),
        second_t.T,
        third,
        skip,
        bias.reshape(C),
    )


def solution(mesh):
    field = P("batch", "space", None, None, None)
    dense = P("space", "batch", None, None, None)
    whole = P()
    return jax.shard_map(
        local,
        mesh=mesh,
        in_specs=(field, field, dense, whole, P("space", None, None)) + (whole,) * 7,
        out_specs=(field, field, dense) + (whole,) * 7,
        check_vma=False,
    )
```

```python
import math

import jax
import jax.numpy as jnp
import ml_dtypes
import numpy as np
from jax import lax
from jax.experimental import pallas as pl
from jax.experimental.pallas import tpu as pltpu
from jax.sharding import PartitionSpec as P

MESH = pl.DeviceIdType.MESH
F32 = jnp.float32
BF16 = jnp.bfloat16
HIGH = lax.Precision.HIGHEST

C = 64
N1 = 64
N2 = 64
N3 = 128
K1 = 32
K2 = 32
K3 = 16
L2 = 16
R = 16
SAMPLES = 8
NS = 32
NB = 8
ROWS = N2 // NS
CG = 8
CQ = 8
SLOTS = L2 // NB
HALF = NS * 16
GRAD_SCALE = float(SAMPLES * N1 * N2 * N3) ** (-0.5)


def rounded(values):
    return np.asarray(values, np.float32).astype(ml_dtypes.bfloat16)


def twiddles(frequency, length):
    index = np.mod(frequency[:, None] * np.arange(length)[None, :], length)
    radians = index.astype(np.float32) * np.float32(2.0 * math.pi / length)
    return np.cos(radians), np.sin(radians)


def retained(amount):
    position = np.arange(amount)
    return np.where(position % 2 == 0, position // 2, -((position + 1) // 2))


def build_tables():
    factor = float(N1 * N2 * N3 * K1 * K2 * K3) ** (-0.25)
    cos1, sin1 = twiddles(retained(K1), N1)
    t0 = np.float32(factor) * cos1
    t1 = np.float32(-factor) * sin1
    one = np.block([[t0, -t1], [t1, t0]])
    cos2, sin2 = twiddles(retained(K2), N2)
    two = np.zeros((2, K2, N2, 2), np.float32)
    two[0, :, :, 0] = cos2
    two[0, :, :, 1] = sin2
    two[1, :, :, 0] = -sin2
    two[1, :, :, 1] = cos2
    two = two.reshape(2, K2, NS, ROWS, 2).transpose(0, 1, 3, 2, 4).reshape(2 * K2, 2 * N2)
    cos3, sin3 = twiddles(np.arange(K3), N3)
    three = np.zeros((CQ, N3, 2, K3, CQ), np.float32)
    for q in range(CQ):
        three[q, :, 0, :, q] = cos3.T
        three[q, :, 1, :, q] = -sin3.T
    three = three.reshape(CQ * N3, 2 * K3 * CQ)
    eye = np.eye(R, dtype=np.float32)

    def tiled(signs):
        return np.concatenate([sign * eye for sign in signs] + [np.zeros((R, 64), np.float32)], axis=1)

    patterns = np.concatenate(
        [
            tiled((1, 0, 0, 1)),
            tiled((1, 0, 1, 0)),
            tiled((0, 1, -1, 0)),
            tiled((0, 1, 0, 1)),
            tiled((1, 0, 0, -1)),
            tiled((0, 1, 1, 0)),
        ],
        axis=1,
    )
    spread = np.stack([tiled((1, 1, 1, 1)), tiled((1, 1, 0, 0)), tiled((0, 0, 1, 1))])
    select = np.zeros((K3, K3, 128), np.float32)
    for k in range(K3):
        select[k, k] = 1.0
    return (
        rounded(three),
        rounded(three.T),
        rounded(one),
        rounded(one.T),
        rounded(two),
        rounded(two.T),
        rounded(patterns),
        spread.astype(np.float32),
        rounded(select.reshape(K3, K3 * 128)),
    )


def dot(a, b, precision=None):
    return jnp.dot(a, b, preferred_element_type=F32, precision=precision)


def dot_nt(a, b, precision=None):
    return lax.dot_general(
        a, b, (((1,), (1,)), ((), ())), preferred_element_type=F32, precision=precision
    )


def dot_tn(a, b):
    return lax.dot_general(a, b, (((0,), (0,)), ((), ())), preferred_element_type=F32)


def lanes(shape):
    return lax.broadcasted_iota(jnp.int32, shape, len(shape) - 1)


def rows(shape):
    return lax.broadcasted_iota(jnp.int32, shape, 0)


def swap_groups(parts):
    parts = list(parts)
    group = lanes(parts[0].shape) // CQ
    for bit in (1, 2, 4, 8):
        low = (group & bit) == 0
        for a in range(16):
            if a & bit:
                continue
            first, second = parts[a], parts[a + bit]
            parts[a] = jnp.where(low, first, pltpu.roll(second, 8 * bit, 1))
            parts[a + bit] = jnp.where(low, pltpu.roll(first, 128 - 8 * bit, 1), second)
    return parts


def left_by(value, amount):
    return pltpu.roll(value, 128 - amount, 1)


def drain(block, sem):
    pltpu.make_async_copy(block, block, sem).wait()


def backward_row(blocks, zf, left_v, one_t):
    zf[...] = blocks.reshape(HALF, 128).astype(F32)
    block = jnp.concatenate(
        [
            jnp.concatenate(
                [zf[pl.ds(part * 8 + g, K1, stride=16), :].astype(BF16) for part in range(2)],
                axis=0,
            )
            for g in range(CG)
        ],
        axis=1,
    )
    field = dot(one_t, block).astype(BF16)
    for g in range(CG):
        left_v[g * N1 : (g + 1) * N1, :128] = field[:N1, g * 128 : (g + 1) * 128]
        left_v[g * N1 : (g + 1) * N1, 128:] = field[N1:, g * 128 : (g + 1) * 128]


def each_pair(left_v, three_t, body, after=None):
    @pl.loop(0, CQ // 2, unroll=4)
    def _(pair):
        column = pl.multiple_of(pair * 256, 256)
        field = dot(left_v[...], three_t[:, pl.ds(column, 256)])
        made = [
            body(pair * 2 + half, field[:, half * 128 : (half + 1) * 128].reshape(CG, N1, N3))
            for half in range(2)
        ]
        if after is not None:
            after(column, jnp.concatenate([v.reshape(CG * N1, N3) for v in made], axis=1))


def kernel(
    owner_ref,
    bias_ref,
    x_hbm,
    three_hbm,
    one_hbm,
    hot_hbm,
    skip_hbm,
    fin_hbm,
    fout_hbm,
    first_hbm,
    second_hbm,
    third_hbm,
    two_hbm,
    two_t_hbm,
    pat_hbm,
    spread_hbm,
    select_hbm,
    one_t_hbm,
    three_t_hbm,
    cot_hbm,
    w_hbm,
    out_hbm,
    skip_out_hbm,
    ig_hbm,
    dg_hbm,
    blocks_hbm,
    red_hbm,
    x_ref,
    three_ref,
    one_ref,
    hot_ref,
    skip_ref,
    fin_ref,
    fout_ref,
    first_ref,
    second_ref,
    third_ref,
    two_ref,
    two_t_ref,
    pat_ref,
    spread_ref,
    select_ref,
    one_t_ref,
    three_t_ref,
    cot_v,
    w_v,
    out_v,
    gp_v,
    dg_v,
    skip_v,
    ig_v,
    kron_v,
    kron_back_v,
    left_v,
    total_v,
    zf,
    sbuf,
    rbuf,
    bsend,
    brecv,
    sm,
    s16,
    maskf,
    ph,
    coef_b,
    prod_v,
    fac_v,
    xs,
    bz,
    lefts_v,
    grads_v,
    sgs,
    pk,
    r_batch,
    r_near,
    r_far,
    r_all,
    part_near,
    part_far,
    part_all,
    in_sem,
    out_sem,
    ssend,
    srecv,
    bssem,
    brsem,
    rsend,
    rrecv,
):
    me_s = lax.axis_index("space")
    me_b = lax.axis_index("batch")
    def fetch(src, dst, index):
        copy = pltpu.make_async_copy(src, dst, in_sem.at[index])
        copy.start()
        return copy

    x_copies = [fetch(x_hbm.at[0], x_ref.at[0], 0)]
    three_copy = fetch(three_hbm, three_ref, 2)
    one_copy = fetch(one_hbm, one_ref, 3)
    x_copies.append(fetch(x_hbm.at[1], x_ref.at[1], 1))
    barrier = pltpu.get_barrier_semaphore()

    def each_space_peer(body):
        for step in (2, 1, 3, 0):

            @pl.loop(0 if step else 1, 8)
            def _(d):
                body(
                    lax.rem(me_s // 8 + d // 2, 4) * 8
                    + lax.rem(me_s // 2 + step, 4) * 2
                    + lax.rem(me_s + d, 2)
                )

    def greet(peer):
        pl.semaphore_signal(barrier, inc=1, device_id={"space": peer}, device_id_type=MESH)

    each_space_peer(greet)

    def each_batch_peer(body):
        for z_step, y_step in ((1, 2), (1, 1), (1, 3), (0, 2), (1, 0), (0, 1), (0, 3)):
            body(lax.rem(me_b // 4 + z_step, 2) * 4 + lax.rem(me_b + y_step, 4))

    def greet_batch(peer):
        pl.semaphore_signal(barrier, inc=1, device_id={"batch": peer}, device_id_type=MESH)

    each_batch_peer(greet_batch)

    small_copies = [
        fetch(src, dst, 4 + index)
        for index, (src, dst) in enumerate(
            (
                (hot_hbm, hot_ref),
                (skip_hbm, skip_ref),
                (fin_hbm, fin_ref),
                (fout_hbm, fout_ref),
                (first_hbm, first_ref),
                (second_hbm, second_ref),
                (third_hbm, third_ref),
                (two_hbm, two_ref),
                (two_t_hbm, two_t_ref),
                (pat_hbm, pat_ref),
                (spread_hbm, spread_ref),
                (select_hbm, select_ref),
                (one_t_hbm, one_t_ref),
                (three_t_hbm, three_t_ref),
            )
        )
    ]
    cot_copy = fetch(cot_hbm, cot_v, 18)
    w_copy = fetch(w_hbm.at[0], w_v, 19)

    def space_start(*indices):
        def send_block(peer):
            for index in indices:
                pltpu.make_async_remote_copy(
                    src_ref=sbuf.at[index, peer],
                    dst_ref=rbuf.at[index, me_s],
                    send_sem=ssend.at[index],
                    recv_sem=srecv.at[index],
                    device_id={"space": peer},
                    device_id_type=MESH,
                ).start()

        each_space_peer(send_block)
        for index in indices:
            rbuf[index, me_s] = sbuf[index, me_s]

    def space_wait(index):
        drain(rbuf.at[index, pl.ds(0, NS - 1)], srecv.at[index])

    def batch_start(phase, fill=None):
        def send_block(peer):
            if fill is not None:
                fill(bsend, phase, peer, peer)
            pltpu.make_async_remote_copy(
                src_ref=bsend.at[phase, peer],
                dst_ref=brecv.at[phase, me_b],
                send_sem=bssem.at[phase],
                recv_sem=brsem.at[phase],
                device_id={"batch": peer},
                device_id_type=MESH,
            ).start()

        each_batch_peer(send_block)
        if fill is not None:
            fill(brecv, phase, me_b, me_b)
        else:
            brecv[phase, me_b] = bsend[phase, me_b]

    def batch_wait(phase):
        drain(brecv.at[phase, pl.ds(0, NB - 1)], brsem.at[phase])

    def forward_row(src, n, index):
        total = None
        for q in range(0, CQ, 2):
            pair = jnp.concatenate(
                [src[n, :, q].reshape(CG * N1, N3), src[n, :, q + 1].reshape(CG * N1, N3)], axis=1
            )
            term = dot(pair, three_ref[q * N3 : (q + 2) * N3, :])
            total = term if total is None else total + term
        fill_row(total, n, index)

    def fill_row(total, n, index):
        total = total.astype(BF16)
        right = jnp.concatenate(
            [
                jnp.concatenate(
                    [total[g * N1 : (g + 1) * N1, :128], total[g * N1 : (g + 1) * N1, 128:]], axis=0
                )
                for g in range(CG)
            ],
            axis=1,
        )
        modes = dot(one_ref[...], right)
        for g in range(CG):
            for part in range(2):
                zf[pl.ds(n * HALF + part * 8 + g, K1, stride=16), :] = modes[
                    part * K1 : (part + 1) * K1, g * 128 : (g + 1) * 128
                ]
        sbuf[index] = zf[n * HALF : (n + 1) * HALF, :].astype(BF16).reshape(NS, 16, 128)

    def modes_in(phase, table):
        for n in range(ROWS):
            space_wait(2 * phase + n)
            zf[n * HALF : (n + 1) * HALF, :] = rbuf[2 * phase + n].reshape(HALF, 128).astype(F32)
        cells = jnp.concatenate(
            [zf[pl.ds(g, 2 * N2, stride=8), :].astype(BF16) for g in range(CG)], axis=1
        )
        modes = dot(table, cells)
        parts = [
            modes[part * K2 : (part + 1) * K2, g * 128 : (g + 1) * 128]
            for part in range(2)
            for g in range(CG)
        ]
        return swap_groups(parts)

    def modes_out(by_frequency, table, phase):
        parts = swap_groups(by_frequency)
        spectrum = jnp.concatenate(
            [
                jnp.concatenate([parts[part * CG + g] for g in range(CG)], axis=1).astype(BF16)
                for part in range(2)
            ],
            axis=0,
        )
        for n in range(ROWS):
            cells = dot(table[n * N2 : (n + 1) * N2], spectrum)
            for g in range(CG):
                zf[pl.ds(n * HALF + g, N2, stride=8), :] = cells[:, g * 128 : (g + 1) * 128]
            sbuf[2 * phase + n] = (
                zf[n * HALF : (n + 1) * HALF, :].astype(BF16).reshape(NS, 16, 128)
            )
            space_start(2 * phase + n)

    def mix_channels(src, kron, with_bias):
        @pl.loop(0, N1 // 16)
        def _(step):
            cut = pl.ds(pl.multiple_of(step * 16, 16), 16)
            right = jnp.concatenate(
                [src[n, :, :, cut, :].reshape(C * 16, N3) for n in range(ROWS)], axis=1
            )
            mixed = dot(kron[...], right)
            for n in range(ROWS):
                value = mixed[:, n * N3 : (n + 1) * N3].reshape(C, 16, N3)
                if with_bias:
                    value = jnp.concatenate([value[c : c + 1] + bias_ref[c] for c in range(C)], axis=0)
                skip_v[n, :, :, cut, :] = value.astype(BF16).reshape(CG, CQ, 16, N3)

    spread_rows = (rows((C * 16, C)) // 16 == lanes((C * 16, C))).astype(F32)
    spread_half = spread_rows.astype(BF16)

    def build_kron(base, kron):
        expanded = dot(spread_half, base).astype(BF16)
        for block in range(4):
            cut = slice(block * 256, (block + 1) * 256)
            full = dot_nt(expanded[cut], spread_half)
            same = (rows((256, 1024)) & 15) == (lanes((256, 1024)) & 15)
            kron[cut, :] = jnp.where(same, full, 0.0).astype(BF16)

    three_copy.wait()
    one_copy.wait()
    for n in range(ROWS):
        x_copies[n].wait()
        forward_row(x_ref, n, n)
    pl.semaphore_wait(barrier, NS - 1 + NB - 1)
    space_start(0, 1)

    for copy in small_copies:
        copy.wait()
    side = (2 * K2, 2 * K2)

    def permutation(index, other):
        position = index & (K2 - 1)
        target = index
        for slot in range(L2):
            target = jnp.where(position == slot, index - position + owner_ref[slot], target)
        return (target == other).astype(F32)

    perm = permutation(rows(side), lanes(side))
    perm_t = permutation(lanes(side), rows(side))
    perm_half = perm.astype(BF16)
    two = dot(perm_half, two_ref[...]).astype(BF16)
    two_t = dot_nt(two_t_ref[...], perm_half).astype(BF16)
    second = dot_nt(perm[:K2, :K2], second_ref[...], HIGH)
    second_l = dot(second, spread_ref[0], HIGH)
    third_l = dot(third_ref[...], spread_ref[0], HIGH)
    own = (lanes((8, K1)) == me_s).astype(F32)
    first_l = (
        dot(dot_nt(own, first_ref[0], HIGH), spread_ref[1], HIGH)
        + dot(dot_nt(own, first_ref[1], HIGH), spread_ref[2], HIGH)
    )[0:1]
    for k in range(K3):
        ph[k * K2 : (k + 1) * K2, :] = first_l * (second_l * third_l[k : k + 1])
    hot = dot(perm_half[:L2, :L2], hot_ref[0].astype(F32).astype(BF16)).astype(BF16)
    spread_hot = dot(hot, select_ref[...])
    for k in range(K3):
        maskf[k] = spread_hot[:, k * 128 : (k + 1) * 128]

    def expand(factor, top, bottom, width):
        pieces = [
            dot_tn(factor, pat_ref[:, start * 128 : start * 128 + width]) for start in (top, bottom)
        ]
        return jnp.concatenate(pieces, axis=0).astype(BF16)

    fin_all = expand(fin_ref[...], 0, 2, 256)
    fin_b = fin_all[:, 128:]
    fout_b = expand(fout_ref[...], 1, 3, 128)
    fout_c = expand(fout_ref[...], 4, 5, 128)

    build_kron(skip_ref[...].astype(F32).T.astype(BF16), kron_v)
    mix_channels(x_ref, kron_v, True)
    build_kron(skip_ref[...], kron_back_v)

    spectrum = modes_in(0, two)
    for k in range(K3):
        sm[k * K2 : (k + 1) * K2, :] = spectrum[k]

    def slots_out(dst, phase, index, owner):
        for slot in range(SLOTS):
            dst[phase, index, slot * K3 : (slot + 1) * K3, :] = sm[
                pl.ds(owner * SLOTS + slot, K3, stride=K2), :
            ].astype(BF16)

    def slots_in(phase):
        bz[...] = brecv[phase].reshape(NB * 32, 128).astype(F32)
        for slot in range(L2):
            sm[pl.ds(slot, K3, stride=K2), :] = bz[slot * K3 : (slot + 1) * K3, :]

    batch_start(0, slots_out)
    s16[...] = sm[...].astype(BF16)
    coef = dot(s16[...], fin_all)
    coef_b[...] = coef[:, 128:]
    prod_v[...] = (coef[:, :128] * ph[...]).astype(BF16)
    fac_v[...] = dot_nt(prod_v[...], fout_b)
    w_copy.wait()
    batch_wait(0)
    xs[...] = brecv[0].reshape(NB * 32, 128).astype(F32)
    sign = jnp.where(lanes((8, 128)) < 64, -1.0, 1.0)
    for index in range(SLOTS * K3):
        slot, k = divmod(index, K3)
        value = xs[pl.ds(index, NB, stride=32), :]
        left = jnp.concatenate([value, pltpu.roll(value, 64, 1)], axis=0).astype(BF16)
        lefts_v[index] = left
        both = dot(left[:, :C], w_v[slot, k])
        bz[pl.ds(index, NB, stride=32), :] = both[:8] + sign * pltpu.roll(both[8:], 64, 1)
    bsend[1] = bz[...].astype(BF16).reshape(NB, 32, 128)
    batch_start(1)
    batch_wait(1)
    slots_in(1)
    out_spec = []
    for k in range(K3):
        low = jnp.where(
            maskf[k] > 0.0, sm[k * K2 : k * K2 + L2, :], fac_v[k * K2 : k * K2 + L2, :]
        )
        out_spec.append(jnp.concatenate([low, fac_v[k * K2 + L2 : (k + 1) * K2, :]], axis=0))
    modes_out(out_spec, two_t, 1)
    cot_copy.wait()

    for n in range(ROWS):
        space_wait(2 + n)
        backward_row(rbuf[2 + n], zf.at[pl.ds(n * HALF, HALF)], left_v, one_t_ref[...])

        def activate(q, field):
            v = field + skip_v[n, :, q].astype(F32)
            square = v * v
            k0 = math.sqrt(2.0 / math.pi)
            gate = 0.5 * jnp.tanh(v * (k0 + (k0 * 0.044715) * square)) + 0.5
            active = v * gate
            out_v[n, :, q] = active.astype(BF16)
            slope = gate + active * (1.0 - gate) * (2.0 * k0 + (6.0 * k0 * 0.044715) * square)
            made = (cot_v[n, :, q].astype(F32) * slope).astype(BF16)
            gp_v[n, :, q] = made
            return made

        def gather(column, pair):
            total_v[...] += dot(pair, three_ref[pl.ds(column, 256), :])

        total_v[...] = jnp.zeros_like(total_v)
        each_pair(left_v, three_t_ref, activate, gather)
        fill_row(total_v[...], n, 4 + n)
        space_start(4 + n)
    out_copy = pltpu.make_async_copy(out_v, out_hbm, out_sem.at[0])
    out_copy.start()

    same = ((rows((16, 256)) & 15) == (lanes((16, 256)) & 15)).astype(F32)
    ones = jnp.ones((16, ROWS * 4 * N3), BF16)

    def cut_channels(src, start):
        return jnp.concatenate(
            [
                src[n, pl.ds(start * 2, 2), :, b * 16 : (b + 1) * 16, :].reshape(256, N3)
                for n in range(ROWS)
                for b in range(N1 // 16)
            ],
            axis=1,
        )

    for column in range(4):
        grads = cut_channels(gp_v, column)
        here = slice(column * 256, (column + 1) * 256)
        sgs[C : C + 16, here] = dot_nt(ones, grads)

        @pl.loop(0, 4)
        def _(block):
            full = dot_nt(cut_channels(x_ref, block), grads).reshape(16, 16, 256)
            sgs[pl.ds(pl.multiple_of(block * 16, 16), 16), here] = jnp.sum(full * same[None], axis=1)

    skip_grad = dot(sgs[...], spread_rows, HIGH)

    grad_spec = modes_in(2, two)
    for k in range(K3):
        sm[k * K2 : k * K2 + L2, :] = grad_spec[k][:L2] * maskf[k]
        fac_v[k * K2 : (k + 1) * K2, :] = grad_spec[k]
    batch_start(2, slots_out)
    cold = []
    for k in range(K3):
        low = fac_v[k * K2 : k * K2 + L2, :] * (1.0 - maskf[k])
        high = fac_v[k * K2 + L2 : (k + 1) * K2, :]
        cold.append(jnp.concatenate([low, high], axis=0).astype(BF16))
    cold = jnp.concatenate(cold, axis=0)
    back = dot(cold, fout_c)
    prod_back = (back * ph[...]).astype(BF16)
    fac_v[...] = dot_nt(prod_back, fin_b)
    in_full = dot_tn(s16[...], prod_back)
    out_full = dot_tn(cold, prod_v[...])
    back = back * coef_b[...]
    first_sum = jnp.zeros((K2, 128), F32)
    second_sum = jnp.zeros((K2, 128), F32)
    third_rows = []
    for k in range(K3):
        term = back[k * K2 : (k + 1) * K2]
        by_third = term * third_l[k : k + 1]
        first_sum = first_sum + by_third * second_l
        second_sum = second_sum + by_third * first_l
        third_rows.append(jnp.sum(term * first_l * second_l, axis=0, keepdims=True))
    first_row = jnp.sum(first_sum, axis=0, keepdims=True)
    third_sum = jnp.concatenate(third_rows, axis=0)

    def folded(full):
        pairs = full + left_by(full, 32)
        return pairs[:C] + left_by(pairs[C:], 16)

    shape = (C, 128)
    lane, row = lanes(shape), rows(shape)

    def below(value):
        return jnp.concatenate([value, jnp.zeros((C - value.shape[0], 128), F32)], axis=0)

    def fold_all(value):
        pairs = value + left_by(value, 16)
        return pairs + left_by(pairs, 32)

    second_part = dot(perm_t[:K2, :K2], fold_all(second_sum), HIGH)
    third_part = fold_all(third_sum)
    first_part = first_row + left_by(first_row, 16)
    middle = jnp.concatenate([second_part, third_part, jnp.zeros((16, 128), F32)], axis=0)
    zero64 = jnp.zeros((C, 64), F32)
    wide = jnp.concatenate([skip_grad[:C], zero64], axis=1)
    bias_row = jnp.concatenate([skip_grad[C : C + 1], zero64[:1]], axis=1)
    packed = jnp.where(lane < 64, wide, 0.0)
    packed = jnp.where((lane >= 64) & (lane < 80), pltpu.roll(folded(in_full), 64, 1), packed)
    packed = jnp.where((lane >= 80) & (lane < 96), pltpu.roll(folded(out_full), 80, 1), packed)
    inside = (lane >= 96) & (lane < 112)
    packed = jnp.where(inside, pltpu.roll(middle, 96, 1), packed)
    for piece in range(4):
        moved = pltpu.roll(bias_row, 96 - 16 * piece, 1)
        packed = jnp.where(inside & (row == 48 + piece), moved, packed)
    last = lane >= 112
    packed = jnp.where(last & (row == me_s), pltpu.roll(first_part, 112, 1), packed)
    packed = jnp.where(last & (row == me_s + 32), pltpu.roll(first_part, 80, 1), packed)
    pk[...] = (packed * GRAD_SCALE).reshape(NB, 8, 128)

    def send(src, dst, step, to):
        pltpu.make_async_remote_copy(
            src_ref=src,
            dst_ref=dst,
            send_sem=rsend.at[step],
            recv_sem=rrecv.at[step],
            device_id=to,
            device_id_type=MESH,
        ).start()

    near = (me_s // 8) * 2 + lax.rem(me_s, 2)
    far = lax.rem(me_s // 2, 4)

    @pl.loop(1, NB)
    def _(d):
        peer = lax.rem(me_b + d, NB)
        send(pk.at[peer], r_batch.at[me_b], 0, {"batch": peer})

    r_batch[me_b] = pk[me_b]

    batch_wait(2)
    bz[...] = brecv[2].reshape(NB * 32, 128).astype(F32)
    for index in range(SLOTS * K3):
        slot, k = divmod(index, K3)
        grad = bz[pl.ds(index, NB, stride=32), :]
        grads = jnp.concatenate([grad, -sign * pltpu.roll(grad, 64, 1)], axis=0).astype(BF16)
        grads_v[index] = grads
        weights = w_v[slot, k]
        both = dot_nt(grads, jnp.concatenate([weights, weights], axis=0))
        bz[pl.ds(index, NB, stride=32), :] = jnp.where(sign < 0.0, both[:8], both[8:])
    bsend[3] = bz[...].astype(BF16).reshape(NB, 32, 128)
    batch_start(3)

    drain(r_batch.at[pl.ds(0, NB - 1)], rrecv.at[0])
    part_near[...] = jnp.sum(r_batch[...], axis=0)

    @pl.loop(1, 8)
    def _(d):
        slot = lax.rem(near + d, 8)
        peer = (slot // 2) * 8 + far * 2 + lax.rem(slot, 2)
        send(part_near, r_near.at[near], 1, {"space": peer})

    r_near[near] = part_near[...]

    mix_channels(gp_v, kron_back_v, False)
    skip_copy = pltpu.make_async_copy(skip_v, skip_out_hbm, out_sem.at[2])
    skip_copy.start()

    batch_wait(3)
    slots_in(3)
    grad_spectrum = []
    for k in range(K3):
        low = fac_v[k * K2 : k * K2 + L2, :] + sm[k * K2 : k * K2 + L2, :]
        grad_spectrum.append(
            jnp.concatenate([low, fac_v[k * K2 + L2 : (k + 1) * K2, :]], axis=0)
        )
    modes_out(grad_spectrum, two_t, 3)


    drain(r_near.at[pl.ds(0, 7)], rrecv.at[1])
    part_far[...] = jnp.sum(r_near[...], axis=0)

    @pl.loop(1, 4)
    def _(d):
        slot = lax.rem(far + d, 4)
        peer = (near // 2) * 8 + slot * 2 + lax.rem(near, 2)
        send(part_far, r_far.at[far], 2, {"space": peer})

    r_far[far] = part_far[...]

    for index in range(SLOTS * K3):
        slot, k = divmod(index, K3)
        dg_v[slot, k] = dot_tn(lefts_v[index], grads_v[index])[:C]
    dg_copy = pltpu.make_async_copy(dg_v, dg_hbm.at[0], out_sem.at[1])
    dg_copy.start()

    drain(r_far.at[pl.ds(0, 3)], rrecv.at[2])
    part_all[...] = jnp.sum(r_far[...], axis=0)

    @pl.loop(1, NB)
    def _(d):
        send(part_all, r_all.at[me_b], 3, {"batch": lax.rem(me_b + d, NB)})

    r_all[me_b] = part_all[...]
    space_wait(6)
    backward_row(rbuf[6], zf.at[pl.ds(0, HALF)], left_v, one_t_ref[...])

    def finish(q, field):
        ig_v[:, q] = (field + skip_v[0, :, q].astype(F32)).astype(BF16)

    each_pair(left_v, three_t_ref, finish)
    ig_copy = pltpu.make_async_copy(ig_v, ig_hbm, out_sem.at[3])
    ig_copy.start()

    space_wait(7)
    blocks_copy = pltpu.make_async_copy(rbuf.at[7], blocks_hbm, out_sem.at[4])
    blocks_copy.start()
    drain(r_all.at[pl.ds(0, NB - 1)], rrecv.at[3])
    red_copy = pltpu.make_async_copy(r_all, red_hbm, out_sem.at[5])
    red_copy.start()
    for index in range(8):
        drain(sbuf.at[index, pl.ds(0, NS - 1)], ssend.at[index])
    for phase in range(4):
        drain(bsend.at[phase, pl.ds(0, NB - 1)], bssem.at[phase])
    drain(pk.at[pl.ds(0, NB - 1)], rsend.at[0])
    drain(r_near.at[pl.ds(0, 7)], rsend.at[1])
    drain(r_far.at[pl.ds(0, 3)], rsend.at[2])
    drain(r_all.at[pl.ds(0, NB - 1)], rsend.at[3])
    for started in (out_copy, dg_copy, skip_copy, ig_copy, blocks_copy, red_copy):
        started.wait()


def finish_kernel(
    blocks_hbm,
    packed_hbm,
    one_t_hbm,
    three_t_hbm,
    skip_hbm,
    out_in,
    dg_in,
    ig_in,
    out_hbm,
    ig_hbm,
    dg_hbm,
    fin_hbm,
    fout_hbm,
    first_hbm,
    second_hbm,
    third_hbm,
    mix_hbm,
    bias_hbm,
    blocks_v,
    packed_v,
    one_t_v,
    three_t_v,
    skip_v,
    out_v,
    dg_v,
    ig_v,
    left_v,
    zf,
    fin_v,
    fout_v,
    first_v,
    second_v,
    third_v,
    mix_v,
    bias_v,
    sem,
):
    def copy(src, dst, index):
        started = pltpu.make_async_copy(src, dst, sem.at[index])
        started.start()
        return started

    arriving = [
        copy(src, dst, index)
        for index, (src, dst) in enumerate(
            (
                (blocks_hbm, blocks_v),
                (one_t_hbm, one_t_v),
                (three_t_hbm, three_t_v),
                (skip_hbm.at[1], skip_v),
                (packed_hbm, packed_v),
                (out_in, out_v),
                (ig_in, ig_v.at[0]),
                (dg_in, dg_v),
            )
        )
    ]
    waits = []

    def pass_on(index, src, dst):
        arriving[index].wait()
        waits.append(copy(src, dst, 8 + index))

    for index in range(4):
        arriving[index].wait()
    backward_row(blocks_v[...], zf, left_v, one_t_v[...])
    arriving[4].wait()
    packed = packed_v[...].reshape(C, 128)
    turned = packed.T
    fin_v[...] = turned[64:80]
    fout_v[...] = turned[80:96]
    second_v[...] = turned[96:112, :K2]
    first_v[0] = turned[112:, :K1]
    first_v[1] = turned[112:, K1:]
    third_v[...] = left_by(packed, 96)[K2 : K2 + K3, :R]
    mix_v[...] = packed[:, :C]
    bias = jnp.zeros((1, 128), F32)
    lane = lanes((1, 128))
    for piece in range(4):
        moved = pltpu.roll(packed[48 + piece : 49 + piece], (32 + 16 * piece) % 128, 1)
        bias = jnp.where((lane >= 16 * piece) & (lane < 16 * (piece + 1)), moved, bias)
    bias_v[...] = bias[:, :C]
    small = (
        (fin_v, fin_hbm),
        (fout_v, fout_hbm),
        (first_v, first_hbm),
        (second_v, second_hbm),
        (third_v, third_hbm),
        (mix_v, mix_hbm),
        (bias_v, bias_hbm),
    )
    waits += [copy(src, dst, 17 + index) for index, (src, dst) in enumerate(small)]
    for pair in range(CQ // 2):
        field = dot(left_v[...], three_t_v[:, pair * 256 : (pair + 1) * 256])
        for half in range(2):
            q = pair * 2 + half
            value = field[:, half * 128 : (half + 1) * 128].reshape(CG, N1, N3)
            ig_v[1, :, q] = (value + skip_v[:, q].astype(F32)).astype(BF16)
        cut = (1, slice(None), pl.ds(pair * 2, 2))
        waits.append(copy(ig_v.at[cut], ig_hbm.at[cut], 24 + pair))
        if pair == 0:
            pass_on(5, out_v, out_hbm)
        if pair == 1:
            pass_on(6, ig_v.at[0], ig_hbm.at[0])
        if pair == 2:
            pass_on(7, dg_v, dg_hbm)
    for started in waits:
        started.wait()


def local(
    inputs,
    cotangent,
    dense_weights,
    owner_table,
    hot_mask,
    skip_weight,
    bias_vector,
    input_factor,
    output_factor,
    first_factor,
    second_factor,
    third_factor,
):
    field = (ROWS, CG, CQ, N1, N3)
    three, three_t, one, one_t, two, two_t, patterns, spread, select = [
        jnp.asarray(table) for table in build_tables()
    ]
    smem = pl.BlockSpec(memory_space=pltpu.SMEM)
    hbm = pl.BlockSpec(memory_space=pltpu.HBM)
    dense = (SLOTS, K3, C, 2 * C)
    operands = (
        inputs.reshape(field),
        three,
        one,
        hot_mask,
        skip_weight,
        input_factor.T,
        output_factor.T,
        jnp.swapaxes(first_factor, 1, 2),
        second_factor.T,
        third_factor,
        two,
        two_t,
        patterns,
        spread,
        select,
        one_t,
        three_t,
        cotangent.reshape(field),
    )
    blocks = (NS, 16, 128)
    row = field[1:]
    output, skip_part, grad_row, dense_grad, received, packed = pl.pallas_call(
        kernel,
        out_shape=(
            jax.ShapeDtypeStruct(field, BF16),
            jax.ShapeDtypeStruct(field, BF16),
            jax.ShapeDtypeStruct(row, BF16),
            jax.ShapeDtypeStruct((1,) + dense, F32),
            jax.ShapeDtypeStruct(blocks, BF16),
            jax.ShapeDtypeStruct((NB, 8, 128), F32),
        ),
        in_specs=[smem, smem] + [hbm] * 19,
        out_specs=(hbm,) * 6,
        scratch_shapes=[pltpu.VMEM(value.shape, value.dtype) for value in operands]
        + [
            pltpu.VMEM(dense, BF16),
            pltpu.VMEM(field, BF16),
            pltpu.VMEM(field, BF16),
            pltpu.VMEM(dense, F32),
            pltpu.VMEM(field, BF16),
            pltpu.VMEM(row, BF16),
            pltpu.VMEM((C * 16, C * 16), BF16),
            pltpu.VMEM((C * 16, C * 16), BF16),
            pltpu.VMEM((CG * N1, 256), BF16),
            pltpu.VMEM((CG * N1, 256), F32),
            pltpu.VMEM((ROWS * HALF, 128), F32),
            pltpu.VMEM((8,) + blocks, BF16),
            pltpu.VMEM((8,) + blocks, BF16),
            pltpu.VMEM((4, NB, 32, 128), BF16),
            pltpu.VMEM((4, NB, 32, 128), BF16),
            pltpu.VMEM((K3 * K2, 128), F32),
            pltpu.VMEM((K3 * K2, 128), BF16),
            pltpu.VMEM((K3, L2, 128), F32),
            pltpu.VMEM((K3 * K2, 128), F32),
            pltpu.VMEM((K3 * K2, 128), F32),
            pltpu.VMEM((K3 * K2, 128), BF16),
            pltpu.VMEM((K3 * K2, 128), F32),
            pltpu.VMEM((NB * 32, 128), F32),
            pltpu.VMEM((NB * 32, 128), F32),
            pltpu.VMEM((SLOTS * K3, 16, 128), BF16),
            pltpu.VMEM((SLOTS * K3, 16, 128), BF16),
            pltpu.VMEM((C + 16, C * 16), F32),
            pltpu.VMEM((NB, 8, 128), F32),
            pltpu.VMEM((NB, 8, 128), F32),
            pltpu.VMEM((8, 8, 128), F32),
            pltpu.VMEM((4, 8, 128), F32),
            pltpu.VMEM((NB, 8, 128), F32),
            pltpu.VMEM((8, 128), F32),
            pltpu.VMEM((8, 128), F32),
            pltpu.VMEM((8, 128), F32),
            pltpu.SemaphoreType.DMA((20,)),
            pltpu.SemaphoreType.DMA((6,)),
            pltpu.SemaphoreType.DMA((8,)),
            pltpu.SemaphoreType.DMA((8,)),
            pltpu.SemaphoreType.DMA((4,)),
            pltpu.SemaphoreType.DMA((4,)),
            pltpu.SemaphoreType.DMA((4,)),
            pltpu.SemaphoreType.DMA((4,)),
        ],
        compiler_params=pltpu.CompilerParams(
            collective_id=0, has_side_effects=True, vmem_limit_bytes=64 * 2**20
        ),
    )(owner_table, bias_vector, *operands, dense_weights)
    results = (
        (field, BF16),
        (field, BF16),
        ((1,) + dense, F32),
        ((R, C), F32),
        ((R, C), F32),
        ((2, R, K1), F32),
        ((R, K2), F32),
        ((K3, R), F32),
        ((C, C), F32),
        ((1, C), F32),
    )
    output, input_grad, dense_grad, in_t, out_t, first_t, second_t, third, skip, bias = pl.pallas_call(
        finish_kernel,
        out_shape=tuple(jax.ShapeDtypeStruct(*result) for result in results),
        in_specs=[hbm] * 8,
        out_specs=(hbm,) * len(results),
        scratch_shapes=[
            pltpu.VMEM(blocks, BF16),
            pltpu.VMEM((NB, 8, 128), F32),
            pltpu.VMEM(one_t.shape, BF16),
            pltpu.VMEM(three_t.shape, BF16),
            pltpu.VMEM(row, BF16),
            pltpu.VMEM(field, BF16),
            pltpu.VMEM((1,) + dense, F32),
            pltpu.VMEM(field, BF16),
            pltpu.VMEM((CG * N1, 256), BF16),
            pltpu.VMEM((HALF, 128), F32),
        ]
        + [pltpu.VMEM(*result) for result in results[3:]]
        + [pltpu.SemaphoreType.DMA((28,))],
        compiler_params=pltpu.CompilerParams(vmem_limit_bytes=64 * 2**20),
    )(received, packed, one_t, three_t, skip_part, output, dense_grad, grad_row)
    return (
        output.reshape(inputs.shape),
        input_grad.reshape(inputs.shape),
        dense_grad,
        in_t.T,
        out_t.T,
        jnp.swapaxes(first_t, 1, 2),
        second_t.T,
        third,
        skip,
        bias.reshape(C),
    )


def solution(mesh):
    field = P("batch", "space", None, None, None)
    dense = P("space", "batch", None, None, None)
    whole = P()
    return jax.shard_map(
        local,
        mesh=mesh,
        in_specs=(field, field, dense, whole, P("space", None, None)) + (whole,) * 7,
        out_specs=(field, field, dense) + (whole,) * 7,
        check_vma=False,
    )
```

```python
import math

import jax
import jax.numpy as jnp
import ml_dtypes
import numpy as np
from jax import lax
from jax.experimental import pallas as pl
from jax.experimental.pallas import tpu as pltpu
from jax.sharding import PartitionSpec as P

MESH = pl.DeviceIdType.MESH
F32 = jnp.float32
BF16 = jnp.bfloat16
HIGH = lax.Precision.HIGHEST

C = 64
N1 = 64
N2 = 64
N3 = 128
K1 = 32
K2 = 32
K3 = 16
L2 = 16
R = 16
SAMPLES = 8
NS = 32
NB = 8
ROWS = N2 // NS
CG = 8
CQ = 8
SLOTS = L2 // NB
HALF = NS * 16
GRAD_SCALE = float(SAMPLES * N1 * N2 * N3) ** (-0.5)


def rounded(values):
    return np.asarray(values, np.float32).astype(ml_dtypes.bfloat16)


def twiddles(frequency, length):
    index = np.mod(frequency[:, None] * np.arange(length)[None, :], length)
    radians = index.astype(np.float32) * np.float32(2.0 * math.pi / length)
    return np.cos(radians), np.sin(radians)


def retained(amount):
    position = np.arange(amount)
    return np.where(position % 2 == 0, position // 2, -((position + 1) // 2))


def build_tables():
    factor = float(N1 * N2 * N3 * K1 * K2 * K3) ** (-0.25)
    cos1, sin1 = twiddles(retained(K1), N1)
    t0 = np.float32(factor) * cos1
    t1 = np.float32(-factor) * sin1
    one = np.block([[t0, -t1], [t1, t0]])
    cos2, sin2 = twiddles(retained(K2), N2)
    two = np.zeros((2, K2, N2, 2), np.float32)
    two[0, :, :, 0] = cos2
    two[0, :, :, 1] = sin2
    two[1, :, :, 0] = -sin2
    two[1, :, :, 1] = cos2
    two = two.reshape(2, K2, NS, ROWS, 2).transpose(0, 1, 3, 2, 4).reshape(2 * K2, 2 * N2)
    cos3, sin3 = twiddles(np.arange(K3), N3)
    three = np.zeros((CQ, N3, 2, K3, CQ), np.float32)
    for q in range(CQ):
        three[q, :, 0, :, q] = cos3.T
        three[q, :, 1, :, q] = -sin3.T
    three = three.reshape(CQ * N3, 2 * K3 * CQ)
    eye = np.eye(R, dtype=np.float32)

    def tiled(signs):
        return np.concatenate([sign * eye for sign in signs] + [np.zeros((R, 64), np.float32)], axis=1)

    patterns = np.concatenate(
        [
            tiled((1, 0, 0, 1)),
            tiled((1, 0, 1, 0)),
            tiled((0, 1, -1, 0)),
            tiled((0, 1, 0, 1)),
            tiled((1, 0, 0, -1)),
            tiled((0, 1, 1, 0)),
        ],
        axis=1,
    )
    spread = np.stack([tiled((1, 1, 1, 1)), tiled((1, 1, 0, 0)), tiled((0, 0, 1, 1))])
    select = np.zeros((K3, K3, 128), np.float32)
    for k in range(K3):
        select[k, k] = 1.0
    return (
        rounded(three),
        rounded(three.T),
        rounded(one),
        rounded(one.T),
        rounded(two),
        rounded(two.T),
        rounded(patterns),
        spread.astype(np.float32),
        rounded(select.reshape(K3, K3 * 128)),
    )


def dot(a, b, precision=None):
    return jnp.dot(a, b, preferred_element_type=F32, precision=precision)


def dot_nt(a, b, precision=None):
    return lax.dot_general(
        a, b, (((1,), (1,)), ((), ())), preferred_element_type=F32, precision=precision
    )


def dot_tn(a, b):
    return lax.dot_general(a, b, (((0,), (0,)), ((), ())), preferred_element_type=F32)


def lanes(shape):
    return lax.broadcasted_iota(jnp.int32, shape, len(shape) - 1)


def rows(shape):
    return lax.broadcasted_iota(jnp.int32, shape, 0)


def swap_groups(parts):
    parts = list(parts)
    group = lanes(parts[0].shape) // CQ
    for bit in (1, 2, 4, 8):
        low = (group & bit) == 0
        for a in range(16):
            if a & bit:
                continue
            first, second = parts[a], parts[a + bit]
            parts[a] = jnp.where(low, first, pltpu.roll(second, 8 * bit, 1))
            parts[a + bit] = jnp.where(low, pltpu.roll(first, 128 - 8 * bit, 1), second)
    return parts


def left_by(value, amount):
    return pltpu.roll(value, 128 - amount, 1)


def drain(block, sem):
    pltpu.make_async_copy(block, block, sem).wait()


def backward_row(blocks, zf, left_v, one_t):
    zf[...] = blocks.reshape(HALF, 128).astype(F32)
    block = jnp.concatenate(
        [
            jnp.concatenate(
                [zf[pl.ds(part * 8 + g, K1, stride=16), :].astype(BF16) for part in range(2)],
                axis=0,
            )
            for g in range(CG)
        ],
        axis=1,
    )
    field = dot(one_t, block).astype(BF16)
    for g in range(CG):
        left_v[g * N1 : (g + 1) * N1, :128] = field[:N1, g * 128 : (g + 1) * 128]
        left_v[g * N1 : (g + 1) * N1, 128:] = field[N1:, g * 128 : (g + 1) * 128]


def each_pair(left_v, three_t, body, after=None):
    @pl.loop(0, CQ // 2, unroll=4)
    def _(pair):
        column = pl.multiple_of(pair * 256, 256)
        field = dot(left_v[...], three_t[:, pl.ds(column, 256)])
        made = [
            body(pair * 2 + half, field[:, half * 128 : (half + 1) * 128].reshape(CG, N1, N3))
            for half in range(2)
        ]
        if after is not None:
            after(column, jnp.concatenate([v.reshape(CG * N1, N3) for v in made], axis=1))


def kernel(
    owner_ref,
    bias_ref,
    x_hbm,
    three_hbm,
    one_hbm,
    hot_hbm,
    skip_hbm,
    fin_hbm,
    fout_hbm,
    first_hbm,
    second_hbm,
    third_hbm,
    two_hbm,
    two_t_hbm,
    pat_hbm,
    spread_hbm,
    select_hbm,
    one_t_hbm,
    three_t_hbm,
    cot_hbm,
    w_hbm,
    out_hbm,
    skip_out_hbm,
    ig_hbm,
    dg_hbm,
    blocks_hbm,
    red_hbm,
    x_ref,
    three_ref,
    one_ref,
    hot_ref,
    skip_ref,
    fin_ref,
    fout_ref,
    first_ref,
    second_ref,
    third_ref,
    two_ref,
    two_t_ref,
    pat_ref,
    spread_ref,
    select_ref,
    one_t_ref,
    three_t_ref,
    cot_v,
    w_v,
    out_v,
    gp_v,
    dg_v,
    skip_v,
    ig_v,
    kron_v,
    kron_back_v,
    left_v,
    total_v,
    zf,
    sbuf,
    rbuf,
    bsend,
    brecv,
    sm,
    s16,
    maskf,
    ph,
    coef_b,
    prod_v,
    fac_v,
    xs,
    bz,
    lefts_v,
    grads_v,
    sgs,
    pk,
    r_batch,
    r_near,
    r_far,
    r_all,
    part_near,
    part_far,
    part_all,
    in_sem,
    out_sem,
    ssend,
    srecv,
    bssem,
    brsem,
    rsend,
    rrecv,
):
    me_s = lax.axis_index("space")
    me_b = lax.axis_index("batch")
    barrier = pltpu.get_barrier_semaphore()

    def each_space_peer(body):
        for step in (2, 1, 3, 0):

            @pl.loop(0 if step else 1, 8)
            def _(d):
                body(
                    lax.rem(me_s // 8 + d // 2, 4) * 8
                    + lax.rem(me_s // 2 + step, 4) * 2
                    + lax.rem(me_s + d, 2)
                )

    def greet(peer):
        pl.semaphore_signal(barrier, inc=1, device_id={"space": peer}, device_id_type=MESH)

    each_space_peer(greet)

    def each_batch_peer(body):
        for z_step, y_step in ((1, 2), (1, 1), (1, 3), (0, 2), (1, 0), (0, 1), (0, 3)):
            body(lax.rem(me_b // 4 + z_step, 2) * 4 + lax.rem(me_b + y_step, 4))

    def greet_batch(peer):
        pl.semaphore_signal(barrier, inc=1, device_id={"batch": peer}, device_id_type=MESH)

    each_batch_peer(greet_batch)

    def fetch(src, dst, index):
        copy = pltpu.make_async_copy(src, dst, in_sem.at[index])
        copy.start()
        return copy

    x_copies = [fetch(x_hbm.at[0], x_ref.at[0], 0)]
    three_copy = fetch(three_hbm, three_ref, 2)
    one_copy = fetch(one_hbm, one_ref, 3)
    x_copies.append(fetch(x_hbm.at[1], x_ref.at[1], 1))
    small_copies = [
        fetch(src, dst, 4 + index)
        for index, (src, dst) in enumerate(
            (
                (hot_hbm, hot_ref),
                (skip_hbm, skip_ref),
                (fin_hbm, fin_ref),
                (fout_hbm, fout_ref),
                (first_hbm, first_ref),
                (second_hbm, second_ref),
                (third_hbm, third_ref),
                (two_hbm, two_ref),
                (two_t_hbm, two_t_ref),
                (pat_hbm, pat_ref),
                (spread_hbm, spread_ref),
                (select_hbm, select_ref),
                (one_t_hbm, one_t_ref),
                (three_t_hbm, three_t_ref),
            )
        )
    ]
    cot_copy = fetch(cot_hbm, cot_v, 18)
    w_copy = fetch(w_hbm.at[0], w_v, 19)

    def space_start(*indices):
        def send_block(peer):
            for index in indices:
                pltpu.make_async_remote_copy(
                    src_ref=sbuf.at[index, peer],
                    dst_ref=rbuf.at[index, me_s],
                    send_sem=ssend.at[index],
                    recv_sem=srecv.at[index],
                    device_id={"space": peer},
                    device_id_type=MESH,
                ).start()

        each_space_peer(send_block)
        for index in indices:
            rbuf[index, me_s] = sbuf[index, me_s]

    def space_wait(index):
        drain(rbuf.at[index, pl.ds(0, NS - 1)], srecv.at[index])

    def batch_start(phase, fill=None):
        def send_block(peer):
            if fill is not None:
                fill(bsend, phase, peer, peer)
            pltpu.make_async_remote_copy(
                src_ref=bsend.at[phase, peer],
                dst_ref=brecv.at[phase, me_b],
                send_sem=bssem.at[phase],
                recv_sem=brsem.at[phase],
                device_id={"batch": peer},
                device_id_type=MESH,
            ).start()

        each_batch_peer(send_block)
        if fill is not None:
            fill(brecv, phase, me_b, me_b)
        else:
            brecv[phase, me_b] = bsend[phase, me_b]

    def batch_wait(phase):
        drain(brecv.at[phase, pl.ds(0, NB - 1)], brsem.at[phase])

    def forward_row(src, n, index):
        total = None
        for q in range(0, CQ, 2):
            pair = jnp.concatenate(
                [src[n, :, q].reshape(CG * N1, N3), src[n, :, q + 1].reshape(CG * N1, N3)], axis=1
            )
            term = dot(pair, three_ref[q * N3 : (q + 2) * N3, :])
            total = term if total is None else total + term
        fill_row(total, n, index)

    def fill_row(total, n, index):
        total = total.astype(BF16)
        right = jnp.concatenate(
            [
                jnp.concatenate(
                    [total[g * N1 : (g + 1) * N1, :128], total[g * N1 : (g + 1) * N1, 128:]], axis=0
                )
                for g in range(CG)
            ],
            axis=1,
        )
        modes = dot(one_ref[...], right)
        for g in range(CG):
            for part in range(2):
                zf[pl.ds(n * HALF + part * 8 + g, K1, stride=16), :] = modes[
                    part * K1 : (part + 1) * K1, g * 128 : (g + 1) * 128
                ]
        sbuf[index] = zf[n * HALF : (n + 1) * HALF, :].astype(BF16).reshape(NS, 16, 128)

    def modes_in(phase, table):
        for n in range(ROWS):
            space_wait(2 * phase + n)
            zf[n * HALF : (n + 1) * HALF, :] = rbuf[2 * phase + n].reshape(HALF, 128).astype(F32)
        cells = jnp.concatenate(
            [zf[pl.ds(g, 2 * N2, stride=8), :].astype(BF16) for g in range(CG)], axis=1
        )
        modes = dot(table, cells)
        parts = [
            modes[part * K2 : (part + 1) * K2, g * 128 : (g + 1) * 128]
            for part in range(2)
            for g in range(CG)
        ]
        return swap_groups(parts)

    def modes_out(by_frequency, table, phase):
        parts = swap_groups(by_frequency)
        spectrum = jnp.concatenate(
            [
                jnp.concatenate([parts[part * CG + g] for g in range(CG)], axis=1).astype(BF16)
                for part in range(2)
            ],
            axis=0,
        )
        for n in range(ROWS):
            cells = dot(table[n * N2 : (n + 1) * N2], spectrum)
            for g in range(CG):
                zf[pl.ds(n * HALF + g, N2, stride=8), :] = cells[:, g * 128 : (g + 1) * 128]
            sbuf[2 * phase + n] = (
                zf[n * HALF : (n + 1) * HALF, :].astype(BF16).reshape(NS, 16, 128)
            )
            space_start(2 * phase + n)

    def mix_channels(src, kron, with_bias):
        @pl.loop(0, N1 // 16)
        def _(step):
            cut = pl.ds(pl.multiple_of(step * 16, 16), 16)
            right = jnp.concatenate(
                [src[n, :, :, cut, :].reshape(C * 16, N3) for n in range(ROWS)], axis=1
            )
            mixed = dot(kron[...], right)
            for n in range(ROWS):
                value = mixed[:, n * N3 : (n + 1) * N3].reshape(C, 16, N3)
                if with_bias:
                    value = jnp.concatenate([value[c : c + 1] + bias_ref[c] for c in range(C)], axis=0)
                skip_v[n, :, :, cut, :] = value.astype(BF16).reshape(CG, CQ, 16, N3)

    spread_rows = (rows((C * 16, C)) // 16 == lanes((C * 16, C))).astype(F32)
    spread_half = spread_rows.astype(BF16)

    def build_kron(base, kron):
        expanded = dot(spread_half, base).astype(BF16)
        for block in range(4):
            cut = slice(block * 256, (block + 1) * 256)
            full = dot_nt(expanded[cut], spread_half)
            same = (rows((256, 1024)) & 15) == (lanes((256, 1024)) & 15)
            kron[cut, :] = jnp.where(same, full, 0.0).astype(BF16)

    three_copy.wait()
    one_copy.wait()
    for n in range(ROWS):
        x_copies[n].wait()
        forward_row(x_ref, n, n)
    pl.semaphore_wait(barrier, NS - 1 + NB - 1)
    space_start(0, 1)

    for copy in small_copies:
        copy.wait()
    side = (2 * K2, 2 * K2)

    def permutation(index, other):
        position = index & (K2 - 1)
        target = index
        for slot in range(L2):
            target = jnp.where(position == slot, index - position + owner_ref[slot], target)
        return (target == other).astype(F32)

    perm = permutation(rows(side), lanes(side))
    perm_t = permutation(lanes(side), rows(side))
    perm_half = perm.astype(BF16)
    two = dot(perm_half, two_ref[...]).astype(BF16)
    two_t = dot_nt(two_t_ref[...], perm_half).astype(BF16)
    second = dot_nt(perm[:K2, :K2], second_ref[...], HIGH)
    second_l = dot(second, spread_ref[0], HIGH)
    third_l = dot(third_ref[...], spread_ref[0], HIGH)
    own = (lanes((8, K1)) == me_s).astype(F32)
    first_l = (
        dot(dot_nt(own, first_ref[0], HIGH), spread_ref[1], HIGH)
        + dot(dot_nt(own, first_ref[1], HIGH), spread_ref[2], HIGH)
    )[0:1]
    for k in range(K3):
        ph[k * K2 : (k + 1) * K2, :] = first_l * (second_l * third_l[k : k + 1])
    hot = dot(perm_half[:L2, :L2], hot_ref[0].astype(F32).astype(BF16)).astype(BF16)
    spread_hot = dot(hot, select_ref[...])
    for k in range(K3):
        maskf[k] = spread_hot[:, k * 128 : (k + 1) * 128]

    def expand(factor, top, bottom, width):
        pieces = [
            dot_tn(factor, pat_ref[:, start * 128 : start * 128 + width]) for start in (top, bottom)
        ]
        return jnp.concatenate(pieces, axis=0).astype(BF16)

    fin_all = expand(fin_ref[...], 0, 2, 256)
    fin_b = fin_all[:, 128:]
    fout_b = expand(fout_ref[...], 1, 3, 128)
    fout_c = expand(fout_ref[...], 4, 5, 128)

    build_kron(skip_ref[...].astype(F32).T.astype(BF16), kron_v)
    mix_channels(x_ref, kron_v, True)
    build_kron(skip_ref[...], kron_back_v)

    spectrum = modes_in(0, two)
    for k in range(K3):
        sm[k * K2 : (k + 1) * K2, :] = spectrum[k]

    def slots_out(dst, phase, index, owner):
        for slot in range(SLOTS):
            dst[phase, index, slot * K3 : (slot + 1) * K3, :] = sm[
                pl.ds(owner * SLOTS + slot, K3, stride=K2), :
            ].astype(BF16)

    def returned(dst, phase, index, owner):
        dst[phase, index] = bz[pl.ds(pl.multiple_of(owner * 32, 32), 32), :].astype(BF16)

    def slots_in(phase):
        bz[...] = brecv[phase].reshape(NB * 32, 128).astype(F32)
        for slot in range(L2):
            sm[pl.ds(slot, K3, stride=K2), :] = bz[slot * K3 : (slot + 1) * K3, :]

    batch_start(0, slots_out)
    s16[...] = sm[...].astype(BF16)
    coef = dot(s16[...], fin_all)
    coef_b[...] = coef[:, 128:]
    prod_v[...] = (coef[:, :128] * ph[...]).astype(BF16)
    fac_v[...] = dot_nt(prod_v[...], fout_b)
    w_copy.wait()
    batch_wait(0)
    xs[...] = brecv[0].reshape(NB * 32, 128).astype(F32)
    sign = jnp.where(lanes((8, 128)) < 64, -1.0, 1.0)
    for index in range(SLOTS * K3):
        slot, k = divmod(index, K3)
        value = xs[pl.ds(index, NB, stride=32), :]
        left = jnp.concatenate([value, pltpu.roll(value, 64, 1)], axis=0).astype(BF16)
        lefts_v[index] = left
        both = dot(left[:, :C], w_v[slot, k])
        bz[pl.ds(index, NB, stride=32), :] = both[:8] + sign * pltpu.roll(both[8:], 64, 1)
    batch_start(1, returned)
    batch_wait(1)
    slots_in(1)
    out_spec = []
    for k in range(K3):
        low = jnp.where(
            maskf[k] > 0.0, sm[k * K2 : k * K2 + L2, :], fac_v[k * K2 : k * K2 + L2, :]
        )
        out_spec.append(jnp.concatenate([low, fac_v[k * K2 + L2 : (k + 1) * K2, :]], axis=0))
    modes_out(out_spec, two_t, 1)
    cot_copy.wait()

    for n in range(ROWS):
        space_wait(2 + n)
        backward_row(rbuf[2 + n], zf.at[pl.ds(n * HALF, HALF)], left_v, one_t_ref[...])

        def activate(q, field):
            v = field + skip_v[n, :, q].astype(F32)
            square = v * v
            k0 = math.sqrt(2.0 / math.pi)
            gate = 0.5 * jnp.tanh(v * (k0 + (k0 * 0.044715) * square)) + 0.5
            active = v * gate
            out_v[n, :, q] = active.astype(BF16)
            slope = gate + active * (1.0 - gate) * (2.0 * k0 + (6.0 * k0 * 0.044715) * square)
            made = (cot_v[n, :, q].astype(F32) * slope).astype(BF16)
            gp_v[n, :, q] = made
            return made

        def gather(column, pair):
            total_v[...] += dot(pair, three_ref[pl.ds(column, 256), :])

        total_v[...] = jnp.zeros_like(total_v)
        each_pair(left_v, three_t_ref, activate, gather)
        fill_row(total_v[...], n, 4 + n)
        space_start(4 + n)
    out_copy = pltpu.make_async_copy(out_v, out_hbm, out_sem.at[0])
    out_copy.start()

    same = ((rows((16, 256)) & 15) == (lanes((16, 256)) & 15)).astype(F32)
    ones = jnp.ones((16, ROWS * 4 * N3), BF16)

    def cut_channels(src, start):
        return jnp.concatenate(
            [
                src[n, pl.ds(start * 2, 2), :, b * 16 : (b + 1) * 16, :].reshape(256, N3)
                for n in range(ROWS)
                for b in range(N1 // 16)
            ],
            axis=1,
        )

    for column in range(4):
        grads = cut_channels(gp_v, column)
        here = slice(column * 256, (column + 1) * 256)
        sgs[C : C + 16, here] = dot_nt(ones, grads)

        @pl.loop(0, 4)
        def _(block):
            full = dot_nt(cut_channels(x_ref, block), grads).reshape(16, 16, 256)
            sgs[pl.ds(pl.multiple_of(block * 16, 16), 16), here] = jnp.sum(full * same[None], axis=1)

    skip_grad = dot(sgs[...], spread_rows, HIGH)

    grad_spec = modes_in(2, two)
    for k in range(K3):
        sm[k * K2 : k * K2 + L2, :] = grad_spec[k][:L2] * maskf[k]
        fac_v[k * K2 : (k + 1) * K2, :] = grad_spec[k]
    batch_start(2, slots_out)
    cold = []
    for k in range(K3):
        low = fac_v[k * K2 : k * K2 + L2, :] * (1.0 - maskf[k])
        high = fac_v[k * K2 + L2 : (k + 1) * K2, :]
        cold.append(jnp.concatenate([low, high], axis=0).astype(BF16))
    cold = jnp.concatenate(cold, axis=0)
    back = dot(cold, fout_c)
    prod_back = (back * ph[...]).astype(BF16)
    fac_v[...] = dot_nt(prod_back, fin_b)
    in_full = dot_tn(s16[...], prod_back)
    out_full = dot_tn(cold, prod_v[...])
    back = back * coef_b[...]
    first_sum = jnp.zeros((K2, 128), F32)
    second_sum = jnp.zeros((K2, 128), F32)
    third_rows = []
    for k in range(K3):
        term = back[k * K2 : (k + 1) * K2]
        by_third = term * third_l[k : k + 1]
        first_sum = first_sum + by_third * second_l
        second_sum = second_sum + by_third * first_l
        third_rows.append(jnp.sum(term * first_l * second_l, axis=0, keepdims=True))
    first_row = jnp.sum(first_sum, axis=0, keepdims=True)
    third_sum = jnp.concatenate(third_rows, axis=0)

    def folded(full):
        pairs = full + left_by(full, 32)
        return pairs[:C] + left_by(pairs[C:], 16)

    shape = (C, 128)
    lane, row = lanes(shape), rows(shape)

    def below(value):
        return jnp.concatenate([value, jnp.zeros((C - value.shape[0], 128), F32)], axis=0)

    def fold_all(value):
        pairs = value + left_by(value, 16)
        return pairs + left_by(pairs, 32)

    second_part = dot(perm_t[:K2, :K2], fold_all(second_sum), HIGH)
    third_part = fold_all(third_sum)
    first_part = first_row + left_by(first_row, 16)
    middle = jnp.concatenate([second_part, third_part, jnp.zeros((16, 128), F32)], axis=0)
    zero64 = jnp.zeros((C, 64), F32)
    wide = jnp.concatenate([skip_grad[:C], zero64], axis=1)
    bias_row = jnp.concatenate([skip_grad[C : C + 1], zero64[:1]], axis=1)
    packed = jnp.where(lane < 64, wide, 0.0)
    packed = jnp.where((lane >= 64) & (lane < 80), pltpu.roll(folded(in_full), 64, 1), packed)
    packed = jnp.where((lane >= 80) & (lane < 96), pltpu.roll(folded(out_full), 80, 1), packed)
    inside = (lane >= 96) & (lane < 112)
    packed = jnp.where(inside, pltpu.roll(middle, 96, 1), packed)
    for piece in range(4):
        moved = pltpu.roll(bias_row, 96 - 16 * piece, 1)
        packed = jnp.where(inside & (row == 48 + piece), moved, packed)
    last = lane >= 112
    packed = jnp.where(last & (row == me_s), pltpu.roll(first_part, 112, 1), packed)
    packed = jnp.where(last & (row == me_s + 32), pltpu.roll(first_part, 80, 1), packed)
    pk[...] = (packed * GRAD_SCALE).reshape(NB, 8, 128)

    def send(src, dst, step, to):
        pltpu.make_async_remote_copy(
            src_ref=src,
            dst_ref=dst,
            send_sem=rsend.at[step],
            recv_sem=rrecv.at[step],
            device_id=to,
            device_id_type=MESH,
        ).start()

    near = (me_s // 8) * 2 + lax.rem(me_s, 2)
    far = lax.rem(me_s // 2, 4)

    @pl.loop(1, NB)
    def _(d):
        peer = lax.rem(me_b + d, NB)
        send(pk.at[peer], r_batch.at[me_b], 0, {"batch": peer})

    r_batch[me_b] = pk[me_b]

    batch_wait(2)
    bz[...] = brecv[2].reshape(NB * 32, 128).astype(F32)
    for index in range(SLOTS * K3):
        slot, k = divmod(index, K3)
        grad = bz[pl.ds(index, NB, stride=32), :]
        grads = jnp.concatenate([grad, -sign * pltpu.roll(grad, 64, 1)], axis=0).astype(BF16)
        grads_v[index] = grads
        weights = w_v[slot, k]
        both = dot_nt(grads, jnp.concatenate([weights, weights], axis=0))
        bz[pl.ds(index, NB, stride=32), :] = jnp.where(sign < 0.0, both[:8], both[8:])
    batch_start(3, returned)

    drain(r_batch.at[pl.ds(0, NB - 1)], rrecv.at[0])
    part_near[...] = jnp.sum(r_batch[...], axis=0)

    @pl.loop(1, 8)
    def _(d):
        slot = lax.rem(near + d, 8)
        peer = (slot // 2) * 8 + far * 2 + lax.rem(slot, 2)
        send(part_near, r_near.at[near], 1, {"space": peer})

    r_near[near] = part_near[...]

    batch_wait(3)
    slots_in(3)
    grad_spectrum = []
    for k in range(K3):
        low = fac_v[k * K2 : k * K2 + L2, :] + sm[k * K2 : k * K2 + L2, :]
        grad_spectrum.append(
            jnp.concatenate([low, fac_v[k * K2 + L2 : (k + 1) * K2, :]], axis=0)
        )
    modes_out(grad_spectrum, two_t, 3)


    drain(r_near.at[pl.ds(0, 7)], rrecv.at[1])
    part_far[...] = jnp.sum(r_near[...], axis=0)

    @pl.loop(1, 4)
    def _(d):
        slot = lax.rem(far + d, 4)
        peer = (near // 2) * 8 + slot * 2 + lax.rem(near, 2)
        send(part_far, r_far.at[far], 2, {"space": peer})

    r_far[far] = part_far[...]

    for index in range(SLOTS * K3):
        slot, k = divmod(index, K3)
        dg_v[slot, k] = dot_tn(lefts_v[index], grads_v[index])[:C]
    dg_copy = pltpu.make_async_copy(dg_v, dg_hbm.at[0], out_sem.at[1])
    dg_copy.start()

    mix_channels(gp_v, kron_back_v, False)
    skip_copy = pltpu.make_async_copy(skip_v, skip_out_hbm, out_sem.at[2])
    skip_copy.start()

    drain(r_far.at[pl.ds(0, 3)], rrecv.at[2])
    part_all[...] = jnp.sum(r_far[...], axis=0)

    @pl.loop(1, NB)
    def _(d):
        send(part_all, r_all.at[me_b], 3, {"batch": lax.rem(me_b + d, NB)})

    r_all[me_b] = part_all[...]
    space_wait(6)
    backward_row(rbuf[6], zf.at[pl.ds(0, HALF)], left_v, one_t_ref[...])

    def finish(q, field):
        ig_v[:, q] = (field + skip_v[0, :, q].astype(F32)).astype(BF16)

    each_pair(left_v, three_t_ref, finish)
    ig_copy = pltpu.make_async_copy(ig_v, ig_hbm, out_sem.at[3])
    ig_copy.start()

    space_wait(7)
    blocks_copy = pltpu.make_async_copy(rbuf.at[7], blocks_hbm, out_sem.at[4])
    blocks_copy.start()
    drain(r_all.at[pl.ds(0, NB - 1)], rrecv.at[3])
    red_copy = pltpu.make_async_copy(r_all, red_hbm, out_sem.at[5])
    red_copy.start()
    for index in range(8):
        drain(sbuf.at[index, pl.ds(0, NS - 1)], ssend.at[index])
    for phase in range(4):
        drain(bsend.at[phase, pl.ds(0, NB - 1)], bssem.at[phase])
    drain(pk.at[pl.ds(0, NB - 1)], rsend.at[0])
    drain(r_near.at[pl.ds(0, 7)], rsend.at[1])
    drain(r_far.at[pl.ds(0, 3)], rsend.at[2])
    drain(r_all.at[pl.ds(0, NB - 1)], rsend.at[3])
    for started in (out_copy, dg_copy, skip_copy, ig_copy, blocks_copy, red_copy):
        started.wait()


def finish_kernel(
    blocks_hbm,
    packed_hbm,
    one_t_hbm,
    three_t_hbm,
    skip_hbm,
    out_in,
    dg_in,
    ig_in,
    out_hbm,
    ig_hbm,
    dg_hbm,
    fin_hbm,
    fout_hbm,
    first_hbm,
    second_hbm,
    third_hbm,
    mix_hbm,
    bias_hbm,
    blocks_v,
    packed_v,
    one_t_v,
    three_t_v,
    skip_v,
    out_v,
    dg_v,
    ig_v,
    left_v,
    zf,
    fin_v,
    fout_v,
    first_v,
    second_v,
    third_v,
    mix_v,
    bias_v,
    sem,
):
    def copy(src, dst, index):
        started = pltpu.make_async_copy(src, dst, sem.at[index])
        started.start()
        return started

    arriving = [
        copy(src, dst, index)
        for index, (src, dst) in enumerate(
            (
                (blocks_hbm, blocks_v),
                (one_t_hbm, one_t_v),
                (three_t_hbm, three_t_v),
                (skip_hbm.at[1], skip_v),
                (packed_hbm, packed_v),
                (out_in, out_v),
                (ig_in, ig_v.at[0]),
                (dg_in, dg_v),
            )
        )
    ]
    waits = []

    def pass_on(index, src, dst):
        arriving[index].wait()
        waits.append(copy(src, dst, 8 + index))

    for index in range(4):
        arriving[index].wait()
    backward_row(blocks_v[...], zf, left_v, one_t_v[...])
    arriving[4].wait()
    packed = packed_v[...].reshape(C, 128)
    turned = packed.T
    fin_v[...] = turned[64:80]
    fout_v[...] = turned[80:96]
    second_v[...] = turned[96:112, :K2]
    first_v[0] = turned[112:, :K1]
    first_v[1] = turned[112:, K1:]
    third_v[...] = left_by(packed, 96)[K2 : K2 + K3, :R]
    mix_v[...] = packed[:, :C]
    bias = jnp.zeros((1, 128), F32)
    lane = lanes((1, 128))
    for piece in range(4):
        moved = pltpu.roll(packed[48 + piece : 49 + piece], (32 + 16 * piece) % 128, 1)
        bias = jnp.where((lane >= 16 * piece) & (lane < 16 * (piece + 1)), moved, bias)
    bias_v[...] = bias[:, :C]
    small = (
        (fin_v, fin_hbm),
        (fout_v, fout_hbm),
        (first_v, first_hbm),
        (second_v, second_hbm),
        (third_v, third_hbm),
        (mix_v, mix_hbm),
        (bias_v, bias_hbm),
    )
    waits += [copy(src, dst, 17 + index) for index, (src, dst) in enumerate(small)]
    for pair in range(CQ // 2):
        field = dot(left_v[...], three_t_v[:, pair * 256 : (pair + 1) * 256])
        for half in range(2):
            q = pair * 2 + half
            value = field[:, half * 128 : (half + 1) * 128].reshape(CG, N1, N3)
            ig_v[1, :, q] = (value + skip_v[:, q].astype(F32)).astype(BF16)
        cut = (1, slice(None), pl.ds(pair * 2, 2))
        waits.append(copy(ig_v.at[cut], ig_hbm.at[cut], 24 + pair))
        if pair == 0:
            pass_on(5, out_v, out_hbm)
        if pair == 1:
            pass_on(6, ig_v.at[0], ig_hbm.at[0])
        if pair == 2:
            pass_on(7, dg_v, dg_hbm)
    for started in waits:
        started.wait()


def local(
    inputs,
    cotangent,
    dense_weights,
    owner_table,
    hot_mask,
    skip_weight,
    bias_vector,
    input_factor,
    output_factor,
    first_factor,
    second_factor,
    third_factor,
):
    field = (ROWS, CG, CQ, N1, N3)
    three, three_t, one, one_t, two, two_t, patterns, spread, select = [
        jnp.asarray(table) for table in build_tables()
    ]
    smem = pl.BlockSpec(memory_space=pltpu.SMEM)
    hbm = pl.BlockSpec(memory_space=pltpu.HBM)
    dense = (SLOTS, K3, C, 2 * C)
    operands = (
        inputs.reshape(field),
        three,
        one,
        hot_mask,
        skip_weight,
        input_factor.T,
        output_factor.T,
        jnp.swapaxes(first_factor, 1, 2),
        second_factor.T,
        third_factor,
        two,
        two_t,
        patterns,
        spread,
        select,
        one_t,
        three_t,
        cotangent.reshape(field),
    )
    blocks = (NS, 16, 128)
    row = field[1:]
    output, skip_part, grad_row, dense_grad, received, packed = pl.pallas_call(
        kernel,
        out_shape=(
            jax.ShapeDtypeStruct(field, BF16),
            jax.ShapeDtypeStruct(field, BF16),
            jax.ShapeDtypeStruct(row, BF16),
            jax.ShapeDtypeStruct((1,) + dense, F32),
            jax.ShapeDtypeStruct(blocks, BF16),
            jax.ShapeDtypeStruct((NB, 8, 128), F32),
        ),
        in_specs=[smem, smem] + [hbm] * 19,
        out_specs=(hbm,) * 6,
        scratch_shapes=[pltpu.VMEM(value.shape, value.dtype) for value in operands]
        + [
            pltpu.VMEM(dense, BF16),
            pltpu.VMEM(field, BF16),
            pltpu.VMEM(field, BF16),
            pltpu.VMEM(dense, F32),
            pltpu.VMEM(field, BF16),
            pltpu.VMEM(row, BF16),
            pltpu.VMEM((C * 16, C * 16), BF16),
            pltpu.VMEM((C * 16, C * 16), BF16),
            pltpu.VMEM((CG * N1, 256), BF16),
            pltpu.VMEM((CG * N1, 256), F32),
            pltpu.VMEM((ROWS * HALF, 128), F32),
            pltpu.VMEM((8,) + blocks, BF16),
            pltpu.VMEM((8,) + blocks, BF16),
            pltpu.VMEM((4, NB, 32, 128), BF16),
            pltpu.VMEM((4, NB, 32, 128), BF16),
            pltpu.VMEM((K3 * K2, 128), F32),
            pltpu.VMEM((K3 * K2, 128), BF16),
            pltpu.VMEM((K3, L2, 128), F32),
            pltpu.VMEM((K3 * K2, 128), F32),
            pltpu.VMEM((K3 * K2, 128), F32),
            pltpu.VMEM((K3 * K2, 128), BF16),
            pltpu.VMEM((K3 * K2, 128), F32),
            pltpu.VMEM((NB * 32, 128), F32),
            pltpu.VMEM((NB * 32, 128), F32),
            pltpu.VMEM((SLOTS * K3, 16, 128), BF16),
            pltpu.VMEM((SLOTS * K3, 16, 128), BF16),
            pltpu.VMEM((C + 16, C * 16), F32),
            pltpu.VMEM((NB, 8, 128), F32),
            pltpu.VMEM((NB, 8, 128), F32),
            pltpu.VMEM((8, 8, 128), F32),
            pltpu.VMEM((4, 8, 128), F32),
            pltpu.VMEM((NB, 8, 128), F32),
            pltpu.VMEM((8, 128), F32),
            pltpu.VMEM((8, 128), F32),
            pltpu.VMEM((8, 128), F32),
            pltpu.SemaphoreType.DMA((20,)),
            pltpu.SemaphoreType.DMA((6,)),
            pltpu.SemaphoreType.DMA((8,)),
            pltpu.SemaphoreType.DMA((8,)),
            pltpu.SemaphoreType.DMA((4,)),
            pltpu.SemaphoreType.DMA((4,)),
            pltpu.SemaphoreType.DMA((4,)),
            pltpu.SemaphoreType.DMA((4,)),
        ],
        compiler_params=pltpu.CompilerParams(
            collective_id=0, has_side_effects=True, vmem_limit_bytes=64 * 2**20
        ),
    )(owner_table, bias_vector, *operands, dense_weights)
    results = (
        (field, BF16),
        (field, BF16),
        ((1,) + dense, F32),
        ((R, C), F32),
        ((R, C), F32),
        ((2, R, K1), F32),
        ((R, K2), F32),
        ((K3, R), F32),
        ((C, C), F32),
        ((1, C), F32),
    )
    output, input_grad, dense_grad, in_t, out_t, first_t, second_t, third, skip, bias = pl.pallas_call(
        finish_kernel,
        out_shape=tuple(jax.ShapeDtypeStruct(*result) for result in results),
        in_specs=[hbm] * 8,
        out_specs=(hbm,) * len(results),
        scratch_shapes=[
            pltpu.VMEM(blocks, BF16),
            pltpu.VMEM((NB, 8, 128), F32),
            pltpu.VMEM(one_t.shape, BF16),
            pltpu.VMEM(three_t.shape, BF16),
            pltpu.VMEM(row, BF16),
            pltpu.VMEM(field, BF16),
            pltpu.VMEM((1,) + dense, F32),
            pltpu.VMEM(field, BF16),
            pltpu.VMEM((CG * N1, 256), BF16),
            pltpu.VMEM((HALF, 128), F32),
        ]
        + [pltpu.VMEM(*result) for result in results[3:]]
        + [pltpu.SemaphoreType.DMA((28,))],
        compiler_params=pltpu.CompilerParams(vmem_limit_bytes=64 * 2**20),
    )(received, packed, one_t, three_t, skip_part, output, dense_grad, grad_row)
    return (
        output.reshape(inputs.shape),
        input_grad.reshape(inputs.shape),
        dense_grad,
        in_t.T,
        out_t.T,
        jnp.swapaxes(first_t, 1, 2),
        second_t.T,
        third,
        skip,
        bias.reshape(C),
    )


def solution(mesh):
    field = P("batch", "space", None, None, None)
    dense = P("space", "batch", None, None, None)
    whole = P()
    return jax.shard_map(
        local,
        mesh=mesh,
        in_specs=(field, field, dense, whole, P("space", None, None)) + (whole,) * 7,
        out_specs=(field, field, dense) + (whole,) * 7,
        check_vma=False,
    )
```
